128 devices in a mesh: tp: 16 (over z, x_lo, core), dp: 8 (over x_hi, y).
Axes of the slice: x: 4 (x_hi: 2, x_lo: 2; x = x_hi * 2 + x_lo), y: 4, z: 4, core: 2. Of those that a mesh axis runs over, the one named last changes fastest.
Arguments:
- hidden_in: bfloat16 [16384, 7168], P(('dp', 'tp')), may hold values from -6 to 6
- norm_gain: float32 [7168], replicated, may hold values from 0.25 to 1.75
- w_qkv: bfloat16 [3, 7168, 4096], P(None, None, 'tp')
- w_out: bfloat16 [4096, 3584], P('tp'), may hold values from -0.1875 to 0.1875
- lengths: int32 [16], replicated, may hold values from 256 to 1024, as said below
- student_in: bfloat16 [16384, 1024], P(('dp', 'tp')), may hold values from -6 to 6
- student_gain: float32 [1024], replicated, may hold values from 0.25 to 1.75
- proj_weight: bfloat16 [3584, 1024], P('tp'), may hold values from -0.1875 to 0.1875
- loss_scale: float32 [1], replicated, may hold values from 32768 to 131072
Outputs:
- student_grad: bfloat16 [16384, 1024], P(('dp', 'tp'))
- proj_grad: bfloat16 [3584, 1024], P('tp')
- gain_grad: float32 [1024], replicated
- loss: float32 [], replicated
The draws below stay inside these ranges and needn't reach their ends.
Inputs may be any that keep to these rules, and one draw needn't show every extreme that they name: One of the lengths equals 1024.
All inputs are finite; a program needn't handle non-finite values.
Results may differ from the reference program's by a relative error of at most 0.02.
Values may be sent and summed in bfloat16 or wider, within the bound.
A program may use at most 192 MiB of HBM per device.

```python
import math
import jax
import jax.numpy as jnp
from jax import lax

D = 7168
HEADS = 32
HEAD = 128
HW = 3584
DS = 1024
LEN = 1024
SEQS = 2
NSEQ = 16
TOKENS = 16384
N_TP = 16
N_DP = 8


def draw_lengths(key, part):
    key = jax.random.fold_in(key, 11)
    first_key, second_key = jax.random.split(key)
    drawn = jax.random.randint(first_key, (NSEQ,), LEN // 4, LEN + 1)
    chosen = jax.random.randint(second_key, (), 0, NSEQ)
    return jnp.where(jnp.arange(NSEQ) == chosen, LEN, drawn).astype(jnp.int32)


def draw_w_qkv(key, part):
    key = jax.random.fold_in(key, 5)
    base_key = jax.random.fold_in(key, 0)
    base = jax.random.normal(base_key, (3, D, HEADS * HEAD), jnp.float32) / math.sqrt(D)
    return base.astype(jnp.bfloat16)


def shard_levels(stream_key, shape, shards, low, largest):
    def one(dim, shards_of):
        steps = jax.random.uniform(jax.random.fold_in(jax.random.fold_in(stream_key, 6), dim), (shards_of,), jnp.float32, low / len(shards), largest / len(shards))
        return jnp.repeat(jnp.exp(steps), shape[dim] // shards_of).reshape((-1,) + (1,) * (len(shape) - dim - 1))

    level = one(*shards[0])
    for cut in shards[1:]:
        level = level * one(*cut)
    return level


def bell_draw(stream_key, dims, scale, most, pieces=(), kind=jnp.bfloat16):
    entries = scale * jax.random.normal(stream_key, dims, jnp.float32)
    if pieces:
        entries = entries * shard_levels(stream_key, dims, pieces, -0.22, 0.18)
    return jnp.clip(entries, -most, most).astype(kind)


def setup_inputs(seed: int = 0) -> dict:
    arg_keys = jax.random.split(jax.random.key(seed), 10)
    hidden_in = bell_draw(arg_keys[0], (TOKENS, D), 1.0, 6.0, ((0, 128),))
    norm_gain = jnp.clip(1.0 + 0.15 * jax.random.normal(arg_keys[1], (D,), jnp.float32), 0.25, 1.75)
    w_qkv = draw_w_qkv(jax.random.fold_in(arg_keys[9], 71), 0)
    w_out = bell_draw(arg_keys[3], (HEADS * HEAD, HW), (HEADS * HEAD // 4) ** -0.5, 0.1875, ((0, 16),))
    lengths = draw_lengths(jax.random.fold_in(arg_keys[9], 71), 0)
    student_in = bell_draw(arg_keys[5], (TOKENS, DS), 1.0, 6.0, ((0, 128),))
    student_gain = jnp.clip(1.0 + 0.15 * jax.random.normal(arg_keys[6], (DS,), jnp.float32), 0.25, 1.75)
    proj_weight = bell_draw(arg_keys[7], (HW, DS), DS ** -0.5, 0.1875, ((0, 16),))
    loss_scale = jnp.clip(jnp.exp(jax.random.uniform(arg_keys[8], (1,), jnp.float32, math.log(32768.0), math.log(131072.0))), 32768.0, 131072.0)
    return dict(hidden_in=hidden_in, norm_gain=norm_gain, w_qkv=w_qkv, w_out=w_out, lengths=lengths, student_in=student_in, student_gain=student_gain, proj_weight=proj_weight, loss_scale=loss_scale)


def layer_norm(rows, gain):
    values = rows.astype(jnp.float32)
    centred = values - lax.optimization_barrier(jnp.mean(values, axis=-1, keepdims=True))
    spread = lax.optimization_barrier(jnp.mean(centred * centred, axis=-1, keepdims=True))
    return (centred * lax.rsqrt(spread + 1e-05) * gain).astype(jnp.bfloat16)

def rms_norm(rows, gain):
    return rows * lax.rsqrt(lax.optimization_barrier(jnp.mean(rows * rows, axis=-1, keepdims=True)) + 1e-06) * gain

def valid_rows(first_row, count, group_lengths):
    rows = first_row + jnp.arange(count, dtype=jnp.int32)
    caption = rows // LEN
    position = rows % LEN
    picked = jnp.where(caption[:, None] == jnp.arange(SEQS, dtype=jnp.int32)[None, :], group_lengths[None, :], 0)
    return position < lax.optimization_barrier(jnp.sum(picked, axis=1))

def single_caption(inputs):
    query, keys, values, length = inputs
    scores = jnp.einsum('qhd,khd->hqk', query.astype(jnp.float32), keys.astype(jnp.float32)) * (1.0 / math.sqrt(HEAD))
    position = jnp.arange(LEN, dtype=jnp.int32)
    allowed = (position[None, :] <= position[:, None]) & (position[None, :] < length)
    scores = jnp.where(allowed[None], scores, -1e+30)
    weights = jnp.exp(scores - lax.optimization_barrier(jnp.max(scores, axis=-1, keepdims=True)))
    probs = (weights / lax.optimization_barrier(jnp.sum(weights, axis=-1, keepdims=True))).astype(jnp.bfloat16)
    return jnp.einsum('hqk,khd->qhd', probs.astype(jnp.float32), values.astype(jnp.float32)).astype(jnp.bfloat16)

def reference(hidden_in, norm_gain, w_qkv, w_out, lengths, student_in, student_gain, proj_weight, loss_scale):
    group_rows = SEQS * LEN
    count = jnp.sum(lengths).astype(jnp.float32)
    factor = 2.0 * loss_scale[0] / (count * HW)

    def group_step(carry, inputs):
        proj_total, gain_total, loss_total = carry
        teacher_rows, student_rows, group_lengths = inputs
        normed = layer_norm(teacher_rows, norm_gain)
        shaped = []
        for index in range(3):
            projected = jnp.dot(normed, w_qkv[index], preferred_element_type=jnp.float32).astype(jnp.bfloat16)
            shaped.append(projected.reshape(SEQS, LEN, HEADS, HEAD))
        context = lax.map(single_caption, (shaped[0], shaped[1], shaped[2], group_lengths))
        context = context.reshape(group_rows, N_TP, HEADS * HEAD // N_TP)
        parts = jnp.einsum('tif,ifc->itc', context.astype(jnp.float32), w_out.reshape(N_TP, HEADS * HEAD // N_TP, HW).astype(jnp.float32))
        rounded = lax.optimization_barrier(parts.astype(jnp.bfloat16))
        mixed = lax.optimization_barrier(jnp.sum(rounded.astype(jnp.float32), axis=0))
        target = (teacher_rows[:, :HW].astype(jnp.float32) + mixed).astype(jnp.bfloat16)
        student_f32 = student_rows.astype(jnp.float32)
        student_norm = rms_norm(student_f32, student_gain).astype(jnp.bfloat16)
        mapped = jnp.dot(student_norm, proj_weight.T, preferred_element_type=jnp.float32)
        valid = valid_rows(0, group_rows, group_lengths)
        diff = jnp.where(valid[:, None], mapped - target.astype(jnp.float32), 0.0)
        loss_part = jnp.sum(diff * diff)
        delta = (diff * factor).astype(jnp.bfloat16)
        proj_part = jnp.dot(delta.T, student_norm, preferred_element_type=jnp.float32)
        norm_back = jnp.dot(delta, proj_weight, preferred_element_type=jnp.float32)
        unused, pull_back = jax.vjp(rms_norm, student_f32, student_gain)
        row_grad, gain_part = pull_back(norm_back)
        carry = (proj_total + proj_part, gain_total + gain_part, loss_total + loss_part)
        return (carry, row_grad.astype(jnp.bfloat16))
    start = (jnp.zeros((HW, DS), jnp.float32), jnp.zeros((DS,), jnp.float32), jnp.zeros((), jnp.float32))
    inputs = (hidden_in.reshape(N_DP, group_rows, D), student_in.reshape(N_DP, group_rows, DS), lengths.reshape(N_DP, SEQS))
    totals, row_grads = lax.scan(group_step, start, inputs)
    proj_total, gain_total, loss_total = totals
    return (row_grads.reshape(TOKENS, DS), proj_total.astype(jnp.bfloat16), gain_total, loss_total / (count * HW))
```

```python
import functools
import math

import jax
import jax.numpy as jnp
from jax import lax
from jax.experimental import pallas as pl
from jax.experimental.pallas import tpu as pltpu
from jax.sharding import PartitionSpec as P

HEAD = 128
HW = 3584
LEN = 1024
SEQS = 2
D = 7168
ROWS = 128
FIRST = 80
MESH = pl.DeviceIdType.MESH
MIB = 1 << 20


def place():
    tp = lax.axis_index("tp")
    return tp // 4, (tp // 2) % 2, tp % 2


def at(z, x, core):
    return {"tp": (z % 4) * 4 + x * 2 + core}


def across(z, x, core):
    dp = lax.axis_index("dp")
    return {"tp": z * 4 + (1 - x) * 2 + core, "dp": (1 - dp // 4) * 4 + dp % 4}


def remote(src, dst, send, recv, device):
    return pltpu.make_async_remote_copy(
        src_ref=src, dst_ref=dst, send_sem=send, recv_sem=recv, device_id=device, device_id_type=MESH
    )


def greet(devices):
    barrier = pltpu.get_barrier_semaphore()
    for device in devices:
        pl.semaphore_signal(barrier, 1, device_id=device, device_id_type=MESH)
    pl.semaphore_wait(barrier, len(devices))


def project_kernel(
    x_ref, gain_ref, w_hbm, wout_hbm, qkv_ref, wout_all, normed, rows, w, send, recv, wsend, wrecv, local
):
    z, x, core = place()
    other = 1 - x
    kept = z // 2
    rel = (z - 2 * core + 4) % 4
    ahead = (rel == 0) | (rel == 3)
    step = jnp.where(ahead, 1, -1)
    near = (z + step + 4) % 4
    onward = (z - step + 4) % 4
    via = jnp.where(ahead, 1, 0)
    far = (z + 2) % 4

    greet(
        [at(z, x, 1 - core)]
        + [at(zz, x, c) for zz in (z + 1, z + 3) for c in (0, 1)]
        + [at(z, other, c) for c in (0, 1)]
        + [across(z, x, c) for c in (0, 1)]
    )

    w_out_going = [
        remote(w_hbm.at[k], w.at[core, k], wsend.at[k], wrecv.at[k], at(z, x, 1 - core)) for k in range(3)
    ]
    w_own = [pltpu.make_async_copy(w_hbm.at[k], w.at[core, k], local.at[k]) for k in range(3)]
    slot = x * 2 + core
    proj_going = [
        remote(wout_hbm, wout_all.at[slot], wsend.at[3], wrecv.at[3 + core], at(z, x, 1 - core)),
        remote(wout_hbm, wout_all.at[slot], wsend.at[4], wrecv.at[5 + core], across(z, x, 0)),
        remote(wout_hbm, wout_all.at[slot], wsend.at[5], wrecv.at[5 + core], across(z, x, 1)),
    ]
    proj_own = pltpu.make_async_copy(wout_hbm, wout_all.at[slot], local.at[3])
    for copy in w_own + w_out_going + proj_going + [proj_own]:
        copy.start()

    def part(chunk_z, chunk_x, s, cls):
        chunk = (chunk_z % 2) * 2 + chunk_x
        start, size = ((0, FIRST), (FIRST, ROWS - FIRST))[cls]
        return rows.at[chunk, pl.ds(pl.multiple_of(s * ROWS + start, 16), size)]

    def sem(chunk_z, chunk_x, s, cls):
        return recv.at[((chunk_z % 2) * 2 + chunk_x) * 4 + s * 2 + cls]

    def arrived(chunk_z, chunk_x, s, cls):
        ref = part(chunk_z, chunk_x, s, cls)
        remote(ref, ref, send.at[0], sem(chunk_z, chunk_x, s, cls), at(z, x, 1 - core)).wait_recv()

    def forward(chunk_z, chunk_x, s, cls, index, device):
        ref = part(chunk_z, chunk_x, s, cls)
        return remote(ref, ref, send.at[index], sem(chunk_z, chunk_x, s, cls), device)

    def norm(start, size):
        def one(i, carry):
            block = pl.ds(pl.multiple_of(start + i * 16, 16), 16)
            values = x_ref[block, :].astype(jnp.float32)
            centred = values - jnp.mean(values, axis=-1, keepdims=True)
            spread = jnp.mean(centred * centred, axis=-1, keepdims=True)
            normed[block, :] = (centred * lax.rsqrt(spread + 1e-05) * gain_ref[...]).astype(jnp.bfloat16)
            return carry

        lax.fori_loop(0, size // 16, one, 0)

    def own_copies(cls):
        start, size = ((0, FIRST), (FIRST, ROWS - FIRST))[cls]
        src = normed.at[pl.ds(start, size)]
        dst = part(z, x, core, cls)
        got = sem(z, x, core, cls)
        base = cls * 4
        return (
            [
                remote(src, dst, send.at[base], got, at(z + 1, x, kept)),
                remote(src, dst, send.at[base + 1], got, at(z + 3, x, kept)),
                remote(src, dst, send.at[base + 2], got, at(z, other, kept)),
            ],
            remote(src, dst, send.at[base + 3], got, at(z, x, 1 - core)),
            pltpu.make_async_copy(src, dst, local.at[4 + cls]),
        )

    for cls, (start, size) in ((1, (FIRST, ROWS - FIRST)), (0, (0, FIRST))):
        norm(start, size)
        away, sibling, here = own_copies(cls)
        for copy in away:
            copy.start()

        @pl.when(core == kept)
        def _():
            here.start()

        @pl.when(core != kept)
        def _():
            sibling.start()

    def multiply(chunk_z, chunk_x):
        chunk = (chunk_z % 2) * 2 + chunk_x

        def one(n, carry):
            out = jnp.dot(rows[chunk], w[n % 2, n // 2], preferred_element_type=jnp.float32)
            qkv_ref[n, pl.ds(pl.multiple_of(chunk * 256, 256), 256), :] = out.astype(jnp.bfloat16)
            return carry

        lax.fori_loop(0, 6, one, 0)

    source = rel < 2

    fx = []
    for s in (0, 1):
        arrived(near, x, s, 1)
        fx.append(forward(near, x, s, 1, 8 + s, at(z, other, core)))
        fx[-1].start()
    on_b = forward(near, x, via, 1, 10, at(onward, x, core))
    on_b.start()

    for copy in w_own:
        copy.wait()
    for k in range(3):
        remote(w_hbm.at[k], w.at[1 - core, k], wsend.at[k], wrecv.at[k], at(z, x, 1 - core)).wait_recv()

    @pl.when(source)
    def _():
        for cls in (0, 1):
            arrived(z, x, 1 - core, cls)
            own_copies(cls)[2].wait()
        multiply(z, x)

    for s in (0, 1):
        arrived(near, x, s, 0)
    on_a = forward(near, x, via, 0, 11, at(onward, x, core))
    on_a.start()

    def spread():
        return [
            forward(z, other, s, 0, 12 + s * 2 + i, at(zz, x, core))
            for s in (0, 1)
            for i, zz in enumerate((z + 1, z + 3))
        ]

    def crossing():
        return [forward(far, x, s, 1, 12 + s, at(z, other, core)) for s in (0, 1)]

    @pl.when(source)
    def _():
        for s in (0, 1):
            arrived(z, other, s, 0)
        for copy in spread():
            copy.start()
        for s in (0, 1):
            arrived(z, other, s, 1)
        multiply(z, other)

    @pl.when(jnp.logical_not(source))
    def _():
        for s in (0, 1):
            arrived(far, x, s, 1)
        for copy in crossing():
            copy.start()
        multiply(near, x)

    for s in (0, 1):
        arrived(near, other, s, 0)
    on_p = forward(near, other, via, 0, 16, at(onward, x, core))
    on_p.start()

    @pl.when(source)
    def _():
        multiply(near, x)

    for s in (0, 1):
        arrived(near, other, s, 1)
    multiply(near, other)

    @pl.when(jnp.logical_not(source))
    def _():
        for s in (0, 1):
            arrived(far, x, s, 0)
        multiply(far, x)
        for s in (0, 1):
            arrived(far, other, s, 0)
            arrived(far, other, s, 1)
        multiply(far, other)

    for cls in (0, 1):
        away, sibling, here = own_copies(cls)
        for copy in away:
            copy.wait_send()

        @pl.when(core != kept)
        def _():
            sibling.wait_send()

    for copy in fx + [on_b, on_a, on_p]:
        copy.wait_send()

    @pl.when(source)
    def _():
        for copy in spread():
            copy.wait_send()

    @pl.when(jnp.logical_not(source))
    def _():
        for copy in crossing():
            copy.wait_send()

    for copy in w_out_going + proj_going:
        copy.wait_send()
    proj_own.wait()
    remote(
        wout_hbm, wout_all.at[x * 2 + 1 - core], wsend.at[3], wrecv.at[3 + 1 - core], at(z, x, 1 - core)
    ).wait_recv()
    for c in (0, 1):
        remote(wout_hbm, wout_all.at[other * 2 + c], wsend.at[4], wrecv.at[5 + c], across(z, x, c)).wait_recv()


def project(hidden, gain, w_qkv, w_out):
    return pl.pallas_call(
        project_kernel,
        name="project",
        out_shape=(
            jax.ShapeDtypeStruct((6, LEN, 256), jnp.bfloat16),
            jax.ShapeDtypeStruct((4, 256, HW), jnp.bfloat16),
        ),
        in_specs=[
            pl.BlockSpec(memory_space=pltpu.VMEM),
            pl.BlockSpec(memory_space=pltpu.VMEM),
            pl.BlockSpec(memory_space=pltpu.HBM),
            pl.BlockSpec(memory_space=pltpu.HBM),
        ],
        out_specs=(pl.BlockSpec(memory_space=pltpu.VMEM), pl.BlockSpec(memory_space=pltpu.HBM)),
        scratch_shapes=[
            pltpu.VMEM((ROWS, D), jnp.bfloat16),
            pltpu.VMEM((4, 2 * ROWS, D), jnp.bfloat16),
            pltpu.VMEM((2, 3, D, 256), jnp.bfloat16),
            pltpu.SemaphoreType.DMA((17,)),
            pltpu.SemaphoreType.DMA((16,)),
            pltpu.SemaphoreType.DMA((6,)),
            pltpu.SemaphoreType.DMA((7,)),
            pltpu.SemaphoreType.DMA((6,)),
        ],
        compiler_params=pltpu.CompilerParams(
            collective_id=0, has_side_effects=True, vmem_limit_bytes=60 * MIB
        ),
    )(hidden, gain, w_qkv, w_out)


def attend_kernel(
    len_ref, qkv_ref, wout_ref, hid_hbm, target_ref, hid_ref, ctx, ctx_in, stage, parts, send, recv, osend, orecv, local
):
    z, x, core = place()
    other = 1 - x
    kept = z // 2
    length = len_ref[0]
    fetch = pltpu.make_async_copy(hid_hbm.at[:, pl.ds(0, HW)], hid_ref, local)
    fetch.start()

    greet(
        [at(z, x, 1 - core)]
        + [at(zz, x, c) for zz in (z + 1, z + 2, z + 3) for c in (0, 1)]
        + [at(z, other, core)]
    )

    def attend(chunk, keys, zq, mine):
        start = pl.multiple_of(chunk * 256, 256)
        row = lax.broadcasted_iota(jnp.int32, (256, keys), 0) + start
        col = lax.broadcasted_iota(jnp.int32, (256, keys), 1)
        allowed = (col <= row) & (col < length)

        def pair(half, carry):
            for h in (0, 1):
                lanes = slice(h * HEAD, (h + 1) * HEAD)
                q = qkv_ref[half, pl.ds(start, 256), lanes]
                k = qkv_ref[2 + half, :keys, lanes]
                v = qkv_ref[4 + half, :keys, lanes]
                scores = lax.dot_general(
                    q, k, (((1,), (1,)), ((), ())), preferred_element_type=jnp.float32
                ) * (1.0 / math.sqrt(HEAD))
                scores = jnp.where(allowed, scores, -1e30)
                weights = jnp.exp(scores - jnp.max(scores, axis=-1, keepdims=True))
                total = jnp.sum(weights, axis=-1, keepdims=True)
                out = jnp.dot(weights.astype(jnp.bfloat16), v, preferred_element_type=jnp.float32)
                ctx[zq * 2 + mine, half, :, lanes] = (out / total).astype(jnp.bfloat16)
            return carry

        lax.fori_loop(0, 2, pair, 0)

    def swap(zq):
        return remote(ctx.at[zq * 2], ctx_in.at[zq], send.at[zq], recv.at[zq], at(z, other, core))

    def give(zq, s):
        return remote(
            stage.at[zq, pl.ds(s * ROWS, ROWS)],
            parts.at[z],
            osend.at[zq * 2 + s],
            orecv.at[z],
            at(2 * core + zq, x, s),
        )

    def keep(zq, s):
        return pltpu.make_async_copy(stage.at[zq, pl.ds(s * ROWS, ROWS)], parts.at[z], osend.at[zq * 2 + s])

    for zq in (0, 1):
        keys = (zq + 1) * 512
        attend(zq * 2 + other, keys, zq, 0)
        swap(zq).start()
        attend(zq * 2 + x, keys, zq, 1)
        swap(zq).wait_recv()

        def one(n, carry):
            lanes = pl.ds(pl.multiple_of(n * 512, 512), 512)
            out = jnp.zeros((256, 512), jnp.float32)
            for half in (0, 1):
                out += jnp.dot(
                    ctx[zq * 2 + 1, half], wout_ref[x * 2 + half, :, lanes], preferred_element_type=jnp.float32
                )
                out += jnp.dot(
                    ctx_in[zq, half], wout_ref[other * 2 + half, :, lanes], preferred_element_type=jnp.float32
                )
            stage[zq, :, lanes] = out.astype(jnp.bfloat16)
            return carry

        lax.fori_loop(0, HW // 512, one, 0)
        for s in (0, 1):
            mine = (2 * core + zq == z) & (core == s)

            @pl.when(mine)
            def _():
                keep(zq, s).start()

            @pl.when(jnp.logical_not(mine))
            def _():
                give(zq, s).start()

    for zq in (0, 1):
        swap(zq).wait_send()
        for s in (0, 1):
            mine = (2 * core + zq == z) & (core == s)

            @pl.when(mine)
            def _():
                keep(zq, s).wait()

            @pl.when(jnp.logical_not(mine))
            def _():
                give(zq, s).wait_send()

    for far in (0, 1, 2, 3):

        @pl.when((z != far) | (core != kept))
        def _():
            remote(
                parts.at[far], parts.at[far], osend.at[0], orecv.at[far], at(z, x, 1 - core)
            ).wait_recv()

    fetch.wait()

    def total(i, carry):
        block = pl.ds(pl.multiple_of(i * 16, 16), 16)
        value = hid_ref[block, :].astype(jnp.float32)
        mixed = parts[0, block, :].astype(jnp.float32)
        for far in (1, 2, 3):
            mixed += parts[far, block, :].astype(jnp.float32)
        target_ref[block, :] = (value + mixed).astype(jnp.bfloat16)
        return carry

    lax.fori_loop(0, ROWS // 16, total, 0)


def attend(length, qkv, w_out, hidden):
    vmem = pl.BlockSpec(memory_space=pltpu.VMEM)
    return pl.pallas_call(
        attend_kernel,
        name="attend",
        out_shape=jax.ShapeDtypeStruct((ROWS, HW), jnp.bfloat16),
        in_specs=[
            pl.BlockSpec(memory_space=pltpu.SMEM),
            vmem,
            vmem,
            pl.BlockSpec(memory_space=pltpu.HBM),
        ],
        out_specs=vmem,
        scratch_shapes=[
            pltpu.VMEM((ROWS, HW), jnp.bfloat16),
            pltpu.VMEM((4, 2, 256, 256), jnp.bfloat16),
            pltpu.VMEM((2, 2, 256, 256), jnp.bfloat16),
            pltpu.VMEM((2, 256, HW), jnp.bfloat16),
            pltpu.VMEM((4, ROWS, HW), jnp.bfloat16),
            pltpu.SemaphoreType.DMA((2,)),
            pltpu.SemaphoreType.DMA((2,)),
            pltpu.SemaphoreType.DMA((4,)),
            pltpu.SemaphoreType.DMA((4,)),
            pltpu.SemaphoreType.DMA,
        ],
        compiler_params=pltpu.CompilerParams(
            collective_id=1, has_side_effects=True, vmem_limit_bytes=48 * MIB
        ),
    )(length, qkv, w_out, hidden)


def rms_norm(rows, gain):
    return rows * lax.rsqrt(jnp.mean(rows * rows, axis=-1, keepdims=True) + 1e-06) * gain


def valid_rows(first_row, count, group_lengths):
    rows = first_row + jnp.arange(count, dtype=jnp.int32)
    caption = rows // LEN
    position = rows % LEN
    picked = jnp.where(
        caption[:, None] == jnp.arange(SEQS, dtype=jnp.int32)[None, :], group_lengths[None, :], 0
    )
    return position < jnp.sum(picked, axis=1)


def shards(
    hidden_in, norm_gain, w_qkv, w_out, lengths, student_in, student_gain, proj_weight, loss_scale
):
    rows_dev = hidden_in.shape[0]
    tp_place = lax.axis_index("tp")
    group = lax.axis_index("dp")
    group_lengths = lax.dynamic_slice_in_dim(lengths, group * SEQS, SEQS)
    count = jnp.sum(lengths).astype(jnp.float32)
    factor = 2.0 * loss_scale[0] / (count * HW)
    own_rows = student_in.astype(jnp.float32)

    qkv, w_out_all = project(hidden_in, norm_gain.reshape(1, D), w_qkv, w_out)
    length = lax.dynamic_slice_in_dim(lengths, group * SEQS + tp_place % 2, 1)
    target = attend(length, qkv, w_out_all, hidden_in)

    proj_whole = lax.all_gather(proj_weight, "tp", axis=0, tiled=True)
    student_norm = rms_norm(own_rows, student_gain).astype(jnp.bfloat16)
    mapped = lax.dot_general(
        student_norm, proj_whole, (((1,), (1,)), ((), ())), preferred_element_type=jnp.float32
    )
    valid = valid_rows(tp_place * rows_dev, rows_dev, group_lengths)
    diff = jnp.where(valid[:, None], mapped - target.astype(jnp.float32), 0.0)
    loss_part = jnp.sum(diff * diff)
    delta = (diff * factor).astype(jnp.bfloat16)
    norm_back = jnp.dot(delta, proj_whole, preferred_element_type=jnp.float32)
    proj_part = lax.psum_scatter(
        lax.dot_general(
            delta, student_norm, (((0,), (0,)), ((), ())), preferred_element_type=jnp.float32
        ).astype(jnp.bfloat16),
        "tp",
        scatter_dimension=0,
        tiled=True,
    )
    proj_total = lax.psum(proj_part, "dp").astype(jnp.float32)
    unused, pull_back = jax.vjp(rms_norm, own_rows, student_gain)
    row_grad, gain_part = pull_back(norm_back)
    loss_total, gain_total = lax.psum((loss_part, gain_part), ("tp", "dp"))
    return (
        row_grad.astype(jnp.bfloat16),
        proj_total.astype(jnp.bfloat16),
        gain_total,
        loss_total / (count * HW),
    )


def solution(mesh):
    placed = (
        P(("dp", "tp"), None),
        P(),
        P(None, None, "tp"),
        P("tp", None),
        P(),
        P(("dp", "tp"), None),
        P(),
        P("tp", None),
        P(),
    )
    return jax.shard_map(
        shards,
        mesh=mesh,
        in_specs=placed,
        out_specs=(P(("dp", "tp"), None), P("tp", None), P(), P()),
        check_vma=False,
    )
```

```python
import functools
import math

import jax
import jax.numpy as jnp
from jax import lax
from jax.experimental import pallas as pl
from jax.experimental.pallas import tpu as pltpu
from jax.sharding import PartitionSpec as P

HEAD = 128
HW = 3584
LEN = 1024
SEQS = 2
D = 7168
DS = 1024
PROJ = 224
ROWS = 128
FIRST = 80
MESH = pl.DeviceIdType.MESH
MIB = 1 << 20


def place():
    tp = lax.axis_index("tp")
    return tp // 4, (tp // 2) % 2, tp % 2


def at(z, x, core):
    return {"tp": (z % 4) * 4 + x * 2 + core}


def across(z, x, core):
    dp = lax.axis_index("dp")
    return {"tp": z * 4 + (1 - x) * 2 + core, "dp": (1 - dp // 4) * 4 + dp % 4}


def beside(z, x, core, i):
    dp = lax.axis_index("dp")
    return {"tp": z * 4 + x * 2 + core, "dp": dp // 4 * 4 + (dp + i) % 4}


def remote(src, dst, send, recv, device):
    return pltpu.make_async_remote_copy(
        src_ref=src, dst_ref=dst, send_sem=send, recv_sem=recv, device_id=device, device_id_type=MESH
    )


def rms_norm(rows, gain):
    return rows * lax.rsqrt(jnp.mean(rows * rows, axis=-1, keepdims=True) + 1e-06) * gain


def greet(devices):
    barrier = pltpu.get_barrier_semaphore()
    for device in devices:
        pl.semaphore_signal(barrier, 1, device_id=device, device_id_type=MESH)
    pl.semaphore_wait(barrier, len(devices))


def project_kernel(
    x_ref, gain_ref, w_hbm, wout_hbm, qkv_ref, wout_all, normed, rows, w, send, recv, wsend, wrecv, local
):
    z, x, core = place()
    other = 1 - x
    kept = z // 2
    rel = (z - 2 * core + 4) % 4
    ahead = (rel == 0) | (rel == 3)
    step = jnp.where(ahead, 1, -1)
    near = (z + step + 4) % 4
    onward = (z - step + 4) % 4
    via = jnp.where(ahead, 1, 0)
    far = (z + 2) % 4

    greet(
        [at(z, x, 1 - core)]
        + [at(zz, x, c) for zz in (z + 1, z + 3) for c in (0, 1)]
        + [at(z, other, c) for c in (0, 1)]
        + [across(z, x, c) for c in (0, 1)]
    )

    w_out_going = [
        remote(w_hbm.at[k], w.at[core, k], wsend.at[k], wrecv.at[k], at(z, x, 1 - core)) for k in range(3)
    ]
    w_own = [pltpu.make_async_copy(w_hbm.at[k], w.at[core, k], local.at[k]) for k in range(3)]
    slot = x * 2 + core
    proj_going = [
        remote(wout_hbm, wout_all.at[slot], wsend.at[3], wrecv.at[3 + core], at(z, x, 1 - core)),
        remote(wout_hbm, wout_all.at[slot], wsend.at[4], wrecv.at[5 + core], across(z, x, 0)),
        remote(wout_hbm, wout_all.at[slot], wsend.at[5], wrecv.at[5 + core], across(z, x, 1)),
    ]
    proj_own = pltpu.make_async_copy(wout_hbm, wout_all.at[slot], local.at[3])
    for copy in w_own + w_out_going + proj_going + [proj_own]:
        copy.start()

    def part(chunk_z, chunk_x, s, cls):
        chunk = (chunk_z % 2) * 2 + chunk_x
        start, size = ((0, FIRST), (FIRST, ROWS - FIRST))[cls]
        return rows.at[chunk, pl.ds(pl.multiple_of(s * ROWS + start, 16), size)]

    def sem(chunk_z, chunk_x, s, cls):
        return recv.at[((chunk_z % 2) * 2 + chunk_x) * 4 + s * 2 + cls]

    def arrived(chunk_z, chunk_x, s, cls):
        ref = part(chunk_z, chunk_x, s, cls)
        remote(ref, ref, send.at[0], sem(chunk_z, chunk_x, s, cls), at(z, x, 1 - core)).wait_recv()

    def forward(chunk_z, chunk_x, s, cls, index, device):
        ref = part(chunk_z, chunk_x, s, cls)
        return remote(ref, ref, send.at[index], sem(chunk_z, chunk_x, s, cls), device)

    def norm(start, size):
        def one(i, carry):
            block = pl.ds(pl.multiple_of(start + i * 16, 16), 16)
            values = x_ref[block, :].astype(jnp.float32)
            centred = values - jnp.mean(values, axis=-1, keepdims=True)
            spread = jnp.mean(centred * centred, axis=-1, keepdims=True)
            normed[block, :] = (centred * lax.rsqrt(spread + 1e-05) * gain_ref[...]).astype(jnp.bfloat16)
            return carry

        lax.fori_loop(0, size // 16, one, 0)

    def own_copies(cls):
        start, size = ((0, FIRST), (FIRST, ROWS - FIRST))[cls]
        src = normed.at[pl.ds(start, size)]
        dst = part(z, x, core, cls)
        got = sem(z, x, core, cls)
        base = cls * 4
        return (
            [
                remote(src, dst, send.at[base], got, at(z + 1, x, kept)),
                remote(src, dst, send.at[base + 1], got, at(z + 3, x, kept)),
                remote(src, dst, send.at[base + 2], got, at(z, other, kept)),
            ],
            remote(src, dst, send.at[base + 3], got, at(z, x, 1 - core)),
            pltpu.make_async_copy(src, dst, local.at[4 + cls]),
        )

    for cls, (start, size) in ((1, (FIRST, ROWS - FIRST)), (0, (0, FIRST))):
        norm(start, size)
        away, sibling, here = own_copies(cls)
        for copy in away:
            copy.start()

        @pl.when(core == kept)
        def _():
            here.start()

        @pl.when(core != kept)
        def _():
            sibling.start()

    def multiply(chunk_z, chunk_x):
        chunk = (chunk_z % 2) * 2 + chunk_x

        def one(n, carry):
            out = jnp.dot(rows[chunk], w[n % 2, n // 2], preferred_element_type=jnp.float32)
            qkv_ref[n, pl.ds(pl.multiple_of(chunk * 256, 256), 256), :] = out.astype(jnp.bfloat16)
            return carry

        lax.fori_loop(0, 6, one, 0)

    source = rel < 2

    fx = []
    for s in (0, 1):
        arrived(near, x, s, 1)
        fx.append(forward(near, x, s, 1, 8 + s, at(z, other, core)))
        fx[-1].start()
    on_b = forward(near, x, via, 1, 10, at(onward, x, core))
    on_b.start()

    for copy in w_own:
        copy.wait()
    for k in range(3):
        remote(w_hbm.at[k], w.at[1 - core, k], wsend.at[k], wrecv.at[k], at(z, x, 1 - core)).wait_recv()

    @pl.when(source)
    def _():
        for cls in (0, 1):
            arrived(z, x, 1 - core, cls)
            own_copies(cls)[2].wait()
        multiply(z, x)

    for s in (0, 1):
        arrived(near, x, s, 0)
    on_a = forward(near, x, via, 0, 11, at(onward, x, core))
    on_a.start()

    def spread():
        return [
            forward(z, other, s, 0, 12 + s * 2 + i, at(zz, x, core))
            for s in (0, 1)
            for i, zz in enumerate((z + 1, z + 3))
        ]

    def crossing():
        return [forward(far, x, s, 1, 12 + s, at(z, other, core)) for s in (0, 1)]

    @pl.when(source)
    def _():
        for s in (0, 1):
            arrived(z, other, s, 0)
        for copy in spread():
            copy.start()
        for s in (0, 1):
            arrived(z, other, s, 1)
        multiply(z, other)

    @pl.when(jnp.logical_not(source))
    def _():
        for s in (0, 1):
            arrived(far, x, s, 1)
        for copy in crossing():
            copy.start()
        multiply(near, x)

    for s in (0, 1):
        arrived(near, other, s, 0)
    on_p = forward(near, other, via, 0, 16, at(onward, x, core))
    on_p.start()

    @pl.when(source)
    def _():
        multiply(near, x)

    for s in (0, 1):
        arrived(near, other, s, 1)
    multiply(near, other)

    @pl.when(jnp.logical_not(source))
    def _():
        for s in (0, 1):
            arrived(far, x, s, 0)
        multiply(far, x)
        for s in (0, 1):
            arrived(far, other, s, 0)
            arrived(far, other, s, 1)
        multiply(far, other)

    for cls in (0, 1):
        away, sibling, here = own_copies(cls)
        for copy in away:
            copy.wait_send()

        @pl.when(core != kept)
        def _():
            sibling.wait_send()

    for copy in fx + [on_b, on_a, on_p]:
        copy.wait_send()

    @pl.when(source)
    def _():
        for copy in spread():
            copy.wait_send()

    @pl.when(jnp.logical_not(source))
    def _():
        for copy in crossing():
            copy.wait_send()

    for copy in w_out_going + proj_going:
        copy.wait_send()
    proj_own.wait()
    remote(
        wout_hbm, wout_all.at[x * 2 + 1 - core], wsend.at[3], wrecv.at[3 + 1 - core], at(z, x, 1 - core)
    ).wait_recv()
    for c in (0, 1):
        remote(wout_hbm, wout_all.at[other * 2 + c], wsend.at[4], wrecv.at[5 + c], across(z, x, c)).wait_recv()


def project(hidden, gain, w_qkv, w_out):
    return pl.pallas_call(
        project_kernel,
        name="project",
        out_shape=(
            jax.ShapeDtypeStruct((6, LEN, 256), jnp.bfloat16),
            jax.ShapeDtypeStruct((4, 256, HW), jnp.bfloat16),
        ),
        in_specs=[
            pl.BlockSpec(memory_space=pltpu.VMEM),
            pl.BlockSpec(memory_space=pltpu.VMEM),
            pl.BlockSpec(memory_space=pltpu.HBM),
            pl.BlockSpec(memory_space=pltpu.HBM),
        ],
        out_specs=(pl.BlockSpec(memory_space=pltpu.VMEM), pl.BlockSpec(memory_space=pltpu.HBM)),
        scratch_shapes=[
            pltpu.VMEM((ROWS, D), jnp.bfloat16),
            pltpu.VMEM((4, 2 * ROWS, D), jnp.bfloat16),
            pltpu.VMEM((2, 3, D, 256), jnp.bfloat16),
            pltpu.SemaphoreType.DMA((17,)),
            pltpu.SemaphoreType.DMA((16,)),
            pltpu.SemaphoreType.DMA((6,)),
            pltpu.SemaphoreType.DMA((7,)),
            pltpu.SemaphoreType.DMA((6,)),
        ],
        compiler_params=pltpu.CompilerParams(
            collective_id=0, has_side_effects=True, vmem_limit_bytes=60 * MIB
        ),
    )(hidden, gain, w_qkv, w_out)


def attend_kernel(
    len_ref,
    qkv_ref,
    wout_ref,
    hid_hbm,
    proj_ref,
    student_ref,
    sgain_ref,
    target_ref,
    proj_all,
    norm_all,
    hid_ref,
    ctx,
    ctx_in,
    stage,
    parts,
    norm_own,
    send,
    recv,
    osend,
    orecv,
    psend,
    precv,
    nsend,
    nrecv,
    ysend,
    yrecv,
    csend,
    crecv,
    local,
):
    z, x, core = place()
    other = 1 - x
    kept = z // 2
    length = len_ref[0]
    fetch = pltpu.make_async_copy(hid_hbm.at[:, pl.ds(0, HW)], hid_ref, local.at[0])
    fetch.start()
    rows = student_ref[...].astype(jnp.float32)
    norm_own[...] = rms_norm(rows, sgain_ref[...]).astype(jnp.bfloat16)

    peers = [(z + i, xx) for i in range(4) for xx in (x, other)][1:]
    greet(
        [at(z, x, 1 - core)]
        + [at(zz, xx, c) for zz, xx in peers for c in (0, 1)]
        + [beside(z, x, core, i) for i in (1, 2, 3)]
    )

    y = lax.axis_index("dp") % 4
    chip = z * 2 + x
    quarter = proj_ref.at[:, pl.ds(pl.multiple_of(y * 256, 256), 256)]
    proj_here = pltpu.make_async_copy(quarter, proj_all.at[y, chip, core], local.at[1])
    norm_here = pltpu.make_async_copy(norm_own, norm_all.at[core, chip], local.at[2])
    proj_going = [
        remote(quarter, proj_all.at[y, chip, core], psend.at[i], precv.at[chip], at(zz, xx, core))
        for i, (zz, xx) in enumerate(peers)
    ]
    norm_going = [
        remote(norm_own, norm_all.at[core, chip], nsend.at[i], nrecv.at[chip], at(zz, xx, core))
        for i, (zz, xx) in enumerate(peers)
    ]
    for copy in [proj_here, norm_here] + proj_going + norm_going:
        copy.start()

    def along(i):
        ref = proj_all.at[y, :, core]
        return remote(ref, ref, ysend.at[i - 1], yrecv.at[y], beside(z, x, core, i))

    def spread():
        proj_here.wait()
        for zz, xx in peers:
            ref = proj_all.at[y, (zz % 4) * 2 + xx, core]
            remote(ref, ref, psend.at[0], precv.at[(zz % 4) * 2 + xx], at(z, x, 1 - core)).wait_recv()
        for i in (1, 2, 3):
            along(i).start()

    def sibling(c):
        return [
            remote(norm_all.at[c], norm_all.at[c], csend.at[0], crecv.at[0], at(z, x, 1 - core)),
            remote(proj_all.at[:, :, c], proj_all.at[:, :, c], csend.at[1], crecv.at[1], at(z, x, 1 - core)),
        ]

    def share_norm():
        norm_here.wait()
        for zz, xx in peers:
            ref = norm_all.at[core, (zz % 4) * 2 + xx]
            remote(ref, ref, nsend.at[0], nrecv.at[(zz % 4) * 2 + xx], at(z, x, 1 - core)).wait_recv()
        sibling(core)[0].start()

    def share_proj():
        for i in (1, 2, 3):
            ref = proj_all.at[(y + i) % 4, :, core]
            remote(ref, ref, ysend.at[0], yrecv.at[(y + i) % 4], at(z, x, 1 - core)).wait_recv()
        sibling(core)[1].start()

    def attend(chunk, keys, zq, mine):
        start = pl.multiple_of(chunk * 256, 256)
        row = lax.broadcasted_iota(jnp.int32, (256, keys), 0) + start
        col = lax.broadcasted_iota(jnp.int32, (256, keys), 1)
        allowed = (col <= row) & (col < length)

        def pair(half, carry):
            for h in (0, 1):
                lanes = slice(h * HEAD, (h + 1) * HEAD)
                q = qkv_ref[half, pl.ds(start, 256), lanes]
                k = qkv_ref[2 + half, :keys, lanes]
                v = qkv_ref[4 + half, :keys, lanes]
                scores = lax.dot_general(
                    q, k, (((1,), (1,)), ((), ())), preferred_element_type=jnp.float32
                ) * (1.0 / math.sqrt(HEAD))
                scores = jnp.where(allowed, scores, -1e30)
                weights = jnp.exp(scores - jnp.max(scores, axis=-1, keepdims=True))
                total = jnp.sum(weights, axis=-1, keepdims=True)
                out = jnp.dot(weights.astype(jnp.bfloat16), v, preferred_element_type=jnp.float32)
                ctx[zq * 2 + mine, half, :, lanes] = (out / total).astype(jnp.bfloat16)
            return carry

        lax.fori_loop(0, 2, pair, 0)

    def swap(zq):
        return remote(ctx.at[zq * 2], ctx_in.at[zq], send.at[zq], recv.at[zq], at(z, other, core))

    def give(zq, s):
        return remote(
            stage.at[zq, pl.ds(s * ROWS, ROWS)],
            parts.at[z],
            osend.at[zq * 2 + s],
            orecv.at[z],
            at(2 * core + zq, x, s),
        )

    def keep(zq, s):
        return pltpu.make_async_copy(stage.at[zq, pl.ds(s * ROWS, ROWS)], parts.at[z], osend.at[zq * 2 + s])

    for zq in (0, 1):
        keys = (zq + 1) * 512
        attend(zq * 2 + other, keys, zq, 0)
        swap(zq).start()
        (spread, share_norm)[zq]()
        attend(zq * 2 + x, keys, zq, 1)
        swap(zq).wait_recv()

        def one(n, carry):
            lanes = pl.ds(pl.multiple_of(n * 512, 512), 512)
            out = jnp.zeros((256, 512), jnp.float32)
            for half in (0, 1):
                out += jnp.dot(
                    ctx[zq * 2 + 1, half], wout_ref[x * 2 + half, :, lanes], preferred_element_type=jnp.float32
                )
                out += jnp.dot(
                    ctx_in[zq, half], wout_ref[other * 2 + half, :, lanes], preferred_element_type=jnp.float32
                )
            stage[zq, :, lanes] = out.astype(jnp.bfloat16)
            return carry

        lax.fori_loop(0, HW // 512, one, 0)
        for s in (0, 1):
            mine = (2 * core + zq == z) & (core == s)

            @pl.when(mine)
            def _():
                keep(zq, s).start()

            @pl.when(jnp.logical_not(mine))
            def _():
                give(zq, s).start()

    share_proj()
    for zq in (0, 1):
        swap(zq).wait_send()
        for s in (0, 1):
            mine = (2 * core + zq == z) & (core == s)

            @pl.when(mine)
            def _():
                keep(zq, s).wait()

            @pl.when(jnp.logical_not(mine))
            def _():
                give(zq, s).wait_send()

    for far in (0, 1, 2, 3):

        @pl.when((z != far) | (core != kept))
        def _():
            remote(
                parts.at[far], parts.at[far], osend.at[0], orecv.at[far], at(z, x, 1 - core)
            ).wait_recv()

    for copy in proj_going + norm_going + [along(i) for i in (1, 2, 3)] + sibling(core):
        copy.wait_send()
    for copy in sibling(1 - core):
        copy.wait_recv()
    fetch.wait()

    def total(i, carry):
        block = pl.ds(pl.multiple_of(i * 16, 16), 16)
        value = hid_ref[block, :].astype(jnp.float32)
        mixed = parts[0, block, :].astype(jnp.float32)
        for far in (1, 2, 3):
            mixed += parts[far, block, :].astype(jnp.float32)
        target_ref[block, :] = (value + mixed).astype(jnp.bfloat16)
        return carry

    lax.fori_loop(0, ROWS // 16, total, 0)


def attend(length, qkv, w_out, hidden, proj, student, gain):
    vmem = pl.BlockSpec(memory_space=pltpu.VMEM)
    hbm = pl.BlockSpec(memory_space=pltpu.HBM)
    return pl.pallas_call(
        attend_kernel,
        name="attend",
        out_shape=(
            jax.ShapeDtypeStruct((ROWS, HW), jnp.bfloat16),
            jax.ShapeDtypeStruct((4, 8, 2, PROJ, 256), jnp.bfloat16),
            jax.ShapeDtypeStruct((2, 8, ROWS, DS), jnp.bfloat16),
        ),
        in_specs=[pl.BlockSpec(memory_space=pltpu.SMEM), vmem, vmem, hbm, vmem, vmem, vmem],
        out_specs=(vmem, hbm, hbm),
        scratch_shapes=[
            pltpu.VMEM((ROWS, HW), jnp.bfloat16),
            pltpu.VMEM((4, 2, 256, 256), jnp.bfloat16),
            pltpu.VMEM((2, 2, 256, 256), jnp.bfloat16),
            pltpu.VMEM((2, 256, HW), jnp.bfloat16),
            pltpu.VMEM((4, ROWS, HW), jnp.bfloat16),
            pltpu.VMEM((ROWS, DS), jnp.bfloat16),
        ]
        + [pltpu.SemaphoreType.DMA((n,)) for n in (2, 2, 4, 4, 7, 8, 7, 8, 3, 4, 2, 2, 3)],
        compiler_params=pltpu.CompilerParams(
            collective_id=1, has_side_effects=True, vmem_limit_bytes=48 * MIB
        ),
    )(length, qkv, w_out, hidden, proj, student, gain)


def student_kernel(
    len_ref,
    factor_ref,
    target_ref,
    student_ref,
    gain_ref,
    proj_ref,
    norm_ref,
    grad_ref,
    out_ref,
    stat_ref,
    delta,
    flipped,
    flipped_in,
    stat,
    stat_in,
    total,
    total_in,
    piece,
    piece_in,
    summed,
    dsend,
    drecv,
    ssend,
    srecv,
    tsend,
    trecv,
    gsend,
    grecv,
    asend,
    arecv,
    local,
):
    z, x, core = place()
    tp = lax.axis_index("tp")
    dp = lax.axis_index("dp")
    length = len_ref[0]
    factor = factor_ref[0]
    lane = (core * 8 + z * 2 + x) * ROWS

    def mate(i):
        return (tp + i) % 16

    def group(i):
        return (dp + i) % 8

    greet([{"tp": mate(i)} for i in range(1, 16)] + [{"dp": group(i)} for i in range(1, 8)])

    rows = student_ref[...].astype(jnp.float32)
    scale = lax.rsqrt(jnp.mean(rows * rows, axis=-1, keepdims=True) + 1e-06)
    normed = (rows * scale * gain_ref[...]).astype(jnp.bfloat16)
    position = (tp % 8) * ROWS + lax.broadcasted_iota(jnp.int32, (ROWS, 1), 0)
    valid = position < length

    def compare(n, loss):
        base = pl.multiple_of(n * 512, 512)
        mapped = jnp.zeros((ROWS, 512), jnp.float32)
        for k in range(4):
            mapped += lax.dot_general(
                normed[:, k * 256 : (k + 1) * 256],
                proj_ref[k, pl.ds(base, 512), :],
                (((1,), (1,)), ((), ())),
                preferred_element_type=jnp.float32,
            )
        diff = jnp.where(valid, mapped - target_ref[:, pl.ds(base, 512)].astype(jnp.float32), 0.0)
        scaled = diff * factor
        delta[:, pl.ds(base, 512)] = scaled.astype(jnp.bfloat16)
        for t in range(4):
            tile = scaled[:, t * 128 : (t + 1) * 128]
            flipped[pl.ds(pl.multiple_of(base + t * 128, 128), 128), :] = tile.T.astype(jnp.bfloat16)
        return loss + jnp.sum(diff * diff)

    loss = lax.fori_loop(0, HW // 512, compare, jnp.float32(0.0))

    def flip(i):
        src = flipped.at[pl.ds(pl.multiple_of(mate(i) * PROJ, 16), PROJ)]
        dst = flipped_in.at[:, pl.ds(pl.multiple_of(lane, 128), ROWS)]
        return remote(src, dst, dsend.at[i - 1], drecv.at[tp], {"tp": mate(i)})

    own_flip = pltpu.make_async_copy(
        flipped.at[pl.ds(pl.multiple_of(tp * PROJ, 16), PROJ)],
        flipped_in.at[:, pl.ds(pl.multiple_of(lane, 128), ROWS)],
        local.at[0],
    )
    for i in range(1, 16):
        flip(i).start()
    own_flip.start()

    back = [
        jnp.dot(delta[...], proj_ref[k], preferred_element_type=jnp.float32) for k in range(4)
    ]
    dots = jnp.zeros((ROWS, 1), jnp.float32)
    for k in range(4):
        cols = slice(k * 256, (k + 1) * 256)
        dots += jnp.sum(back[k] * gain_ref[:, cols] * rows[:, cols], axis=-1, keepdims=True)
    shift = dots * (scale * scale * scale) * (1.0 / DS)
    for k in range(4):
        cols = slice(k * 256, (k + 1) * 256)
        grad_ref[:, cols] = (
            back[k] * gain_ref[:, cols] * scale - rows[:, cols] * shift
        ).astype(jnp.bfloat16)
        part = jnp.sum(back[k] * (rows[:, cols] * scale), axis=0, keepdims=True)
        stat[2 * k : 2 * k + 1, :] = part[:, :128]
        stat[2 * k + 1 : 2 * k + 2, :] = part[:, 128:]
    stat[8:16, :] = jnp.zeros((8, 128), jnp.float32) + loss

    def tell(i):
        return remote(stat, stat_in.at[tp], ssend.at[i - 1], srecv.at[tp], {"tp": mate(i)})

    for i in range(1, 16):
        tell(i).start()

    for i in range(1, 16):
        far = mate(i)
        got = flipped_in.at[
            :, pl.ds(pl.multiple_of(((far % 2) * 8 + far // 2) * ROWS, 128), ROWS)
        ]
        remote(got, got, dsend.at[0], drecv.at[far], {"tp": far}).wait_recv()
    own_flip.wait()

    def hand(i):
        return remote(piece.at[group(i)], piece_in.at[dp], gsend.at[i - 1], grecv.at[dp], {"dp": group(i)})

    for k in range(4):
        out = jnp.dot(
            flipped_in[...], norm_ref[:, k * 256 : (k + 1) * 256], preferred_element_type=jnp.float32
        ).astype(jnp.bfloat16)
        piece[2 * k] = out[:, :128]
        piece[2 * k + 1] = out[:, 128:]
    for i in range(1, 8):
        hand(i).start()

    for i in range(1, 16):
        far = stat_in.at[mate(i)]
        remote(far, far, ssend.at[0], srecv.at[mate(i)], {"tp": mate(i)}).wait_recv()
    stat_in[tp] = stat[...]
    total[...] = jnp.sum(stat_in[...], axis=0)

    def tell_groups(i):
        return remote(total, total_in.at[dp], tsend.at[i - 1], trecv.at[dp], {"dp": group(i)})

    for i in range(1, 8):
        tell_groups(i).start()

    for i in range(1, 8):
        far = piece_in.at[group(i)]
        remote(far, far, gsend.at[0], grecv.at[group(i)], {"dp": group(i)}).wait_recv()
    piece_in[dp] = piece[dp]
    acc = jnp.zeros((PROJ, 128), jnp.float32)
    for k in range(8):
        acc += piece_in[k].astype(jnp.float32)
    summed[...] = acc.astype(jnp.bfloat16)

    def column(g):
        return out_ref.at[:, pl.ds(pl.multiple_of(g * 128, 128), 128)]

    def publish(i):
        return remote(summed, column(dp), asend.at[i - 1], arecv.at[dp], {"dp": group(i)})

    own_column = pltpu.make_async_copy(summed, column(dp), local.at[1])
    own_column.start()
    for i in range(1, 8):
        publish(i).start()

    for i in range(1, 8):
        far = total_in.at[group(i)]
        remote(far, far, tsend.at[0], trecv.at[group(i)], {"dp": group(i)}).wait_recv()
    total_in[dp] = total[...]
    stat_ref[...] = jnp.sum(total_in[...], axis=0)

    for i in range(1, 8):
        far = column(group(i))
        remote(far, far, asend.at[0], arecv.at[group(i)], {"dp": group(i)}).wait_recv()
    own_column.wait()
    for i in range(1, 16):
        flip(i).wait_send()
        tell(i).wait_send()
    for i in range(1, 8):
        hand(i).wait_send()
        tell_groups(i).wait_send()
        publish(i).wait_send()


def student(length, factor, target, rows, gain, proj, norm):
    vmem = pl.BlockSpec(memory_space=pltpu.VMEM)
    smem = pl.BlockSpec(memory_space=pltpu.SMEM)
    return pl.pallas_call(
        student_kernel,
        name="student",
        out_shape=(
            jax.ShapeDtypeStruct((ROWS, DS), jnp.bfloat16),
            jax.ShapeDtypeStruct((PROJ, DS), jnp.bfloat16),
            jax.ShapeDtypeStruct((16, 128), jnp.float32),
        ),
        in_specs=[smem, smem] + [vmem] * 5,
        out_specs=(vmem, vmem, vmem),
        scratch_shapes=[
            pltpu.VMEM((ROWS, HW), jnp.bfloat16),
            pltpu.VMEM((HW, ROWS), jnp.bfloat16),
            pltpu.VMEM((PROJ, 2 * LEN), jnp.bfloat16),
            pltpu.VMEM((16, 128), jnp.float32),
            pltpu.VMEM((16, 16, 128), jnp.float32),
            pltpu.VMEM((16, 128), jnp.float32),
            pltpu.VMEM((8, 16, 128), jnp.float32),
            pltpu.VMEM((8, PROJ, 128), jnp.bfloat16),
            pltpu.VMEM((8, PROJ, 128), jnp.bfloat16),
            pltpu.VMEM((PROJ, 128), jnp.bfloat16),
        ]
        + [pltpu.SemaphoreType.DMA((n,)) for n in (15, 16, 15, 16, 7, 8, 7, 8, 7, 8, 2)],
        compiler_params=pltpu.CompilerParams(
            collective_id=2, has_side_effects=True, vmem_limit_bytes=48 * MIB
        ),
    )(length, factor, target, rows, gain, proj, norm)


def shards(
    hidden_in, norm_gain, w_qkv, w_out, lengths, student_in, student_gain, proj_weight, loss_scale
):
    tp = lax.axis_index("tp")
    group = lax.axis_index("dp")
    count = jnp.sum(lengths).astype(jnp.float32)
    factor = 2.0 * loss_scale / (count * HW)
    gain = student_gain.reshape(1, DS)

    qkv, w_out_all = project(hidden_in, norm_gain.reshape(1, D), w_qkv, w_out)
    target, proj_all, norm_all = attend(
        lax.dynamic_slice_in_dim(lengths, group * SEQS + tp % 2, 1),
        qkv,
        w_out_all,
        hidden_in,
        proj_weight,
        student_in,
        gain,
    )
    row_grad, proj_grad, stat = student(
        lax.dynamic_slice_in_dim(lengths, group * SEQS + tp // 8, 1),
        factor,
        target,
        student_in,
        gain,
        proj_all.reshape(4, HW, 256),
        norm_all.reshape(2 * LEN, DS),
    )
    return row_grad, proj_grad, stat[:8].reshape(DS), stat[8, 0] / (count * HW)


def solution(mesh):
    placed = (
        P(("dp", "tp"), None),
        P(),
        P(None, None, "tp"),
        P("tp", None),
        P(),
        P(("dp", "tp"), None),
        P(),
        P("tp", None),
        P(),
    )
    return jax.shard_map(
        shards,
        mesh=mesh,
        in_specs=placed,
        out_specs=(P(("dp", "tp"), None), P("tp", None), P(), P()),
        check_vma=False,
    )
```

```python
import functools
import math

import jax
import jax.numpy as jnp
from jax import lax
from jax.experimental import pallas as pl
from jax.experimental.pallas import tpu as pltpu
from jax.sharding import PartitionSpec as P

HEAD = 128
HW = 3584
LEN = 1024
SEQS = 2
D = 7168
DS = 1024
PROJ = 224
ROWS = 128
FIRST = 80
MESH = pl.DeviceIdType.MESH
MIB = 1 << 20


def place():
    tp = lax.axis_index("tp")
    return tp // 4, (tp // 2) % 2, tp % 2


def at(z, x, core):
    return {"tp": (z % 4) * 4 + x * 2 + core}


def across(z, x, core):
    dp = lax.axis_index("dp")
    return {"tp": z * 4 + (1 - x) * 2 + core, "dp": (1 - dp // 4) * 4 + dp % 4}


def beside(z, x, core, i):
    dp = lax.axis_index("dp")
    return {"tp": z * 4 + x * 2 + core, "dp": dp // 4 * 4 + (dp + i) % 4}


def remote(src, dst, send, recv, device):
    return pltpu.make_async_remote_copy(
        src_ref=src, dst_ref=dst, send_sem=send, recv_sem=recv, device_id=device, device_id_type=MESH
    )


def rms_norm(rows, gain):
    return rows * lax.rsqrt(jnp.mean(rows * rows, axis=-1, keepdims=True) + 1e-06) * gain


def greet(devices):
    barrier = pltpu.get_barrier_semaphore()
    for device in devices:
        pl.semaphore_signal(barrier, 1, device_id=device, device_id_type=MESH)
    pl.semaphore_wait(barrier, len(devices))


def project_kernel(
    x_ref,
    gain_ref,
    w_hbm,
    wout_hbm,
    proj_hbm,
    qkv_ref,
    wout_all,
    proj_all,
    normed,
    rows,
    w,
    send,
    recv,
    wsend,
    wrecv,
    psend,
    precv,
    ysend,
    yrecv,
    local,
):
    z, x, core = place()
    other = 1 - x
    kept = z // 2
    rel = (z - 2 * core + 4) % 4
    ahead = (rel == 0) | (rel == 3)
    step = jnp.where(ahead, 1, -1)
    near = (z + step + 4) % 4
    onward = (z - step + 4) % 4
    via = jnp.where(ahead, 1, 0)
    far = (z + 2) % 4

    greet(
        [at(z, x, 1 - core)]
        + [at(zz, x, c) for zz in (z + 1, z + 3) for c in (0, 1)]
        + [at(z, other, c) for c in (0, 1)]
        + [across(z, x, c) for c in (0, 1)]
        + [at(far, x, core)]
        + [beside(z, x, core, i) for i in (1, 2, 3)]
    )

    y = lax.axis_index("dp") % 4

    def held(chip_z, chip_x):
        return proj_all.at[y, (chip_z % 4) * 2 + chip_x, core]

    def held_sem(chip_z, chip_x):
        return precv.at[(chip_z % 4) * 2 + chip_x]

    quarter = proj_hbm.at[:, pl.ds(pl.multiple_of(y * 256, 256), 256)]
    quarter_here = pltpu.make_async_copy(quarter, held(z, x), local.at[6])
    quarter_going = [
        remote(quarter, held(z, x), psend.at[i], held_sem(z, x), at(zz, xx, core))
        for i, (zz, xx) in enumerate(((z + 1, x), (z + 3, x), (z + 2, x), (z, other)))
    ]
    for copy in [quarter_here] + quarter_going:
        copy.start()

    def quarter_wait(chip_z, chip_x):
        ref = held(chip_z, chip_x)
        remote(ref, ref, psend.at[0], held_sem(chip_z, chip_x), at(z, other, core)).wait_recv()

    def quarter_on(i):
        ref = held(z + i, x)
        return remote(ref, ref, psend.at[3 + i], held_sem(z + i, x), at(z, other, core))

    def along(i):
        ref = proj_all.at[y, :, core]
        return remote(ref, ref, ysend.at[i - 1], yrecv.at[y], beside(z, x, core, i))

    def halves(c):
        ref = proj_all.at[:, :, c]
        return remote(ref, ref, ysend.at[3], yrecv.at[4], at(z, x, 1 - core))

    w_out_going = [
        remote(w_hbm.at[k], w.at[core, k], wsend.at[k], wrecv.at[k], at(z, x, 1 - core)) for k in range(3)
    ]
    w_own = [pltpu.make_async_copy(w_hbm.at[k], w.at[core, k], local.at[k]) for k in range(3)]
    slot = x * 2 + core
    proj_going = [
        remote(wout_hbm, wout_all.at[slot], wsend.at[3], wrecv.at[3 + core], at(z, x, 1 - core)),
        remote(wout_hbm, wout_all.at[slot], wsend.at[4], wrecv.at[5 + core], across(z, x, 0)),
        remote(wout_hbm, wout_all.at[slot], wsend.at[5], wrecv.at[5 + core], across(z, x, 1)),
    ]
    proj_own = pltpu.make_async_copy(wout_hbm, wout_all.at[slot], local.at[3])
    for copy in w_own + w_out_going + proj_going + [proj_own]:
        copy.start()

    def part(chunk_z, chunk_x, s, cls):
        chunk = (chunk_z % 2) * 2 + chunk_x
        start, size = ((0, FIRST), (FIRST, ROWS - FIRST))[cls]
        return rows.at[chunk, pl.ds(pl.multiple_of(s * ROWS + start, 16), size)]

    def sem(chunk_z, chunk_x, s, cls):
        return recv.at[((chunk_z % 2) * 2 + chunk_x) * 4 + s * 2 + cls]

    def arrived(chunk_z, chunk_x, s, cls):
        ref = part(chunk_z, chunk_x, s, cls)
        remote(ref, ref, send.at[0], sem(chunk_z, chunk_x, s, cls), at(z, x, 1 - core)).wait_recv()

    def forward(chunk_z, chunk_x, s, cls, index, device):
        ref = part(chunk_z, chunk_x, s, cls)
        return remote(ref, ref, send.at[index], sem(chunk_z, chunk_x, s, cls), device)

    def norm(start, size):
        def one(i, carry):
            block = pl.ds(pl.multiple_of(start + i * 16, 16), 16)
            values = x_ref[block, :].astype(jnp.float32)
            centred = values - jnp.mean(values, axis=-1, keepdims=True)
            spread = jnp.mean(centred * centred, axis=-1, keepdims=True)
            normed[block, :] = (centred * lax.rsqrt(spread + 1e-05) * gain_ref[...]).astype(jnp.bfloat16)
            return carry

        lax.fori_loop(0, size // 16, one, 0)

    def own_copies(cls):
        start, size = ((0, FIRST), (FIRST, ROWS - FIRST))[cls]
        src = normed.at[pl.ds(start, size)]
        dst = part(z, x, core, cls)
        got = sem(z, x, core, cls)
        base = cls * 4
        return (
            [
                remote(src, dst, send.at[base], got, at(z + 1, x, kept)),
                remote(src, dst, send.at[base + 1], got, at(z + 3, x, kept)),
                remote(src, dst, send.at[base + 2], got, at(z, other, kept)),
            ],
            remote(src, dst, send.at[base + 3], got, at(z, x, 1 - core)),
            pltpu.make_async_copy(src, dst, local.at[4 + cls]),
        )

    for cls, (start, size) in ((1, (FIRST, ROWS - FIRST)), (0, (0, FIRST))):
        norm(start, size)
        away, sibling, here = own_copies(cls)
        for copy in away:
            copy.start()

        @pl.when(core == kept)
        def _():
            here.start()

        @pl.when(core != kept)
        def _():
            sibling.start()

    def multiply(chunk_z, chunk_x):
        chunk = (chunk_z % 2) * 2 + chunk_x

        def one(n, carry):
            out = jnp.dot(rows[chunk], w[n % 2, n // 2], preferred_element_type=jnp.float32)
            qkv_ref[n, pl.ds(pl.multiple_of(chunk * 256, 256), 256), :] = out.astype(jnp.bfloat16)
            return carry

        lax.fori_loop(0, 6, one, 0)

    for i in (1, 3, 2):
        quarter_wait(z + i, x)
        quarter_on(i).start()

    source = rel < 2

    fx = []
    for s in (0, 1):
        arrived(near, x, s, 1)
        fx.append(forward(near, x, s, 1, 8 + s, at(z, other, core)))
        fx[-1].start()
    on_b = forward(near, x, via, 1, 10, at(onward, x, core))
    on_b.start()

    for copy in w_own:
        copy.wait()
    for k in range(3):
        remote(w_hbm.at[k], w.at[1 - core, k], wsend.at[k], wrecv.at[k], at(z, x, 1 - core)).wait_recv()

    @pl.when(source)
    def _():
        for cls in (0, 1):
            arrived(z, x, 1 - core, cls)
            own_copies(cls)[2].wait()
        multiply(z, x)

    quarter_here.wait()
    for i in range(4):
        quarter_wait(z + i, other)
    for i in (1, 2, 3):
        along(i).start()

    for s in (0, 1):
        arrived(near, x, s, 0)
    on_a = forward(near, x, via, 0, 11, at(onward, x, core))
    on_a.start()

    def spread():
        return [
            forward(z, other, s, 0, 12 + s * 2 + i, at(zz, x, core))
            for s in (0, 1)
            for i, zz in enumerate((z + 1, z + 3))
        ]

    def crossing():
        return [forward(far, x, s, 1, 12 + s, at(z, other, core)) for s in (0, 1)]

    @pl.when(source)
    def _():
        for s in (0, 1):
            arrived(z, other, s, 0)
        for copy in spread():
            copy.start()
        for s in (0, 1):
            arrived(z, other, s, 1)
        multiply(z, other)

    @pl.when(jnp.logical_not(source))
    def _():
        for s in (0, 1):
            arrived(far, x, s, 1)
        for copy in crossing():
            copy.start()
        multiply(near, x)

    for s in (0, 1):
        arrived(near, other, s, 0)
    on_p = forward(near, other, via, 0, 16, at(onward, x, core))
    on_p.start()

    @pl.when(source)
    def _():
        multiply(near, x)

    for s in (0, 1):
        arrived(near, other, s, 1)
    multiply(near, other)

    for i in (1, 2, 3):
        ref = proj_all.at[(y + i) % 4, :, core]
        remote(ref, ref, ysend.at[0], yrecv.at[(y + i) % 4], at(z, x, 1 - core)).wait_recv()
    halves(core).start()

    @pl.when(jnp.logical_not(source))
    def _():
        for s in (0, 1):
            arrived(far, x, s, 0)
        multiply(far, x)
        for s in (0, 1):
            arrived(far, other, s, 0)
            arrived(far, other, s, 1)
        multiply(far, other)

    for cls in (0, 1):
        away, sibling, here = own_copies(cls)
        for copy in away:
            copy.wait_send()

        @pl.when(core != kept)
        def _():
            sibling.wait_send()

    for copy in fx + [on_b, on_a, on_p]:
        copy.wait_send()

    @pl.when(source)
    def _():
        for copy in spread():
            copy.wait_send()

    @pl.when(jnp.logical_not(source))
    def _():
        for copy in crossing():
            copy.wait_send()

    for copy in w_out_going + proj_going + quarter_going + [quarter_on(i) for i in (1, 2, 3)]:
        copy.wait_send()
    for copy in [along(i) for i in (1, 2, 3)] + [halves(core)]:
        copy.wait_send()
    halves(1 - core).wait_recv()
    proj_own.wait()
    remote(
        wout_hbm, wout_all.at[x * 2 + 1 - core], wsend.at[3], wrecv.at[3 + 1 - core], at(z, x, 1 - core)
    ).wait_recv()
    for c in (0, 1):
        remote(wout_hbm, wout_all.at[other * 2 + c], wsend.at[4], wrecv.at[5 + c], across(z, x, c)).wait_recv()


def project(hidden, gain, w_qkv, w_out, proj):
    vmem = pl.BlockSpec(memory_space=pltpu.VMEM)
    hbm = pl.BlockSpec(memory_space=pltpu.HBM)
    return pl.pallas_call(
        project_kernel,
        name="project",
        out_shape=(
            jax.ShapeDtypeStruct((6, LEN, 256), jnp.bfloat16),
            jax.ShapeDtypeStruct((4, 256, HW), jnp.bfloat16),
            jax.ShapeDtypeStruct((4, 8, 2, PROJ, 256), jnp.bfloat16),
        ),
        in_specs=[vmem, vmem, hbm, hbm, hbm],
        out_specs=(vmem, hbm, hbm),
        scratch_shapes=[
            pltpu.VMEM((ROWS, D), jnp.bfloat16),
            pltpu.VMEM((4, 2 * ROWS, D), jnp.bfloat16),
            pltpu.VMEM((2, 3, D, 256), jnp.bfloat16),
        ]
        + [pltpu.SemaphoreType.DMA((n,)) for n in (17, 16, 6, 7, 7, 8, 4, 5, 7)],
        compiler_params=pltpu.CompilerParams(
            collective_id=0, has_side_effects=True, vmem_limit_bytes=60 * MIB
        ),
    )(hidden, gain, w_qkv, w_out, proj)


def student_kernel(
    key_len_ref,
    row_len_ref,
    factor_ref,
    qkv_ref,
    wout_hbm,
    hid_hbm,
    proj_hbm,
    student_ref,
    gain_ref,
    grad_ref,
    out_ref,
    stat_ref,
    wout_ref,
    hid_ref,
    proj_ref,
    norm_ref,
    normed,
    ctx,
    ctx_in,
    stage,
    parts,
    mapped,
    delta,
    flipped,
    flipped_in,
    stat,
    stat_in,
    total,
    total_in,
    piece,
    piece_in,
    summed,
    send,
    recv,
    osend,
    orecv,
    nsend,
    nrecv,
    dsend,
    drecv,
    ssend,
    srecv,
    tsend,
    trecv,
    gsend,
    grecv,
    asend,
    arecv,
    local,
):
    z, x, core = place()
    other = 1 - x
    kept = z // 2
    tp = lax.axis_index("tp")
    dp = lax.axis_index("dp")
    factor = factor_ref[0]
    key_len = key_len_ref[0]

    fetch_wout = pltpu.make_async_copy(wout_hbm, wout_ref, local.at[0])
    fetch_hid = pltpu.make_async_copy(hid_hbm.at[:, pl.ds(0, HW)], hid_ref, local.at[1])
    fetch_proj = pltpu.make_async_copy(proj_hbm, proj_ref, local.at[2])
    for copy in (fetch_wout, fetch_hid, fetch_proj):
        copy.start()

    def mate(i):
        return (tp + i) % 16

    def group(i):
        return (dp + i) % 8

    greet([{"tp": mate(i)} for i in range(1, 16)] + [{"dp": group(i)} for i in range(1, 8)])

    rows = student_ref[...].astype(jnp.float32)
    scale = lax.rsqrt(jnp.mean(rows * rows, axis=-1, keepdims=True) + 1e-06)
    normed[...] = (rows * scale * gain_ref[...]).astype(jnp.bfloat16)

    def block(chip_z, chip_x, c):
        chip = (chip_z % 4) * 2 + chip_x
        return norm_ref.at[pl.ds(pl.multiple_of((c * 8 + chip) * ROWS, 128), ROWS)]

    def block_sem(chip_z, chip_x):
        return nrecv.at[(chip_z % 4) * 2 + chip_x]

    norm_here = pltpu.make_async_copy(normed, block(z, x, core), local.at[3])
    norm_going = [
        remote(normed, block(z, x, core), nsend.at[i], block_sem(z, x), at(zz, xx, core))
        for i, (zz, xx) in enumerate(((z + 1, x), (z + 3, x), (z + 2, x), (z, other)))
    ]
    for copy in [norm_here] + norm_going:
        copy.start()

    def norm_wait(chip_z, chip_x):
        ref = block(chip_z, chip_x, core)
        remote(ref, ref, nsend.at[0], block_sem(chip_z, chip_x), at(z, other, core)).wait_recv()

    def norm_on(i):
        ref = block(z + i, x, core)
        return remote(ref, ref, nsend.at[3 + i], block_sem(z + i, x), at(z, other, core))

    def norm_half(c):
        ref = norm_ref.at[pl.ds(pl.multiple_of(c * LEN, 128), LEN)]
        return remote(ref, ref, nsend.at[7], nrecv.at[8], at(z, x, 1 - core))

    def attend(chunk, keys, zq, mine):
        start = pl.multiple_of(chunk * 256, 256)
        row = lax.broadcasted_iota(jnp.int32, (256, keys), 0) + start
        col = lax.broadcasted_iota(jnp.int32, (256, keys), 1)
        allowed = (col <= row) & (col < key_len)

        def pair(half, carry):
            for h in (0, 1):
                lanes = slice(h * HEAD, (h + 1) * HEAD)
                q = qkv_ref[half, pl.ds(start, 256), lanes]
                k = qkv_ref[2 + half, :keys, lanes]
                v = qkv_ref[4 + half, :keys, lanes]
                scores = lax.dot_general(
                    q, k, (((1,), (1,)), ((), ())), preferred_element_type=jnp.float32
                ) * (1.0 / math.sqrt(HEAD))
                scores = jnp.where(allowed, scores, -1e30)
                weights = jnp.exp(scores - jnp.max(scores, axis=-1, keepdims=True))
                norm = jnp.sum(weights, axis=-1, keepdims=True)
                out = jnp.dot(weights.astype(jnp.bfloat16), v, preferred_element_type=jnp.float32)
                ctx[zq * 2 + mine, half, :, lanes] = (out / norm).astype(jnp.bfloat16)
            return carry

        lax.fori_loop(0, 2, pair, 0)

    def swap(zq):
        return remote(ctx.at[zq * 2], ctx_in.at[zq], send.at[zq], recv.at[zq], at(z, other, core))

    def give(zq, s):
        return remote(
            stage.at[zq, pl.ds(s * ROWS, ROWS)],
            parts.at[z],
            osend.at[zq * 2 + s],
            orecv.at[z],
            at(2 * core + zq, x, s),
        )

    def keep(zq, s):
        return pltpu.make_async_copy(stage.at[zq, pl.ds(s * ROWS, ROWS)], parts.at[z], osend.at[zq * 2 + s])

    def project_out(zq):
        def one(n, carry):
            lanes = pl.ds(pl.multiple_of(n * 512, 512), 512)
            out = jnp.zeros((256, 512), jnp.float32)
            for half in (0, 1):
                out += jnp.dot(
                    ctx[zq * 2 + 1, half], wout_ref[x * 2 + half, :, lanes], preferred_element_type=jnp.float32
                )
                out += jnp.dot(
                    ctx_in[zq, half], wout_ref[other * 2 + half, :, lanes], preferred_element_type=jnp.float32
                )
            stage[zq, :, lanes] = out.astype(jnp.bfloat16)
            return carry

        lax.fori_loop(0, HW // 512, one, 0)
        for s in (0, 1):
            mine = (2 * core + zq == z) & (core == s)

            @pl.when(mine)
            def _():
                keep(zq, s).start()

            @pl.when(jnp.logical_not(mine))
            def _():
                give(zq, s).start()

    attend(other, 512, 0, 0)
    swap(0).start()
    attend(x, 512, 0, 1)
    for i in (1, 3, 2):
        norm_wait(z + i, x)
        norm_on(i).start()
    fetch_wout.wait()
    swap(0).wait_recv()
    project_out(0)
    attend(2 + other, 1024, 1, 0)
    swap(1).start()
    attend(2 + x, 1024, 1, 1)
    swap(1).wait_recv()
    project_out(1)
    norm_here.wait()
    for i in range(4):
        norm_wait(z + i, other)
    norm_half(core).start()

    fetch_proj.wait()

    def map_rows(n, carry):
        base = pl.multiple_of(n * 512, 512)
        out = jnp.zeros((ROWS, 512), jnp.float32)
        for k in range(4):
            out += lax.dot_general(
                normed[:, k * 256 : (k + 1) * 256],
                proj_ref[k, pl.ds(base, 512), :],
                (((1,), (1,)), ((), ())),
                preferred_element_type=jnp.float32,
            )
        mapped[:, pl.ds(base, 512)] = out
        return carry

    lax.fori_loop(0, HW // 512, map_rows, 0)
    fetch_hid.wait()

    for far in (0, 1, 2, 3):

        @pl.when((z != far) | (core != kept))
        def _():
            remote(
                parts.at[far], parts.at[far], osend.at[0], orecv.at[far], at(z, x, 1 - core)
            ).wait_recv()

    for zq in (0, 1):
        mine = (2 * core + zq == z) & (core == kept)

        @pl.when(mine)
        def _():
            pltpu.make_async_copy(
                stage.at[zq, pl.ds(pl.multiple_of(core * ROWS, 16), ROWS)], parts.at[z], osend.at[zq * 2 + core]
            ).wait()

    position = (tp % 8) * ROWS + lax.broadcasted_iota(jnp.int32, (ROWS, 1), 0)
    valid = position < row_len_ref[0]

    def compare(n, loss):
        cols = pl.ds(pl.multiple_of(n * 512, 512), 512)
        mixed = parts[0, :, cols].astype(jnp.float32)
        for far in (1, 2, 3):
            mixed += parts[far, :, cols].astype(jnp.float32)
        target = (hid_ref[:, cols].astype(jnp.float32) + mixed).astype(jnp.bfloat16)
        diff = jnp.where(valid, mapped[:, cols] - target.astype(jnp.float32), 0.0)
        scaled = diff * factor
        delta[:, cols] = scaled.astype(jnp.bfloat16)
        for t in range(4):
            tile = scaled[:, t * 128 : (t + 1) * 128]
            flipped[pl.ds(pl.multiple_of(n * 512 + t * 128, 128), 128), :] = tile.T.astype(jnp.bfloat16)
        return loss + jnp.sum(diff * diff)

    loss = lax.fori_loop(0, HW // 512, compare, jnp.float32(0.0))

    lane = pl.ds(pl.multiple_of((core * 8 + z * 2 + x) * ROWS, 128), ROWS)

    def flip(i):
        src = flipped.at[pl.ds(pl.multiple_of(mate(i) * PROJ, 16), PROJ)]
        return remote(src, flipped_in.at[:, lane], dsend.at[i - 1], drecv.at[tp], {"tp": mate(i)})

    own_flip = pltpu.make_async_copy(
        flipped.at[pl.ds(pl.multiple_of(tp * PROJ, 16), PROJ)], flipped_in.at[:, lane], local.at[4]
    )
    for i in range(1, 16):
        flip(i).start()
    own_flip.start()

    back = [jnp.dot(delta[...], proj_ref[k], preferred_element_type=jnp.float32) for k in range(4)]
    dots = jnp.zeros((ROWS, 1), jnp.float32)
    for k in range(4):
        cols = slice(k * 256, (k + 1) * 256)
        dots += jnp.sum(back[k] * gain_ref[:, cols] * rows[:, cols], axis=-1, keepdims=True)
    shift = dots * (scale * scale * scale) * (1.0 / DS)
    for k in range(4):
        cols = slice(k * 256, (k + 1) * 256)
        grad_ref[:, cols] = (
            back[k] * gain_ref[:, cols] * scale - rows[:, cols] * shift
        ).astype(jnp.bfloat16)
        part = jnp.sum(back[k] * (rows[:, cols] * scale), axis=0, keepdims=True)
        stat[2 * k : 2 * k + 1, :] = part[:, :128]
        stat[2 * k + 1 : 2 * k + 2, :] = part[:, 128:]
    stat[8:16, :] = jnp.zeros((8, 128), jnp.float32) + loss

    def tell(i):
        return remote(stat, stat_in.at[tp], ssend.at[i - 1], srecv.at[tp], {"tp": mate(i)})

    for i in range(1, 16):
        tell(i).start()

    norm_half(1 - core).wait_recv()
    for i in range(1, 16):
        far = mate(i)
        got = flipped_in.at[:, pl.ds(pl.multiple_of(((far % 2) * 8 + far // 2) * ROWS, 128), ROWS)]
        remote(got, got, dsend.at[0], drecv.at[far], {"tp": far}).wait_recv()
    own_flip.wait()

    def hand(i):
        return remote(piece.at[group(i)], piece_in.at[dp], gsend.at[i - 1], grecv.at[dp], {"dp": group(i)})

    for k in range(4):
        out = jnp.dot(
            flipped_in[...], norm_ref[:, k * 256 : (k + 1) * 256], preferred_element_type=jnp.float32
        ).astype(jnp.bfloat16)
        piece[2 * k] = out[:, :128]
        piece[2 * k + 1] = out[:, 128:]
    for i in range(1, 8):
        hand(i).start()

    for i in range(1, 16):
        far = stat_in.at[mate(i)]
        remote(far, far, ssend.at[0], srecv.at[mate(i)], {"tp": mate(i)}).wait_recv()
    stat_in[tp] = stat[...]
    total[...] = jnp.sum(stat_in[...], axis=0)

    def tell_groups(i):
        return remote(total, total_in.at[dp], tsend.at[i - 1], trecv.at[dp], {"dp": group(i)})

    for i in range(1, 8):
        tell_groups(i).start()

    for i in range(1, 8):
        far = piece_in.at[group(i)]
        remote(far, far, gsend.at[0], grecv.at[group(i)], {"dp": group(i)}).wait_recv()
    piece_in[dp] = piece[dp]
    acc = jnp.zeros((PROJ, 128), jnp.float32)
    for k in range(8):
        acc += piece_in[k].astype(jnp.float32)
    summed[...] = acc.astype(jnp.bfloat16)

    def column(g):
        return out_ref.at[:, pl.ds(pl.multiple_of(g * 128, 128), 128)]

    def publish(i):
        return remote(summed, column(dp), asend.at[i - 1], arecv.at[dp], {"dp": group(i)})

    own_column = pltpu.make_async_copy(summed, column(dp), local.at[5])
    own_column.start()
    for i in range(1, 8):
        publish(i).start()

    for i in range(1, 8):
        far = total_in.at[group(i)]
        remote(far, far, tsend.at[0], trecv.at[group(i)], {"dp": group(i)}).wait_recv()
    total_in[dp] = total[...]
    stat_ref[...] = jnp.sum(total_in[...], axis=0)

    for zq in (0, 1):
        swap(zq).wait_send()
        for s in (0, 1):

            @pl.when((2 * core + zq != z) | (core != s))
            def _():
                give(zq, s).wait_send()

    for copy in norm_going + [norm_on(i) for i in (1, 2, 3)] + [norm_half(core)]:
        copy.wait_send()
    for i in range(1, 16):
        flip(i).wait_send()
        tell(i).wait_send()
    for i in range(1, 8):
        hand(i).wait_send()
        tell_groups(i).wait_send()
    for i in range(1, 8):
        far = column(group(i))
        remote(far, far, asend.at[0], arecv.at[group(i)], {"dp": group(i)}).wait_recv()
        publish(i).wait_send()
    own_column.wait()


def student(key_len, row_len, factor, qkv, w_out, hidden, proj, rows, gain):
    vmem = pl.BlockSpec(memory_space=pltpu.VMEM)
    smem = pl.BlockSpec(memory_space=pltpu.SMEM)
    hbm = pl.BlockSpec(memory_space=pltpu.HBM)
    return pl.pallas_call(
        student_kernel,
        name="student",
        out_shape=(
            jax.ShapeDtypeStruct((ROWS, DS), jnp.bfloat16),
            jax.ShapeDtypeStruct((PROJ, DS), jnp.bfloat16),
            jax.ShapeDtypeStruct((16, 128), jnp.float32),
        ),
        in_specs=[smem, smem, smem, vmem, hbm, hbm, hbm, vmem, vmem],
        out_specs=(vmem, vmem, vmem),
        scratch_shapes=[
            pltpu.VMEM((4, 256, HW), jnp.bfloat16),
            pltpu.VMEM((ROWS, HW), jnp.bfloat16),
            pltpu.VMEM((4, HW, 256), jnp.bfloat16),
            pltpu.VMEM((2 * LEN, DS), jnp.bfloat16),
            pltpu.VMEM((ROWS, DS), jnp.bfloat16),
            pltpu.VMEM((4, 2, 256, 256), jnp.bfloat16),
            pltpu.VMEM((2, 2, 256, 256), jnp.bfloat16),
            pltpu.VMEM((2, 256, HW), jnp.bfloat16),
            pltpu.VMEM((4, ROWS, HW), jnp.bfloat16),
            pltpu.VMEM((ROWS, HW), jnp.float32),
            pltpu.VMEM((ROWS, HW), jnp.bfloat16),
            pltpu.VMEM((HW, ROWS), jnp.bfloat16),
            pltpu.VMEM((PROJ, 2 * LEN), jnp.bfloat16),
            pltpu.VMEM((16, 128), jnp.float32),
            pltpu.VMEM((16, 16, 128), jnp.float32),
            pltpu.VMEM((16, 128), jnp.float32),
            pltpu.VMEM((8, 16, 128), jnp.float32),
            pltpu.VMEM((8, PROJ, 128), jnp.bfloat16),
            pltpu.VMEM((8, PROJ, 128), jnp.bfloat16),
            pltpu.VMEM((PROJ, 128), jnp.bfloat16),
        ]
        + [pltpu.SemaphoreType.DMA((n,)) for n in (2, 2, 4, 4, 8, 9, 15, 16, 15, 16, 7, 8, 7, 8, 7, 8, 6)],
        compiler_params=pltpu.CompilerParams(
            collective_id=1, has_side_effects=True, vmem_limit_bytes=56 * MIB
        ),
    )(key_len, row_len, factor, qkv, w_out, hidden, proj, rows, gain)


def shards(
    hidden_in, norm_gain, w_qkv, w_out, lengths, student_in, student_gain, proj_weight, loss_scale
):
    tp = lax.axis_index("tp")
    group = lax.axis_index("dp")
    count = jnp.sum(lengths).astype(jnp.float32)
    factor = 2.0 * loss_scale / (count * HW)
    gain = student_gain.reshape(1, DS)

    qkv, w_out_all, proj_all = project(hidden_in, norm_gain.reshape(1, D), w_qkv, w_out, proj_weight)
    row_grad, proj_grad, stat = student(
        lax.dynamic_slice_in_dim(lengths, group * SEQS + tp % 2, 1),
        lax.dynamic_slice_in_dim(lengths, group * SEQS + tp // 8, 1),
        factor,
        qkv,
        w_out_all,
        hidden_in,
        proj_all.reshape(4, HW, 256),
        student_in,
        gain,
    )
    return row_grad, proj_grad, stat[:8].reshape(DS), stat[8, 0] / (count * HW)


def solution(mesh):
    placed = (
        P(("dp", "tp"), None),
        P(),
        P(None, None, "tp"),
        P("tp", None),
        P(),
        P(("dp", "tp"), None),
        P(),
        P("tp", None),
        P(),
    )
    return jax.shard_map(
        shards,
        mesh=mesh,
        in_specs=placed,
        out_specs=(P(("dp", "tp"), None), P("tp", None), P(), P()),
        check_vma=False,
    )
```

```python
import functools
import math

import jax
import jax.numpy as jnp
from jax import lax
from jax.experimental import pallas as pl
from jax.experimental.pallas import tpu as pltpu
from jax.sharding import PartitionSpec as P

HEAD = 128
HW = 3584
HALF = HW // 2
LEN = 1024
SEQS = 2
D = 7168
DS = 1024
PROJ = 224
ROWS = 128
FIRST = 80
MESH = pl.DeviceIdType.MESH
MIB = 1 << 20


def place():
    tp = lax.axis_index("tp")
    return tp // 4, (tp // 2) % 2, tp % 2


def at(z, x, core):
    return {"tp": (z % 4) * 4 + x * 2 + core}


def across(z, x, core):
    dp = lax.axis_index("dp")
    return {"tp": z * 4 + (1 - x) * 2 + core, "dp": (1 - dp // 4) * 4 + dp % 4}


def beside(z, x, core, i):
    dp = lax.axis_index("dp")
    return {"tp": z * 4 + x * 2 + core, "dp": dp // 4 * 4 + (dp + i) % 4}


def remote(src, dst, send, recv, device):
    return pltpu.make_async_remote_copy(
        src_ref=src, dst_ref=dst, send_sem=send, recv_sem=recv, device_id=device, device_id_type=MESH
    )


def rms_norm(rows, gain):
    return rows * lax.rsqrt(jnp.mean(rows * rows, axis=-1, keepdims=True) + 1e-06) * gain


def greet(devices):
    barrier = pltpu.get_barrier_semaphore()
    for device in devices:
        pl.semaphore_signal(barrier, 1, device_id=device, device_id_type=MESH)
    pl.semaphore_wait(barrier, len(devices))


def project_kernel(
    x_ref,
    gain_ref,
    w_hbm,
    wout_hbm,
    proj_hbm,
    qkv_ref,
    wout_all,
    proj_all,
    normed,
    rows,
    w,
    send,
    recv,
    wsend,
    wrecv,
    psend,
    precv,
    ysend,
    yrecv,
    local,
):
    z, x, core = place()
    other = 1 - x
    kept = z // 2
    rel = (z - 2 * core + 4) % 4
    ahead = (rel == 0) | (rel == 3)
    step = jnp.where(ahead, 1, -1)
    near = (z + step + 4) % 4
    onward = (z - step + 4) % 4
    via = jnp.where(ahead, 1, 0)
    far = (z + 2) % 4

    greet(
        [at(z, x, 1 - core)]
        + [at(zz, x, c) for zz in (z + 1, z + 3) for c in (0, 1)]
        + [at(z, other, c) for c in (0, 1)]
        + [across(z, x, c) for c in (0, 1)]
        + [at(far, x, core)]
        + [beside(z, x, core, i) for i in (1, 2, 3)]
    )

    y = lax.axis_index("dp") % 4

    def held(chip_z, chip_x):
        return proj_all.at[y, (chip_z % 4) * 2 + chip_x, core]

    def held_sem(chip_z, chip_x):
        return precv.at[(chip_z % 4) * 2 + chip_x]

    quarter = proj_hbm.at[:, pl.ds(pl.multiple_of(y * 256, 256), 256)]
    quarter_here = pltpu.make_async_copy(quarter, held(z, x), local.at[6])
    quarter_going = [
        remote(quarter, held(z, x), psend.at[i], held_sem(z, x), at(zz, xx, core))
        for i, (zz, xx) in enumerate(((z + 1, x), (z + 3, x), (z + 2, x), (z, other)))
    ]
    for copy in [quarter_here] + quarter_going:
        copy.start()

    def quarter_wait(chip_z, chip_x):
        ref = held(chip_z, chip_x)
        remote(ref, ref, psend.at[0], held_sem(chip_z, chip_x), at(z, other, core)).wait_recv()

    def quarter_on(i):
        ref = held(z + i, x)
        return remote(ref, ref, psend.at[3 + i], held_sem(z + i, x), at(z, other, core))

    def along(i):
        ref = proj_all.at[y, :, core]
        return remote(ref, ref, ysend.at[i - 1], yrecv.at[y], beside(z, x, core, i))

    def halves(c):
        ref = proj_all.at[:, :, c]
        return remote(ref, ref, ysend.at[3], yrecv.at[4], at(z, x, 1 - core))

    w_out_going = [
        remote(w_hbm.at[k], w.at[core, k], wsend.at[k], wrecv.at[k], at(z, x, 1 - core)) for k in range(3)
    ]
    w_own = [pltpu.make_async_copy(w_hbm.at[k], w.at[core, k], local.at[k]) for k in range(3)]
    slot = x * 2 + core
    proj_going = [
        remote(wout_hbm, wout_all.at[slot], wsend.at[3], wrecv.at[3 + core], at(z, x, 1 - core)),
        remote(wout_hbm, wout_all.at[slot], wsend.at[4], wrecv.at[5 + core], across(z, x, 0)),
        remote(wout_hbm, wout_all.at[slot], wsend.at[5], wrecv.at[5 + core], across(z, x, 1)),
    ]
    proj_own = pltpu.make_async_copy(wout_hbm, wout_all.at[slot], local.at[3])
    for copy in w_own + w_out_going + proj_going + [proj_own]:
        copy.start()

    def part(chunk_z, chunk_x, s, cls):
        chunk = (chunk_z % 2) * 2 + chunk_x
        start, size = ((0, FIRST), (FIRST, ROWS - FIRST))[cls]
        return rows.at[chunk, pl.ds(pl.multiple_of(s * ROWS + start, 16), size)]

    def sem(chunk_z, chunk_x, s, cls):
        return recv.at[((chunk_z % 2) * 2 + chunk_x) * 4 + s * 2 + cls]

    def arrived(chunk_z, chunk_x, s, cls):
        ref = part(chunk_z, chunk_x, s, cls)
        remote(ref, ref, send.at[0], sem(chunk_z, chunk_x, s, cls), at(z, x, 1 - core)).wait_recv()

    def forward(chunk_z, chunk_x, s, cls, index, device):
        ref = part(chunk_z, chunk_x, s, cls)
        return remote(ref, ref, send.at[index], sem(chunk_z, chunk_x, s, cls), device)

    def norm(start, size):
        def one(i, carry):
            block = pl.ds(pl.multiple_of(start + i * 16, 16), 16)
            values = x_ref[block, :].astype(jnp.float32)
            centred = values - jnp.mean(values, axis=-1, keepdims=True)
            spread = jnp.mean(centred * centred, axis=-1, keepdims=True)
            normed[block, :] = (centred * lax.rsqrt(spread + 1e-05) * gain_ref[...]).astype(jnp.bfloat16)
            return carry

        lax.fori_loop(0, size // 16, one, 0)

    def own_copies(cls):
        start, size = ((0, FIRST), (FIRST, ROWS - FIRST))[cls]
        src = normed.at[pl.ds(start, size)]
        dst = part(z, x, core, cls)
        got = sem(z, x, core, cls)
        base = cls * 4
        return (
            [
                remote(src, dst, send.at[base], got, at(z + 1, x, kept)),
                remote(src, dst, send.at[base + 1], got, at(z + 3, x, kept)),
                remote(src, dst, send.at[base + 2], got, at(z, other, kept)),
            ],
            remote(src, dst, send.at[base + 3], got, at(z, x, 1 - core)),
            pltpu.make_async_copy(src, dst, local.at[4 + cls]),
        )

    for cls, (start, size) in ((1, (FIRST, ROWS - FIRST)), (0, (0, FIRST))):
        norm(start, size)
        away, sibling, here = own_copies(cls)
        for copy in away:
            copy.start()

        @pl.when(core == kept)
        def _():
            here.start()

        @pl.when(core != kept)
        def _():
            sibling.start()

    def multiply(chunk_z, chunk_x):
        chunk = (chunk_z % 2) * 2 + chunk_x

        def one(n, carry):
            out = jnp.dot(rows[chunk], w[n % 2, n // 2], preferred_element_type=jnp.float32)
            qkv_ref[n, pl.ds(pl.multiple_of(chunk * 256, 256), 256), :] = out.astype(jnp.bfloat16)
            return carry

        lax.fori_loop(0, 6, one, 0)

    for i in (1, 3, 2):
        quarter_wait(z + i, x)
        quarter_on(i).start()

    source = rel < 2

    fx = []
    for s in (0, 1):
        arrived(near, x, s, 1)
        fx.append(forward(near, x, s, 1, 8 + s, at(z, other, core)))
        fx[-1].start()
    on_b = forward(near, x, via, 1, 10, at(onward, x, core))
    on_b.start()

    for copy in w_own:
        copy.wait()
    for k in range(3):
        remote(w_hbm.at[k], w.at[1 - core, k], wsend.at[k], wrecv.at[k], at(z, x, 1 - core)).wait_recv()

    @pl.when(source)
    def _():
        for cls in (0, 1):
            arrived(z, x, 1 - core, cls)
            own_copies(cls)[2].wait()
        multiply(z, x)

    quarter_here.wait()
    for i in range(4):
        quarter_wait(z + i, other)
    for i in (1, 2, 3):
        along(i).start()

    for s in (0, 1):
        arrived(near, x, s, 0)
    on_a = forward(near, x, via, 0, 11, at(onward, x, core))
    on_a.start()

    def spread():
        return [
            forward(z, other, s, 0, 12 + s * 2 + i, at(zz, x, core))
            for s in (0, 1)
            for i, zz in enumerate((z + 1, z + 3))
        ]

    def crossing():
        return [forward(far, x, s, 1, 12 + s, at(z, other, core)) for s in (0, 1)]

    @pl.when(source)
    def _():
        for s in (0, 1):
            arrived(z, other, s, 0)
        for copy in spread():
            copy.start()
        for s in (0, 1):
            arrived(z, other, s, 1)
        multiply(z, other)

    @pl.when(jnp.logical_not(source))
    def _():
        for s in (0, 1):
            arrived(far, x, s, 1)
        for copy in crossing():
            copy.start()
        multiply(near, x)

    for s in (0, 1):
        arrived(near, other, s, 0)
    on_p = forward(near, other, via, 0, 16, at(onward, x, core))
    on_p.start()

    @pl.when(source)
    def _():
        multiply(near, x)

    for s in (0, 1):
        arrived(near, other, s, 1)
    multiply(near, other)

    for i in (1, 2, 3):
        ref = proj_all.at[(y + i) % 4, :, core]
        remote(ref, ref, ysend.at[0], yrecv.at[(y + i) % 4], at(z, x, 1 - core)).wait_recv()
    halves(core).start()

    @pl.when(jnp.logical_not(source))
    def _():
        for s in (0, 1):
            arrived(far, x, s, 0)
        multiply(far, x)
        for s in (0, 1):
            arrived(far, other, s, 0)
            arrived(far, other, s, 1)
        multiply(far, other)

    for cls in (0, 1):
        away, sibling, here = own_copies(cls)
        for copy in away:
            copy.wait_send()

        @pl.when(core != kept)
        def _():
            sibling.wait_send()

    for copy in fx + [on_b, on_a, on_p]:
        copy.wait_send()

    @pl.when(source)
    def _():
        for copy in spread():
            copy.wait_send()

    @pl.when(jnp.logical_not(source))
    def _():
        for copy in crossing():
            copy.wait_send()

    for copy in w_out_going + proj_going + quarter_going + [quarter_on(i) for i in (1, 2, 3)]:
        copy.wait_send()
    for copy in [along(i) for i in (1, 2, 3)] + [halves(core)]:
        copy.wait_send()
    halves(1 - core).wait_recv()
    proj_own.wait()
    remote(
        wout_hbm, wout_all.at[x * 2 + 1 - core], wsend.at[3], wrecv.at[3 + 1 - core], at(z, x, 1 - core)
    ).wait_recv()
    for c in (0, 1):
        remote(wout_hbm, wout_all.at[other * 2 + c], wsend.at[4], wrecv.at[5 + c], across(z, x, c)).wait_recv()


def project(hidden, gain, w_qkv, w_out, proj):
    vmem = pl.BlockSpec(memory_space=pltpu.VMEM)
    hbm = pl.BlockSpec(memory_space=pltpu.HBM)
    return pl.pallas_call(
        project_kernel,
        name="project",
        out_shape=(
            jax.ShapeDtypeStruct((6, LEN, 256), jnp.bfloat16),
            jax.ShapeDtypeStruct((4, 256, HW), jnp.bfloat16),
            jax.ShapeDtypeStruct((4, 8, 2, PROJ, 256), jnp.bfloat16),
        ),
        in_specs=[vmem, vmem, hbm, hbm, hbm],
        out_specs=(vmem, hbm, hbm),
        scratch_shapes=[
            pltpu.VMEM((ROWS, D), jnp.bfloat16),
            pltpu.VMEM((4, 2 * ROWS, D), jnp.bfloat16),
            pltpu.VMEM((2, 3, D, 256), jnp.bfloat16),
        ]
        + [pltpu.SemaphoreType.DMA((n,)) for n in (17, 16, 6, 7, 7, 8, 4, 5, 7)],
        compiler_params=pltpu.CompilerParams(
            collective_id=0, has_side_effects=True, vmem_limit_bytes=60 * MIB
        ),
    )(hidden, gain, w_qkv, w_out, proj)


def student_kernel(
    len_ref,
    scale_ref,
    qkv_ref,
    wout_hbm,
    hid_hbm,
    proj_hbm,
    student_ref,
    gain_ref,
    grad_ref,
    out_ref,
    stat_ref,
    wout_ref,
    hid_ref,
    proj_ref,
    norm_ref,
    normed,
    ctx,
    ctx_in,
    stage,
    parts,
    relay,
    mapped,
    delta,
    flipped,
    flipped_in,
    stat,
    stat_in,
    total,
    total_in,
    piece,
    piece_in,
    summed,
    send,
    recv,
    osend,
    orecv,
    rrecv,
    nsend,
    nrecv,
    dsend,
    drecv,
    ssend,
    srecv,
    tsend,
    trecv,
    gsend,
    grecv,
    asend,
    arecv,
    local,
):
    z, x, core = place()
    other = 1 - x
    kept = z // 2
    tp = lax.axis_index("tp")
    dp = lax.axis_index("dp")
    rel = (z - 2 * core + 4) % 4
    ahead = (rel == 0) | (rel == 3)
    step = jnp.where(ahead, 1, -1)
    via = jnp.where(ahead, 0, 1)
    source = rel < 2
    key_len = len_ref[dp * SEQS + core]
    count = len_ref[0]
    for i in range(1, len_ref.shape[0]):
        count += len_ref[i]
    terms = jnp.full((1, 128), 1.0, jnp.float32) * count.astype(jnp.float32) * HW
    factor = (2.0 * scale_ref[0] / terms)[:, :1]

    fetch_wout = pltpu.make_async_copy(wout_hbm, wout_ref, local.at[0])
    fetch_hid = pltpu.make_async_copy(hid_hbm.at[:, pl.ds(0, HW)], hid_ref, local.at[1])
    fetch_proj = pltpu.make_async_copy(proj_hbm, proj_ref, local.at[2])
    for copy in (fetch_wout, fetch_hid, fetch_proj):
        copy.start()

    def mate(i):
        return (tp + i) % 16

    def group(i):
        return (dp + i) % 8

    greet([{"tp": mate(i)} for i in range(1, 16)] + [{"dp": group(i)} for i in range(1, 8)])

    rows = student_ref[...].astype(jnp.float32)
    scale = lax.rsqrt(jnp.mean(rows * rows, axis=-1, keepdims=True) + 1e-06)
    normed[...] = (rows * scale * gain_ref[...]).astype(jnp.bfloat16)

    def block(chip_z, chip_x, c):
        chip = (chip_z % 4) * 2 + chip_x
        return norm_ref.at[pl.ds(pl.multiple_of((c * 8 + chip) * ROWS, 128), ROWS)]

    def block_sem(chip_z, chip_x):
        return nrecv.at[(chip_z % 4) * 2 + chip_x]

    norm_here = pltpu.make_async_copy(normed, block(z, x, core), local.at[3])
    norm_going = [
        remote(normed, block(z, x, core), nsend.at[i], block_sem(z, x), at(zz, xx, core))
        for i, (zz, xx) in enumerate(((z + 1, x), (z + 3, x), (z + 2, x), (z, other)))
    ]
    for copy in [norm_here] + norm_going[:3]:
        copy.start()

    def norm_wait(chip_z, chip_x):
        ref = block(chip_z, chip_x, core)
        remote(ref, ref, nsend.at[0], block_sem(chip_z, chip_x), at(z, other, core)).wait_recv()

    def norm_on(i):
        ref = block(z + i, x, core)
        return remote(ref, ref, nsend.at[3 + i], block_sem(z + i, x), at(z, other, core))

    def norm_half(c):
        ref = norm_ref.at[pl.ds(pl.multiple_of(c * LEN, 128), LEN)]
        return remote(ref, ref, nsend.at[7], nrecv.at[8], at(z, x, 1 - core))

    def attend(chunk, keys, zq, mine):
        start = pl.multiple_of(chunk * 256, 256)
        row = lax.broadcasted_iota(jnp.int32, (256, keys), 0) + start
        col = lax.broadcasted_iota(jnp.int32, (256, keys), 1)
        allowed = (col <= row) & (col < key_len)

        def pair(half, carry):
            for h in (0, 1):
                lanes = slice(h * HEAD, (h + 1) * HEAD)
                q = qkv_ref[half, pl.ds(start, 256), lanes]
                k = qkv_ref[2 + half, :keys, lanes]
                v = qkv_ref[4 + half, :keys, lanes]
                scores = lax.dot_general(
                    q, k, (((1,), (1,)), ((), ())), preferred_element_type=jnp.float32
                ) * (1.0 / math.sqrt(HEAD))
                scores = jnp.where(allowed, scores, -1e30)
                weights = jnp.exp(scores - jnp.max(scores, axis=-1, keepdims=True))
                norm = jnp.sum(weights, axis=-1, keepdims=True)
                out = jnp.dot(weights.astype(jnp.bfloat16), v, preferred_element_type=jnp.float32)
                ctx[zq * 2 + mine, half, :, lanes] = (out / norm).astype(jnp.bfloat16)
            return carry

        lax.fori_loop(0, 2, pair, 0)

    def swap(zq):
        return remote(ctx.at[zq * 2], ctx_in.at[zq], send.at[zq], recv.at[zq], at(z, other, core))

    def side(half):
        return pl.ds(half * HALF, HALF)

    def summand(zq, s, half):
        return stage.at[zq, pl.ds(pl.multiple_of(s * ROWS, 16), ROWS), side(half)]

    def give(zq, s, half):
        slot = jnp.where(ahead, 2, 1)
        return remote(
            summand(zq, s, half),
            parts.at[slot, :, side(half)],
            osend.at[zq * 4 + s * 2 + half],
            orecv.at[slot * 2 + half],
            at(z + step + 4, x, s),
        )

    def pass_on(zq, s, half):
        return remote(
            summand(zq, s, half),
            relay.at[:, side(half)],
            osend.at[zq * 4 + s * 2 + half],
            rrecv.at[half],
            at(z + (1 if s == 0 else 3), x, core),
        )

    def hand_over(zq, half):
        return remote(
            summand(zq, 1 - core, half),
            parts.at[0, :, side(half)],
            osend.at[zq * 4 + (1 - core) * 2 + half],
            orecv.at[half],
            at(z, x, 1 - core),
        )

    def keep(zq, half):
        return pltpu.make_async_copy(
            summand(zq, core, half), parts.at[0, :, side(half)], osend.at[zq * 4 + core * 2 + half]
        )

    def is_near(zq):
        return (rel == 1 - zq) | (rel == 3 - zq)

    def is_far(zq):
        return rel == 2 + zq

    def is_own(zq):
        return rel == zq

    def project_out(zq, half):
        def one(n, carry):
            lanes = pl.ds(pl.multiple_of(half * HALF + n * 896, 128), 896)
            out = jnp.zeros((256, 896), jnp.float32)
            for k in (0, 1):
                out += jnp.dot(
                    ctx[zq * 2 + 1, k], wout_ref[x * 2 + k, :, lanes], preferred_element_type=jnp.float32
                )
                out += jnp.dot(
                    ctx_in[zq, k], wout_ref[other * 2 + k, :, lanes], preferred_element_type=jnp.float32
                )
            stage[zq, :, lanes] = out.astype(jnp.bfloat16)
            return carry

        lax.fori_loop(0, HALF // 896, one, 0)

        @pl.when(is_far(zq))
        def _():
            for s in (0, 1):
                pass_on(zq, s, half).start()

        @pl.when(is_near(zq))
        def _():
            give(zq, 1 - via, half).start()

        @pl.when(is_own(zq))
        def _():
            keep(zq, half).start()
            hand_over(zq, half).start()

    def join(zq, half):
        @pl.when(is_near(zq))
        def _():
            src = relay.at[:, side(half)]
            remote(src, src, osend.at[0], rrecv.at[half], at(z, x, 1 - core)).wait_recv()

            def one(i, carry):
                here = pl.ds(pl.multiple_of(via * ROWS + i * 16, 16), 16)
                there = pl.ds(pl.multiple_of(i * 16, 16), 16)
                both = stage[zq, here, side(half)].astype(jnp.float32) + relay[there, side(half)].astype(
                    jnp.float32
                )
                stage[zq, here, side(half)] = both.astype(jnp.bfloat16)
                return carry

            lax.fori_loop(0, ROWS // 16, one, 0)
            give(zq, via, half).start()

    attend(other, 512, 0, 0)
    swap(0).start()
    attend(x, 512, 0, 1)
    fetch_wout.wait()
    swap(0).wait_recv()
    for half in (0, 1):
        project_out(0, half)
    attend(2 + other, 1024, 1, 0)
    swap(1).start()
    attend(2 + x, 1024, 1, 1)
    for half in (0, 1):
        join(0, half)
    swap(1).wait_recv()
    for half in (0, 1):
        project_out(1, half)
    norm_going[3].start()
    for i in (1, 3, 2):
        norm_wait(z + i, x)
        norm_on(i).start()
    for half in (0, 1):
        join(1, half)

    fetch_proj.wait()

    def map_rows(n, carry):
        base = pl.multiple_of(n * 512, 512)
        out = jnp.zeros((ROWS, 512), jnp.float32)
        for k in range(4):
            out += lax.dot_general(
                normed[:, k * 256 : (k + 1) * 256],
                proj_ref[k, pl.ds(base, 512), :],
                (((1,), (1,)), ((), ())),
                preferred_element_type=jnp.float32,
            )
        mapped[:, pl.ds(base, 512)] = out
        return carry

    lax.fori_loop(0, HW // 512, map_rows, 0)
    fetch_hid.wait()

    position = (tp % 8) * ROWS + lax.broadcasted_iota(jnp.int32, (ROWS, 1), 0)
    valid = position < len_ref[dp * SEQS + kept]
    lane = pl.ds(pl.multiple_of((core * 8 + z * 2 + x) * ROWS, 128), ROWS)

    def owner(half, i):
        return half * 8 + (tp + i) % 8

    def flip(half, i):
        src = flipped.at[pl.ds(pl.multiple_of(owner(half, i) * PROJ, 16), PROJ)]
        return remote(
            src, flipped_in.at[:, lane], dsend.at[half * 8 + i], drecv.at[tp], {"tp": owner(half, i)}
        )

    own_flip = pltpu.make_async_copy(
        flipped.at[pl.ds(pl.multiple_of(tp * PROJ, 16), PROJ)], flipped_in.at[:, lane], local.at[4]
    )

    def compare(n, loss):
        block_cols = pl.ds(pl.multiple_of(n * 256, 256), 256)
        mixed = parts[0, :, block_cols].astype(jnp.float32)
        for slot in (1, 2):
            mixed += parts[slot, :, block_cols].astype(jnp.float32)
        target = (hid_ref[:, block_cols].astype(jnp.float32) + mixed).astype(jnp.bfloat16)
        diff = jnp.where(valid, mapped[:, block_cols] - target.astype(jnp.float32), 0.0)
        scaled = diff * factor
        delta[:, block_cols] = scaled.astype(jnp.bfloat16)
        for t in range(2):
            tile = scaled[:, t * 128 : (t + 1) * 128]
            flipped[pl.ds(pl.multiple_of(n * 256 + t * 128, 128), 128), :] = tile.T.astype(jnp.bfloat16)
        return loss + jnp.sum(diff * diff)

    loss = jnp.float32(0.0)
    for half in (0, 1):
        for slot in (1, 2):
            ref = parts.at[slot, :, side(half)]
            remote(ref, ref, osend.at[0], orecv.at[slot * 2 + half], at(z, x, 1 - core)).wait_recv()

        @pl.when(core == kept)
        def _():
            for zq in (0, 1):

                @pl.when(is_own(zq))
                def _():
                    keep(zq, half).wait()

        @pl.when(core != kept)
        def _():
            ref = parts.at[0, :, side(half)]
            remote(ref, ref, osend.at[0], orecv.at[half], at(z, x, 1 - core)).wait_recv()

        loss = lax.fori_loop(half * 7, half * 7 + 7, compare, loss)
        for i in range(1, 8):
            flip(half, i).start()

        @pl.when(tp // 8 == half)
        def _():
            own_flip.start()

        @pl.when(tp // 8 != half)
        def _():
            flip(half, 0).start()

    norm_here.wait()
    for i in range(4):
        norm_wait(z + i, other)
    norm_half(core).start()

    back = [jnp.dot(delta[...], proj_ref[k], preferred_element_type=jnp.float32) for k in range(4)]
    dots = jnp.zeros((ROWS, 1), jnp.float32)
    for k in range(4):
        cols = slice(k * 256, (k + 1) * 256)
        dots += jnp.sum(back[k] * gain_ref[:, cols] * rows[:, cols], axis=-1, keepdims=True)
    shift = dots * (scale * scale * scale) * (1.0 / DS)
    for k in range(4):
        cols = slice(k * 256, (k + 1) * 256)
        grad_ref[:, cols] = (
            back[k] * gain_ref[:, cols] * scale - rows[:, cols] * shift
        ).astype(jnp.bfloat16)
        part = jnp.sum(back[k] * (rows[:, cols] * scale), axis=0, keepdims=True)
        stat[2 * k : 2 * k + 1, :] = part[:, :128]
        stat[2 * k + 1 : 2 * k + 2, :] = part[:, 128:]
    stat[8:16, :] = jnp.zeros((8, 128), jnp.float32) + loss

    def tell(i):
        return remote(stat, stat_in.at[tp], ssend.at[i - 1], srecv.at[tp], {"tp": mate(i)})

    for i in range(1, 16):
        tell(i).start()

    norm_half(1 - core).wait_recv()
    for i in range(1, 16):
        far = mate(i)
        got = flipped_in.at[:, pl.ds(pl.multiple_of(((far % 2) * 8 + far // 2) * ROWS, 128), ROWS)]
        remote(got, got, dsend.at[0], drecv.at[far], {"tp": far}).wait_recv()
    own_flip.wait()

    def hand(i):
        return remote(piece.at[group(i)], piece_in.at[dp], gsend.at[i - 1], grecv.at[dp], {"dp": group(i)})

    for k in range(4):
        out = jnp.dot(
            flipped_in[...], norm_ref[:, k * 256 : (k + 1) * 256], preferred_element_type=jnp.float32
        ).astype(jnp.bfloat16)
        piece[2 * k] = out[:, :128]
        piece[2 * k + 1] = out[:, 128:]
    for i in range(1, 8):
        hand(i).start()

    for i in range(1, 16):
        far = stat_in.at[mate(i)]
        remote(far, far, ssend.at[0], srecv.at[mate(i)], {"tp": mate(i)}).wait_recv()
    stat_in[tp] = stat[...]
    total[...] = jnp.sum(stat_in[...], axis=0)

    def tell_groups(i):
        return remote(total, total_in.at[dp], tsend.at[i - 1], trecv.at[dp], {"dp": group(i)})

    for i in range(1, 8):
        tell_groups(i).start()

    for i in range(1, 8):
        far = piece_in.at[group(i)]
        remote(far, far, gsend.at[0], grecv.at[group(i)], {"dp": group(i)}).wait_recv()
    piece_in[dp] = piece[dp]
    acc = jnp.zeros((PROJ, 128), jnp.float32)
    for k in range(8):
        acc += piece_in[k].astype(jnp.float32)
    summed[...] = acc.astype(jnp.bfloat16)

    def column(g):
        return out_ref.at[:, pl.ds(pl.multiple_of(g * 128, 128), 128)]

    def publish(i):
        return remote(summed, column(dp), asend.at[i - 1], arecv.at[dp], {"dp": group(i)})

    own_column = pltpu.make_async_copy(summed, column(dp), local.at[5])
    own_column.start()
    for i in range(1, 8):
        publish(i).start()

    for i in range(1, 8):
        far = total_in.at[group(i)]
        remote(far, far, tsend.at[0], trecv.at[group(i)], {"dp": group(i)}).wait_recv()
    total_in[dp] = total[...]
    whole = jnp.sum(total_in[...], axis=0)
    stat_ref[:8, :] = whole[:8, :]
    stat_ref[8:, :] = whole[8:, :] / terms

    for zq in (0, 1):
        swap(zq).wait_send()
        for half in (0, 1):

            @pl.when(is_far(zq))
            def _():
                for s in (0, 1):
                    pass_on(zq, s, half).wait_send()

            @pl.when(is_near(zq))
            def _():
                for s in (0, 1):
                    give(zq, s, half).wait_send()

            @pl.when(is_own(zq))
            def _():
                hand_over(zq, half).wait_send()

                @pl.when(core != kept)
                def _():
                    keep(zq, half).wait()

    for copy in norm_going + [norm_on(i) for i in (1, 2, 3)] + [norm_half(core)]:
        copy.wait_send()
    for half in (0, 1):
        for i in range(1, 8):
            flip(half, i).wait_send()

        @pl.when(tp // 8 != half)
        def _():
            flip(half, 0).wait_send()

    for i in range(1, 16):
        tell(i).wait_send()
    for i in range(1, 8):
        hand(i).wait_send()
        tell_groups(i).wait_send()
    for i in range(1, 8):
        far = column(group(i))
        remote(far, far, asend.at[0], arecv.at[group(i)], {"dp": group(i)}).wait_recv()
        publish(i).wait_send()
    own_column.wait()


def student(lengths, loss_scale, qkv, w_out, hidden, proj, rows, gain):
    vmem = pl.BlockSpec(memory_space=pltpu.VMEM)
    smem = pl.BlockSpec(memory_space=pltpu.SMEM)
    hbm = pl.BlockSpec(memory_space=pltpu.HBM)
    return pl.pallas_call(
        student_kernel,
        name="student",
        out_shape=(
            jax.ShapeDtypeStruct((ROWS, DS), jnp.bfloat16),
            jax.ShapeDtypeStruct((PROJ, DS), jnp.bfloat16),
            jax.ShapeDtypeStruct((16, 128), jnp.float32),
        ),
        in_specs=[smem, smem, vmem, hbm, hbm, hbm, vmem, vmem],
        out_specs=(vmem, vmem, vmem),
        scratch_shapes=[
            pltpu.VMEM((4, 256, HW), jnp.bfloat16),
            pltpu.VMEM((ROWS, HW), jnp.bfloat16),
            pltpu.VMEM((4, HW, 256), jnp.bfloat16),
            pltpu.VMEM((2 * LEN, DS), jnp.bfloat16),
            pltpu.VMEM((ROWS, DS), jnp.bfloat16),
            pltpu.VMEM((4, 2, 256, 256), jnp.bfloat16),
            pltpu.VMEM((2, 2, 256, 256), jnp.bfloat16),
            pltpu.VMEM((2, 256, HW), jnp.bfloat16),
            pltpu.VMEM((3, ROWS, HW), jnp.bfloat16),
            pltpu.VMEM((ROWS, HW), jnp.bfloat16),
            pltpu.VMEM((ROWS, HW), jnp.float32),
            pltpu.VMEM((ROWS, HW), jnp.bfloat16),
            pltpu.VMEM((HW, ROWS), jnp.bfloat16),
            pltpu.VMEM((PROJ, 2 * LEN), jnp.bfloat16),
            pltpu.VMEM((16, 128), jnp.float32),
            pltpu.VMEM((16, 16, 128), jnp.float32),
            pltpu.VMEM((16, 128), jnp.float32),
            pltpu.VMEM((8, 16, 128), jnp.float32),
            pltpu.VMEM((8, PROJ, 128), jnp.bfloat16),
            pltpu.VMEM((8, PROJ, 128), jnp.bfloat16),
            pltpu.VMEM((PROJ, 128), jnp.bfloat16),
        ]
        + [pltpu.SemaphoreType.DMA((n,)) for n in (2, 2, 8, 6, 2, 8, 9, 16, 16, 15, 16, 7, 8, 7, 8, 7, 8, 6)],
        compiler_params=pltpu.CompilerParams(
            collective_id=1, has_side_effects=True, vmem_limit_bytes=56 * MIB
        ),
    )(lengths, loss_scale, qkv, w_out, hidden, proj, rows, gain)


def finish_kernel(grad_in, proj_in, stat_in, grad_ref, proj_ref, gain_ref, loss_ref):
    grad_ref[...] = grad_in[...]
    proj_ref[...] = proj_in[...]
    gain_ref[...] = stat_in[:8, :]
    loss_ref[...] = stat_in[8:9, :1]


def finish(grad, proj, stat):
    return pl.pallas_call(
        finish_kernel,
        name="finish",
        out_shape=(
            jax.ShapeDtypeStruct(grad.shape, grad.dtype),
            jax.ShapeDtypeStruct(proj.shape, proj.dtype),
            jax.ShapeDtypeStruct((8, 128), jnp.float32),
            jax.ShapeDtypeStruct((1, 1), jnp.float32),
        ),
    )(grad, proj, stat)


def shards(
    hidden_in, norm_gain, w_qkv, w_out, lengths, student_in, student_gain, proj_weight, loss_scale
):
    qkv, w_out_all, proj_all = project(hidden_in, norm_gain.reshape(1, D), w_qkv, w_out, proj_weight)
    row_grad, proj_grad, stat = student(
        lengths,
        loss_scale,
        qkv,
        w_out_all,
        hidden_in,
        proj_all.reshape(4, HW, 256),
        student_in,
        student_gain.reshape(1, DS),
    )
    row_grad, proj_grad, gain, loss = finish(row_grad, proj_grad, stat)
    return row_grad, proj_grad, gain.reshape(DS), loss.reshape(())


def solution(mesh):
    placed = (
        P(("dp", "tp"), None),
        P(),
        P(None, None, "tp"),
        P("tp", None),
        P(),
        P(("dp", "tp"), None),
        P(),
        P("tp", None),
        P(),
    )
    return jax.shard_map(
        shards,
        mesh=mesh,
        in_specs=placed,
        out_specs=(P(("dp", "tp"), None), P("tp", None), P(), P()),
        check_vma=False,
    )
```

```python
import functools
import math

import jax
import jax.numpy as jnp
from jax import lax
from jax.experimental import pallas as pl
from jax.experimental.pallas import tpu as pltpu
from jax.sharding import PartitionSpec as P

HEAD = 128
HW = 3584
HALF = HW // 2
LEN = 1024
SEQS = 2
D = 7168
DS = 1024
PROJ = 224
ROWS = 128
FIRST = (80, 64)
MESH = pl.DeviceIdType.MESH
MIB = 1 << 20


def place():
    tp = lax.axis_index("tp")
    return tp // 4, (tp // 2) % 2, tp % 2


def at(z, x, core):
    return {"tp": (z % 4) * 4 + x * 2 + core}


def across(z, x, core):
    dp = lax.axis_index("dp")
    return {"tp": z * 4 + (1 - x) * 2 + core, "dp": (1 - dp // 4) * 4 + dp % 4}


def beside(z, x, core, i):
    dp = lax.axis_index("dp")
    return {"tp": z * 4 + x * 2 + core, "dp": dp // 4 * 4 + (dp + i) % 4}


def remote(src, dst, send, recv, device):
    return pltpu.make_async_remote_copy(
        src_ref=src, dst_ref=dst, send_sem=send, recv_sem=recv, device_id=device, device_id_type=MESH
    )


def rms_norm(rows, gain):
    return rows * lax.rsqrt(jnp.mean(rows * rows, axis=-1, keepdims=True) + 1e-06) * gain


def greet(devices, meanwhile):
    barrier = pltpu.get_barrier_semaphore()
    for device in devices:
        pl.semaphore_signal(barrier, 1, device_id=device, device_id_type=MESH)
    meanwhile()
    pl.semaphore_wait(barrier, len(devices))


def project_kernel(
    x_ref,
    gain_ref,
    w_hbm,
    wout_hbm,
    proj_hbm,
    qkv_ref,
    wout_all,
    proj_all,
    normed,
    rows,
    w,
    send,
    recv,
    wsend,
    wrecv,
    psend,
    precv,
    ysend,
    yrecv,
    local,
):
    z, x, core = place()
    other = 1 - x
    kept = z // 2
    rel = (z - 2 * core + 4) % 4
    ahead = (rel == 0) | (rel == 3)
    step = jnp.where(ahead, 1, -1)
    near = (z + step + 4) % 4
    onward = (z - step + 4) % 4
    far = (z + 2) % 4

    def norm(start, size):
        def one(i, carry):
            block = pl.ds(pl.multiple_of(start + i * 16, 16), 16)
            values = x_ref[block, :].astype(jnp.float32)
            centred = values - jnp.mean(values, axis=-1, keepdims=True)
            spread = jnp.mean(centred * centred, axis=-1, keepdims=True)
            normed[block, :] = (centred * lax.rsqrt(spread + 1e-05) * gain_ref[...]).astype(jnp.bfloat16)
            return carry

        lax.fori_loop(0, size // 16, one, 0)

    greet(
        [at(z, x, 1 - core)]
        + [at(zz, x, c) for zz in (z + 1, z + 3) for c in (0, 1)]
        + [at(z, other, c) for c in (0, 1)]
        + [across(z, x, c) for c in (0, 1)]
        + [at(far, x, core)]
        + [beside(z, x, core, i) for i in (1, 2, 3)],
        lambda: norm(min(FIRST), ROWS - min(FIRST)),
    )

    y = lax.axis_index("dp") % 4

    def held(chip_z, chip_x):
        return proj_all.at[y, (chip_z % 4) * 2 + chip_x, core]

    def held_sem(chip_z, chip_x):
        return precv.at[(chip_z % 4) * 2 + chip_x]

    quarter = proj_hbm.at[:, pl.ds(pl.multiple_of(y * 256, 256), 256)]
    quarter_here = pltpu.make_async_copy(quarter, held(z, x), local.at[6])
    quarter_going = [
        remote(quarter, held(z, x), psend.at[i], held_sem(z, x), device)
        for i, device in enumerate(
            (at(z + 1, x, core), at(z + 3, x, core), at(z + 2, x, core), across(z, x, core))
        )
    ]
    for copy in [quarter_here] + quarter_going:
        copy.start()

    def quarter_wait(chip_z, chip_x):
        ref = held(chip_z, chip_x)
        remote(ref, ref, psend.at[0], held_sem(chip_z, chip_x), across(z, x, core)).wait_recv()

    def quarter_on(i):
        ref = held(z + i, x)
        return remote(ref, ref, psend.at[3 + i], held_sem(z + i, x), across(z, x, core))

    def along(i):
        ref = proj_all.at[y, :, core]
        return remote(ref, ref, ysend.at[i - 1], yrecv.at[y], beside(z, x, core, i))

    def halves(c):
        ref = proj_all.at[:, :, c]
        return remote(ref, ref, ysend.at[3], yrecv.at[4], at(z, x, 1 - core))

    w_out_going = [
        remote(w_hbm.at[k], w.at[core, k], wsend.at[k], wrecv.at[k], at(z, x, 1 - core)) for k in range(3)
    ]
    w_own = [pltpu.make_async_copy(w_hbm.at[k], w.at[core, k], local.at[k]) for k in range(3)]
    slot = x * 2 + core
    proj_going = [
        remote(wout_hbm, wout_all.at[slot], wsend.at[3], wrecv.at[3 + core], at(z, x, 1 - core)),
        remote(wout_hbm, wout_all.at[slot], wsend.at[4], wrecv.at[5 + core], across(z, x, 0)),
        remote(wout_hbm, wout_all.at[slot], wsend.at[5], wrecv.at[5 + core], across(z, x, 1)),
    ]
    proj_own = pltpu.make_async_copy(wout_hbm, wout_all.at[slot], local.at[3])
    for copy in w_own + w_out_going + proj_going[:1] + [proj_own]:
        copy.start()

    def part(chunk_z, chunk_x, s, cls):
        chunk = (chunk_z % 2) * 2 + chunk_x
        start, size = ((0, FIRST[s]), (FIRST[s], ROWS - FIRST[s]))[cls]
        return rows.at[chunk, pl.ds(s * ROWS + start, size)]

    def sem(chunk_z, chunk_x, s, cls):
        return recv.at[((chunk_z % 2) * 2 + chunk_x) * 4 + s * 2 + cls]

    def arrived(chunk_z, chunk_x, s, cls):
        ref = part(chunk_z, chunk_x, s, cls)
        remote(ref, ref, send.at[0], sem(chunk_z, chunk_x, s, cls), at(z, x, 1 - core)).wait_recv()

    def forward(chunk_z, chunk_x, s, cls, index, device):
        ref = part(chunk_z, chunk_x, s, cls)
        return remote(ref, ref, send.at[index], sem(chunk_z, chunk_x, s, cls), device)

    def own_copies(cls, s):
        start, size = ((0, FIRST[s]), (FIRST[s], ROWS - FIRST[s]))[cls]
        src = normed.at[pl.ds(start, size)]
        dst = part(z, x, s, cls)
        got = sem(z, x, s, cls)
        base = cls * 4
        return (
            [
                remote(src, dst, send.at[base], got, at(z + 1, x, kept)),
                remote(src, dst, send.at[base + 1], got, at(z + 3, x, kept)),
                remote(src, dst, send.at[base + 2], got, at(z, other, kept)),
            ],
            remote(src, dst, send.at[base + 3], got, at(z, x, 1 - core)),
            pltpu.make_async_copy(src, dst, local.at[4 + cls]),
        )

    for cls in (1, 0):
        if cls == 0:
            norm(0, min(FIRST))
        for s in (0, 1):

            @pl.when(core == s)
            def _():
                away, sibling, here = own_copies(cls, s)
                for copy in away:
                    copy.start()

                @pl.when(core == kept)
                def _():
                    here.start()

                @pl.when(core != kept)
                def _():
                    sibling.start()

    def multiply(chunk_z, chunk_x, start=0, size=2 * ROWS):
        chunk = (chunk_z % 2) * 2 + chunk_x

        def one(n, carry):
            out = jnp.dot(
                rows[chunk, start : start + size], w[n % 2, n // 2], preferred_element_type=jnp.float32
            )
            qkv_ref[n, pl.ds(pl.multiple_of(chunk * 256 + start, 128), size), :] = out.astype(jnp.bfloat16)
            return carry

        lax.fori_loop(0, 6, one, 0)

    source = rel < 2

    for i in (1, 3, 2):
        quarter_wait(z + i, x)
        quarter_on(i).start()
    for copy in proj_going[1:]:
        copy.start()

    fx = []
    for s in (0, 1):
        arrived(near, x, s, 1)
        fx.append(forward(near, x, s, 1, 8 + s, at(z, other, core)))
        fx[-1].start()
    def pass_on(chunk_x, cls, index):
        return [
            (ahead == bool(s), forward(near, chunk_x, s, cls, index, at(onward, x, core))) for s in (0, 1)
        ]

    def begin(pairs):
        for mine, copy in pairs:

            @pl.when(mine)
            def _():
                copy.start()

    begin(pass_on(x, 1, 10))

    for copy in w_own:
        copy.wait()
    for k in range(3):
        remote(w_hbm.at[k], w.at[1 - core, k], wsend.at[k], wrecv.at[k], at(z, x, 1 - core)).wait_recv()

    @pl.when(source)
    def _():
        for cls in (0, 1):
            for s in (0, 1):

                @pl.when(core != s)
                def _():
                    arrived(z, x, s, cls)

                @pl.when(core == s)
                def _():
                    own_copies(cls, s)[2].wait()

        multiply(z, x)

    quarter_here.wait()
    for i in range(4):
        quarter_wait(z + i, other)
    for i in (1, 2, 3):
        along(i).start()

    for s in (0, 1):
        arrived(near, x, s, 0)
    begin(pass_on(x, 0, 11))

    def spread():
        return [
            forward(z, other, s, 0, 12 + s * 2 + i, at(zz, x, core))
            for s in (0, 1)
            for i, zz in enumerate((z + 1, z + 3))
        ]

    def crossing():
        return [forward(far, x, s, 1, 12 + s, at(z, other, core)) for s in (0, 1)]

    @pl.when(source)
    def _():
        for s in (0, 1):
            arrived(z, other, s, 0)
        for copy in spread():
            copy.start()
        for s in (0, 1):
            arrived(z, other, s, 1)
        multiply(z, other)

    @pl.when(jnp.logical_not(source))
    def _():
        for s in (0, 1):
            arrived(far, x, s, 1)
        for copy in crossing():
            copy.start()
        multiply(near, x)

    for s in (0, 1):
        arrived(near, other, s, 0)
    begin(pass_on(other, 0, 16))

    @pl.when(source)
    def _():
        multiply(near, x)

    for i in (1, 2, 3):
        ref = proj_all.at[(y + i) % 4, :, core]
        remote(ref, ref, ysend.at[0], yrecv.at[(y + i) % 4], at(z, x, 1 - core)).wait_recv()
    halves(core).start()

    for s in (0, 1):
        arrived(near, other, s, 1)
    multiply(near, other)

    @pl.when(jnp.logical_not(source))
    def _():
        for s in (0, 1):
            arrived(far, x, s, 0)
        multiply(far, x)
        for s in (0, 1):
            arrived(far, other, s, 0)
            arrived(far, other, s, 1)
            multiply(far, other, s * ROWS, ROWS)

    for cls in (0, 1):
        for s in (0, 1):

            @pl.when(core == s)
            def _():
                away, sibling, here = own_copies(cls, s)
                for copy in away:
                    copy.wait_send()

                @pl.when(core != kept)
                def _():
                    sibling.wait_send()

    for copy in fx:
        copy.wait_send()
    for mine, copy in pass_on(x, 1, 10) + pass_on(x, 0, 11) + pass_on(other, 0, 16):

        @pl.when(mine)
        def _():
            copy.wait_send()

    @pl.when(source)
    def _():
        for copy in spread():
            copy.wait_send()

    @pl.when(jnp.logical_not(source))
    def _():
        for copy in crossing():
            copy.wait_send()

    for copy in w_out_going + proj_going + quarter_going + [quarter_on(i) for i in (1, 2, 3)]:
        copy.wait_send()
    for copy in [along(i) for i in (1, 2, 3)] + [halves(core)]:
        copy.wait_send()
    halves(1 - core).wait_recv()
    proj_own.wait()
    remote(
        wout_hbm, wout_all.at[x * 2 + 1 - core], wsend.at[3], wrecv.at[3 + 1 - core], at(z, x, 1 - core)
    ).wait_recv()
    for c in (0, 1):
        remote(wout_hbm, wout_all.at[other * 2 + c], wsend.at[4], wrecv.at[5 + c], across(z, x, c)).wait_recv()


def project(hidden, gain, w_qkv, w_out, proj):
    vmem = pl.BlockSpec(memory_space=pltpu.VMEM)
    hbm = pl.BlockSpec(memory_space=pltpu.HBM)
    return pl.pallas_call(
        project_kernel,
        name="project",
        out_shape=(
            jax.ShapeDtypeStruct((6, LEN, 256), jnp.bfloat16),
            jax.ShapeDtypeStruct((4, 256, HW), jnp.bfloat16),
            jax.ShapeDtypeStruct((4, 8, 2, PROJ, 256), jnp.bfloat16),
        ),
        in_specs=[vmem, vmem, hbm, hbm, hbm],
        out_specs=(vmem, hbm, hbm),
        scratch_shapes=[
            pltpu.VMEM((ROWS, D), jnp.bfloat16),
            pltpu.VMEM((4, 2 * ROWS, D), jnp.bfloat16),
            pltpu.VMEM((2, 3, D, 256), jnp.bfloat16),
        ]
        + [pltpu.SemaphoreType.DMA((n,)) for n in (17, 16, 6, 7, 7, 8, 4, 5, 7)],
        compiler_params=pltpu.CompilerParams(
            collective_id=0, has_side_effects=True, vmem_limit_bytes=60 * MIB
        ),
    )(hidden, gain, w_qkv, w_out, proj)


def student_kernel(
    len_ref,
    scale_ref,
    qkv_ref,
    wout_hbm,
    hid_hbm,
    proj_hbm,
    student_ref,
    gain_ref,
    grad_ref,
    out_ref,
    stat_ref,
    wout_ref,
    hid_ref,
    proj_ref,
    norm_ref,
    normed,
    ctx,
    ctx_in,
    stage,
    parts,
    relay,
    mapped,
    delta,
    flipped,
    flipped_in,
    stat,
    stat_in,
    total,
    total_in,
    piece,
    piece_in,
    summed,
    send,
    recv,
    osend,
    orecv,
    rrecv,
    nsend,
    nrecv,
    dsend,
    drecv,
    ssend,
    srecv,
    tsend,
    trecv,
    gsend,
    grecv,
    asend,
    arecv,
    local,
):
    z, x, core = place()
    other = 1 - x
    kept = z // 2
    tp = lax.axis_index("tp")
    dp = lax.axis_index("dp")
    rel = (z - 2 * core + 4) % 4
    ahead = (rel == 0) | (rel == 3)
    step = jnp.where(ahead, 1, -1)
    via = jnp.where(ahead, 0, 1)
    source = rel < 2
    key_len = len_ref[dp * SEQS + core]
    count = len_ref[0]
    for i in range(1, len_ref.shape[0]):
        count += len_ref[i]
    terms = jnp.full((1, 128), 1.0, jnp.float32) * count.astype(jnp.float32) * HW
    factor = (2.0 * scale_ref[0] / terms)[:, :1]

    fetch_wout = pltpu.make_async_copy(wout_hbm, wout_ref, local.at[0])
    fetch_hid = pltpu.make_async_copy(hid_hbm.at[:, pl.ds(0, HW)], hid_ref, local.at[1])
    fetch_proj = pltpu.make_async_copy(proj_hbm, proj_ref, local.at[2])
    for copy in (fetch_wout, fetch_hid, fetch_proj):
        copy.start()

    def mate(i):
        return (tp + i) % 16

    def group(i):
        return (dp + i) % 8

    rows = student_ref[...].astype(jnp.float32)
    scale = lax.rsqrt(jnp.mean(rows * rows, axis=-1, keepdims=True) + 1e-06)
    normed[...] = (rows * scale * gain_ref[...]).astype(jnp.bfloat16)

    def attend(chunk, keys, zq, mine):
        start = pl.multiple_of(chunk * 256, 256)
        row = lax.broadcasted_iota(jnp.int32, (256, keys), 0) + start
        col = lax.broadcasted_iota(jnp.int32, (256, keys), 1)
        allowed = (col <= row) & (col < key_len)

        def pair(half, carry):
            for h in (0, 1):
                lanes = slice(h * HEAD, (h + 1) * HEAD)
                q = qkv_ref[half, pl.ds(start, 256), lanes]
                k = qkv_ref[2 + half, :keys, lanes]
                v = qkv_ref[4 + half, :keys, lanes]
                scores = lax.dot_general(
                    q, k, (((1,), (1,)), ((), ())), preferred_element_type=jnp.float32
                ) * (1.0 / math.sqrt(HEAD))
                scores = jnp.where(allowed, scores, -1e30)
                weights = jnp.exp(scores - jnp.max(scores, axis=-1, keepdims=True))
                norm = jnp.sum(weights, axis=-1, keepdims=True)
                out = jnp.dot(weights.astype(jnp.bfloat16), v, preferred_element_type=jnp.float32)
                ctx[zq * 2 + mine, half, :, lanes] = (out / norm).astype(jnp.bfloat16)
            return carry

        lax.fori_loop(0, 2, pair, 0)

    def swap(zq):
        return remote(ctx.at[zq * 2], ctx_in.at[zq], send.at[zq], recv.at[zq], at(z, other, core))

    greet(
        [{"tp": mate(i)} for i in range(1, 16)] + [{"dp": group(i)} for i in range(1, 8)],
        lambda: attend(other, 512, 0, 0),
    )
    swap(0).start()

    def block(chip_z, chip_x, c):
        chip = (chip_z % 4) * 2 + chip_x
        return norm_ref.at[pl.ds(pl.multiple_of((c * 8 + chip) * ROWS, 128), ROWS)]

    def block_sem(chip_z, chip_x):
        return nrecv.at[(chip_z % 4) * 2 + chip_x]

    norm_here = pltpu.make_async_copy(normed, block(z, x, core), local.at[3])
    norm_going = [
        remote(normed, block(z, x, core), nsend.at[i], block_sem(z, x), at(zz, xx, core))
        for i, (zz, xx) in enumerate(((z + 1, x), (z + 3, x), (z + 2, x), (z, other)))
    ]

    def norm_wait(chip_z, chip_x):
        ref = block(chip_z, chip_x, core)
        remote(ref, ref, nsend.at[0], block_sem(chip_z, chip_x), at(z, other, core)).wait_recv()

    def norm_on(i):
        ref = block(z + i, x, core)
        return remote(ref, ref, nsend.at[3 + i], block_sem(z + i, x), at(z, other, core))

    def norm_half(c):
        ref = norm_ref.at[pl.ds(pl.multiple_of(c * LEN, 128), LEN)]
        return remote(ref, ref, nsend.at[7], nrecv.at[8], at(z, x, 1 - core))

    def side(half):
        return pl.ds(half * HALF, HALF)

    def summand(zq, s, half):
        return stage.at[zq, pl.ds(pl.multiple_of(s * ROWS, 16), ROWS), side(half)]

    def give(zq, s, half):
        slot = jnp.where(ahead, 2, 1)
        return remote(
            summand(zq, s, half),
            parts.at[slot, :, side(half)],
            osend.at[zq * 4 + s * 2 + half],
            orecv.at[slot * 2 + half],
            at(z + step + 4, x, s),
        )

    def pass_on(zq, s, half):
        return remote(
            summand(zq, s, half),
            relay.at[:, side(half)],
            osend.at[zq * 4 + s * 2 + half],
            rrecv.at[half],
            at(z + (1 if s == 0 else 3), x, core),
        )

    def hand_over(zq, half):
        return remote(
            summand(zq, 1 - core, half),
            parts.at[0, :, side(half)],
            osend.at[zq * 4 + (1 - core) * 2 + half],
            orecv.at[half],
            at(z, x, 1 - core),
        )

    def keep(zq, half):
        return pltpu.make_async_copy(
            summand(zq, core, half), parts.at[0, :, side(half)], osend.at[zq * 4 + core * 2 + half]
        )

    def is_near(zq):
        return (rel == 1 - zq) | (rel == 3 - zq)

    def is_far(zq):
        return rel == 2 + zq

    def is_own(zq):
        return rel == zq

    def project_out(zq, half):
        def one(n, carry):
            lanes = pl.ds(pl.multiple_of(half * HALF + n * 896, 128), 896)
            out = jnp.zeros((256, 896), jnp.float32)
            for k in (0, 1):
                out += jnp.dot(
                    ctx[zq * 2 + 1, k], wout_ref[x * 2 + k, :, lanes], preferred_element_type=jnp.float32
                )
                out += jnp.dot(
                    ctx_in[zq, k], wout_ref[other * 2 + k, :, lanes], preferred_element_type=jnp.float32
                )
            stage[zq, :, lanes] = out.astype(jnp.bfloat16)
            return carry

        lax.fori_loop(0, HALF // 896, one, 0)

        @pl.when(is_far(zq))
        def _():
            for s in (0, 1):
                pass_on(zq, s, half).start()

        @pl.when(is_near(zq))
        def _():
            give(zq, 1 - via, half).start()

        @pl.when(is_own(zq))
        def _():
            keep(zq, half).start()
            hand_over(zq, half).start()

    def join(zq, half):
        @pl.when(is_near(zq))
        def _():
            src = relay.at[:, side(half)]
            remote(src, src, osend.at[0], rrecv.at[half], at(z, x, 1 - core)).wait_recv()

            def one(i, carry):
                here = pl.ds(pl.multiple_of(via * ROWS + i * 16, 16), 16)
                there = pl.ds(pl.multiple_of(i * 16, 16), 16)
                both = stage[zq, here, side(half)].astype(jnp.float32) + relay[there, side(half)].astype(
                    jnp.float32
                )
                stage[zq, here, side(half)] = both.astype(jnp.bfloat16)
                return carry

            lax.fori_loop(0, ROWS // 16, one, 0)
            give(zq, via, half).start()

    for copy in [norm_here] + norm_going[:3]:
        copy.start()
    attend(2 + other, 1024, 1, 0)
    swap(1).start()
    attend(x, 512, 0, 1)
    fetch_wout.wait()
    swap(0).wait_recv()
    for half in (0, 1):
        project_out(0, half)
    attend(2 + x, 1024, 1, 1)
    swap(1).wait_recv()
    for half in (0, 1):
        project_out(1, half)
    norm_going[3].start()
    for i in (1, 3, 2):
        norm_wait(z + i, x)
        norm_on(i).start()
    join(0, 0)

    fetch_proj.wait()

    def map_rows(n, carry):
        base = pl.multiple_of(n * 512, 512)
        out = jnp.zeros((ROWS, 512), jnp.float32)
        for k in range(4):
            out += lax.dot_general(
                normed[:, k * 256 : (k + 1) * 256],
                proj_ref[k, pl.ds(base, 512), :],
                (((1,), (1,)), ((), ())),
                preferred_element_type=jnp.float32,
            )
        mapped[:, pl.ds(base, 512)] = out
        return carry

    lax.fori_loop(0, HW // 512, map_rows, 0)
    join(0, 1)
    for half in (0, 1):
        join(1, half)
    fetch_hid.wait()
    position = (tp % 8) * ROWS + lax.broadcasted_iota(jnp.int32, (ROWS, 1), 0)
    valid = position < len_ref[dp * SEQS + kept]
    lane = pl.ds(pl.multiple_of((core * 8 + z * 2 + x) * ROWS, 128), ROWS)

    def owner(half, i):
        return half * 8 + (tp + i) % 8

    def flip(half, i):
        src = flipped.at[pl.ds(pl.multiple_of(owner(half, i) * PROJ, 16), PROJ)]
        return remote(
            src, flipped_in.at[:, lane], dsend.at[half * 8 + i], drecv.at[tp], {"tp": owner(half, i)}
        )

    own_flip = pltpu.make_async_copy(
        flipped.at[pl.ds(pl.multiple_of(tp * PROJ, 16), PROJ)], flipped_in.at[:, lane], local.at[4]
    )

    def compare(n, loss):
        block_cols = pl.ds(pl.multiple_of(n * 256, 256), 256)
        mixed = parts[0, :, block_cols].astype(jnp.float32)
        for slot in (1, 2):
            mixed += parts[slot, :, block_cols].astype(jnp.float32)
        target = (hid_ref[:, block_cols].astype(jnp.float32) + mixed).astype(jnp.bfloat16)
        diff = jnp.where(valid, mapped[:, block_cols] - target.astype(jnp.float32), 0.0)
        scaled = diff * factor
        delta[:, block_cols] = scaled.astype(jnp.bfloat16)
        for t in range(2):
            tile = scaled[:, t * 128 : (t + 1) * 128]
            flipped[pl.ds(pl.multiple_of(n * 256 + t * 128, 128), 128), :] = tile.T.astype(jnp.bfloat16)
        return loss + jnp.sum(diff * diff)

    loss = jnp.float32(0.0)
    for half in (0, 1):
        for slot in (1, 2):
            ref = parts.at[slot, :, side(half)]
            remote(ref, ref, osend.at[0], orecv.at[slot * 2 + half], at(z, x, 1 - core)).wait_recv()

        @pl.when(core == kept)
        def _():
            for zq in (0, 1):

                @pl.when(is_own(zq))
                def _():
                    keep(zq, half).wait()

        @pl.when(core != kept)
        def _():
            ref = parts.at[0, :, side(half)]
            remote(ref, ref, osend.at[0], orecv.at[half], at(z, x, 1 - core)).wait_recv()

        loss = lax.fori_loop(half * 7, half * 7 + 7, compare, loss)
        for i in range(1, 8):
            flip(half, i).start()

        @pl.when(tp // 8 == half)
        def _():
            own_flip.start()

        @pl.when(tp // 8 != half)
        def _():
            flip(half, 0).start()

    norm_here.wait()
    for i in range(4):
        norm_wait(z + i, other)
    norm_half(core).start()

    back = [jnp.dot(delta[...], proj_ref[k], preferred_element_type=jnp.float32) for k in range(4)]
    dots = jnp.zeros((ROWS, 1), jnp.float32)
    for k in range(4):
        cols = slice(k * 256, (k + 1) * 256)
        dots += jnp.sum(back[k] * gain_ref[:, cols] * rows[:, cols], axis=-1, keepdims=True)
    shift = dots * (scale * scale * scale) * (1.0 / DS)
    for k in range(4):
        cols = slice(k * 256, (k + 1) * 256)
        grad_ref[:, cols] = (
            back[k] * gain_ref[:, cols] * scale - rows[:, cols] * shift
        ).astype(jnp.bfloat16)
        part = jnp.sum(back[k] * (rows[:, cols] * scale), axis=0, keepdims=True)
        stat[2 * k : 2 * k + 1, :] = part[:, :128]
        stat[2 * k + 1 : 2 * k + 2, :] = part[:, 128:]
    stat[8:16, :] = jnp.zeros((8, 128), jnp.float32) + loss

    def tell(i):
        return remote(stat, stat_in.at[tp], ssend.at[i - 1], srecv.at[tp], {"tp": mate(i)})

    for i in range(1, 16):
        tell(i).start()

    norm_half(1 - core).wait_recv()
    for i in range(1, 16):
        far = mate(i)
        got = flipped_in.at[:, pl.ds(pl.multiple_of(((far % 2) * 8 + far // 2) * ROWS, 128), ROWS)]
        remote(got, got, dsend.at[0], drecv.at[far], {"tp": far}).wait_recv()
    own_flip.wait()

    def hand(g):
        return remote(piece.at[g], piece_in.at[dp], gsend.at[g], grecv.at[dp], {"dp": g})

    for k in range(4):
        out = jnp.dot(
            flipped_in[...], norm_ref[:, k * 256 : (k + 1) * 256], preferred_element_type=jnp.float32
        ).astype(jnp.bfloat16)
        for g in (2 * k, 2 * k + 1):
            piece[g] = out[:, (g % 2) * 128 : (g % 2 + 1) * 128]

            @pl.when(dp != g)
            def _():
                hand(g).start()

    for i in range(1, 16):
        far = stat_in.at[mate(i)]
        remote(far, far, ssend.at[0], srecv.at[mate(i)], {"tp": mate(i)}).wait_recv()
    stat_in[tp] = stat[...]
    total[...] = jnp.sum(stat_in[...], axis=0)

    def tell_groups(i):
        return remote(total, total_in.at[dp], tsend.at[i - 1], trecv.at[dp], {"dp": group(i)})

    for i in range(1, 8):
        tell_groups(i).start()

    for i in range(1, 8):
        far = piece_in.at[group(i)]
        remote(far, far, gsend.at[0], grecv.at[group(i)], {"dp": group(i)}).wait_recv()
    piece_in[dp] = piece[dp]
    acc = jnp.zeros((PROJ, 128), jnp.float32)
    for k in range(8):
        acc += piece_in[k].astype(jnp.float32)
    summed[...] = acc.astype(jnp.bfloat16)

    def column(g):
        return out_ref.at[:, pl.ds(pl.multiple_of(g * 128, 128), 128)]

    def publish(i):
        return remote(summed, column(dp), asend.at[i - 1], arecv.at[dp], {"dp": group(i)})

    own_column = pltpu.make_async_copy(summed, column(dp), local.at[5])
    own_column.start()
    for i in range(1, 8):
        publish(i).start()

    for i in range(1, 8):
        far = total_in.at[group(i)]
        remote(far, far, tsend.at[0], trecv.at[group(i)], {"dp": group(i)}).wait_recv()
    total_in[dp] = total[...]
    whole = jnp.sum(total_in[...], axis=0)
    stat_ref[:8, :] = whole[:8, :]
    stat_ref[8:, :] = whole[8:, :] / terms

    for zq in (0, 1):
        swap(zq).wait_send()
        for half in (0, 1):

            @pl.when(is_far(zq))
            def _():
                for s in (0, 1):
                    pass_on(zq, s, half).wait_send()

            @pl.when(is_near(zq))
            def _():
                for s in (0, 1):
                    give(zq, s, half).wait_send()

            @pl.when(is_own(zq))
            def _():
                hand_over(zq, half).wait_send()

                @pl.when(core != kept)
                def _():
                    keep(zq, half).wait()

    for copy in norm_going + [norm_on(i) for i in (1, 2, 3)] + [norm_half(core)]:
        copy.wait_send()
    for half in (0, 1):
        for i in range(1, 8):
            flip(half, i).wait_send()

        @pl.when(tp // 8 != half)
        def _():
            flip(half, 0).wait_send()

    for i in range(1, 16):
        tell(i).wait_send()
    for g in range(8):

        @pl.when(dp != g)
        def _():
            hand(g).wait_send()

    for i in range(1, 8):
        tell_groups(i).wait_send()
    for i in range(1, 8):
        far = column(group(i))
        remote(far, far, asend.at[0], arecv.at[group(i)], {"dp": group(i)}).wait_recv()
        publish(i).wait_send()
    own_column.wait()


def student(lengths, loss_scale, qkv, w_out, hidden, proj, rows, gain):
    vmem = pl.BlockSpec(memory_space=pltpu.VMEM)
    smem = pl.BlockSpec(memory_space=pltpu.SMEM)
    hbm = pl.BlockSpec(memory_space=pltpu.HBM)
    return pl.pallas_call(
        student_kernel,
        name="student",
        out_shape=(
            jax.ShapeDtypeStruct((ROWS, DS), jnp.bfloat16),
            jax.ShapeDtypeStruct((PROJ, DS), jnp.bfloat16),
            jax.ShapeDtypeStruct((16, 128), jnp.float32),
        ),
        in_specs=[smem, smem, vmem, hbm, hbm, hbm, vmem, vmem],
        out_specs=(vmem, vmem, vmem),
        scratch_shapes=[
            pltpu.VMEM((4, 256, HW), jnp.bfloat16),
            pltpu.VMEM((ROWS, HW), jnp.bfloat16),
            pltpu.VMEM((4, HW, 256), jnp.bfloat16),
            pltpu.VMEM((2 * LEN, DS), jnp.bfloat16),
            pltpu.VMEM((ROWS, DS), jnp.bfloat16),
            pltpu.VMEM((4, 2, 256, 256), jnp.bfloat16),
            pltpu.VMEM((2, 2, 256, 256), jnp.bfloat16),
            pltpu.VMEM((2, 256, HW), jnp.bfloat16),
            pltpu.VMEM((3, ROWS, HW), jnp.bfloat16),
            pltpu.VMEM((ROWS, HW), jnp.bfloat16),
            pltpu.VMEM((ROWS, HW), jnp.float32),
            pltpu.VMEM((ROWS, HW), jnp.bfloat16),
            pltpu.VMEM((HW, ROWS), jnp.bfloat16),
            pltpu.VMEM((PROJ, 2 * LEN), jnp.bfloat16),
            pltpu.VMEM((16, 128), jnp.float32),
            pltpu.VMEM((16, 16, 128), jnp.float32),
            pltpu.VMEM((16, 128), jnp.float32),
            pltpu.VMEM((8, 16, 128), jnp.float32),
            pltpu.VMEM((8, PROJ, 128), jnp.bfloat16),
            pltpu.VMEM((8, PROJ, 128), jnp.bfloat16),
            pltpu.VMEM((PROJ, 128), jnp.bfloat16),
        ]
        + [pltpu.SemaphoreType.DMA((n,)) for n in (2, 2, 8, 6, 2, 8, 9, 16, 16, 15, 16, 7, 8, 8, 8, 7, 8, 6)],
        compiler_params=pltpu.CompilerParams(
            collective_id=1, has_side_effects=True, vmem_limit_bytes=56 * MIB
        ),
    )(lengths, loss_scale, qkv, w_out, hidden, proj, rows, gain)


def finish_kernel(grad_in, proj_in, stat_in, grad_ref, proj_ref, gain_ref, loss_ref):
    grad_ref[...] = grad_in[...]
    proj_ref[...] = proj_in[...]
    gain_ref[...] = stat_in[:8, :]
    loss_ref[...] = stat_in[8:9, :1]


def finish(grad, proj, stat):
    return pl.pallas_call(
        finish_kernel,
        name="finish",
        out_shape=(
            jax.ShapeDtypeStruct(grad.shape, grad.dtype),
            jax.ShapeDtypeStruct(proj.shape, proj.dtype),
            jax.ShapeDtypeStruct((8, 128), jnp.float32),
            jax.ShapeDtypeStruct((1, 1), jnp.float32),
        ),
    )(grad, proj, stat)


def shards(
    hidden_in, norm_gain, w_qkv, w_out, lengths, student_in, student_gain, proj_weight, loss_scale
):
    qkv, w_out_all, proj_all = project(hidden_in, norm_gain.reshape(1, D), w_qkv, w_out, proj_weight)
    row_grad, proj_grad, stat = student(
        lengths,
        loss_scale,
        qkv,
        w_out_all,
        hidden_in,
        proj_all.reshape(4, HW, 256),
        student_in,
        student_gain.reshape(1, DS),
    )
    row_grad, proj_grad, gain, loss = finish(row_grad, proj_grad, stat)
    return row_grad, proj_grad, gain.reshape(DS), loss.reshape(())


def solution(mesh):
    placed = (
        P(("dp", "tp"), None),
        P(),
        P(None, None, "tp"),
        P("tp", None),
        P(),
        P(("dp", "tp"), None),
        P(),
        P("tp", None),
        P(),
    )
    return jax.shard_map(
        shards,
        mesh=mesh,
        in_specs=placed,
        out_specs=(P(("dp", "tp"), None), P("tp", None), P(), P()),
        check_vma=False,
    )
```

```python
import functools
import math

import jax
import jax.numpy as jnp
from jax import lax
from jax.experimental import pallas as pl
from jax.experimental.pallas import tpu as pltpu
from jax.sharding import PartitionSpec as P

HEAD = 128
HW = 3584
PARTS = 4
WIDE = HW // PARTS
TURN = (2, 1, 3, 0)
EACH = 16 // PARTS
LEN = 1024
SEQS = 2
D = 7168
DS = 1024
PROJ = 224
ROWS = 128
FIRST = (80, 64)
MESH = pl.DeviceIdType.MESH
MIB = 1 << 20


def place():
    tp = lax.axis_index("tp")
    return tp // 4, (tp // 2) % 2, tp % 2


def at(z, x, core):
    return {"tp": (z % 4) * 4 + x * 2 + core}


def across(z, x, core):
    dp = lax.axis_index("dp")
    return {"tp": z * 4 + (1 - x) * 2 + core, "dp": (1 - dp // 4) * 4 + dp % 4}


def beside(z, x, core, i):
    dp = lax.axis_index("dp")
    return {"tp": z * 4 + x * 2 + core, "dp": dp // 4 * 4 + (dp + i) % 4}


def remote(src, dst, send, recv, device):
    return pltpu.make_async_remote_copy(
        src_ref=src, dst_ref=dst, send_sem=send, recv_sem=recv, device_id=device, device_id_type=MESH
    )


def rms_norm(rows, gain):
    return rows * lax.rsqrt(jnp.mean(rows * rows, axis=-1, keepdims=True) + 1e-06) * gain


def greet(devices, meanwhile):
    barrier = pltpu.get_barrier_semaphore()
    for device in devices:
        pl.semaphore_signal(barrier, 1, device_id=device, device_id_type=MESH)
    meanwhile()
    pl.semaphore_wait(barrier, len(devices))


def project_kernel(
    x_ref,
    gain_ref,
    w_hbm,
    wout_hbm,
    proj_hbm,
    qkv_ref,
    wout_all,
    proj_all,
    normed,
    rows,
    w,
    send,
    recv,
    wsend,
    wrecv,
    psend,
    precv,
    ysend,
    yrecv,
    local,
):
    z, x, core = place()
    other = 1 - x
    kept = z // 2
    rel = (z - 2 * core + 4) % 4
    ahead = (rel == 0) | (rel == 3)
    step = jnp.where(ahead, 1, -1)
    near = (z + step + 4) % 4
    onward = (z - step + 4) % 4
    far = (z + 2) % 4

    def norm(start, size):
        def one(i, carry):
            block = pl.ds(pl.multiple_of(start + i * 16, 16), 16)
            values = x_ref[block, :].astype(jnp.float32)
            centred = values - jnp.mean(values, axis=-1, keepdims=True)
            spread = jnp.mean(centred * centred, axis=-1, keepdims=True)
            normed[block, :] = (centred * lax.rsqrt(spread + 1e-05) * gain_ref[...]).astype(jnp.bfloat16)
            return carry

        lax.fori_loop(0, size // 16, one, 0)

    greet(
        [at(z, x, 1 - core)]
        + [at(zz, x, c) for zz in (z + 1, z + 3) for c in (0, 1)]
        + [at(z, other, c) for c in (0, 1)]
        + [across(z, x, c) for c in (0, 1)]
        + [at(far, x, core)]
        + [beside(z, x, core, i) for i in (1, 2, 3)],
        lambda: norm(min(FIRST), ROWS - min(FIRST)),
    )

    y = lax.axis_index("dp") % 4

    def held(chip_z, chip_x):
        return proj_all.at[y, (chip_z % 4) * 2 + chip_x, core]

    def held_sem(chip_z, chip_x):
        return precv.at[(chip_z % 4) * 2 + chip_x]

    quarter = proj_hbm.at[:, pl.ds(pl.multiple_of(y * 256, 256), 256)]
    quarter_here = pltpu.make_async_copy(quarter, held(z, x), local.at[6])
    quarter_going = [
        remote(quarter, held(z, x), psend.at[i], held_sem(z, x), device)
        for i, device in enumerate(
            (at(z + 1, x, core), at(z + 3, x, core), at(z + 2, x, core), across(z, x, core))
        )
    ]
    for copy in [quarter_here] + quarter_going:
        copy.start()

    def quarter_wait(chip_z, chip_x):
        ref = held(chip_z, chip_x)
        remote(ref, ref, psend.at[0], held_sem(chip_z, chip_x), across(z, x, core)).wait_recv()

    def quarter_on(i):
        ref = held(z + i, x)
        return remote(ref, ref, psend.at[3 + i], held_sem(z + i, x), across(z, x, core))

    def along(i):
        ref = proj_all.at[y, :, core]
        return remote(ref, ref, ysend.at[i - 1], yrecv.at[y], beside(z, x, core, i))

    def halves(c):
        ref = proj_all.at[:, :, c]
        return remote(ref, ref, ysend.at[3], yrecv.at[4], at(z, x, 1 - core))

    w_out_going = [
        remote(w_hbm.at[k], w.at[core, k], wsend.at[k], wrecv.at[k], at(z, x, 1 - core)) for k in range(3)
    ]
    w_own = [pltpu.make_async_copy(w_hbm.at[k], w.at[core, k], local.at[k]) for k in range(3)]
    slot = x * 2 + core
    proj_going = [
        remote(wout_hbm, wout_all.at[slot], wsend.at[3], wrecv.at[3 + core], at(z, x, 1 - core)),
        remote(wout_hbm, wout_all.at[slot], wsend.at[4], wrecv.at[5 + core], across(z, x, 0)),
        remote(wout_hbm, wout_all.at[slot], wsend.at[5], wrecv.at[5 + core], across(z, x, 1)),
    ]
    proj_own = pltpu.make_async_copy(wout_hbm, wout_all.at[slot], local.at[3])
    for copy in w_own + w_out_going + proj_going[:1] + [proj_own]:
        copy.start()

    def part(chunk_z, chunk_x, s, cls):
        chunk = (chunk_z % 2) * 2 + chunk_x
        start, size = ((0, FIRST[s]), (FIRST[s], ROWS - FIRST[s]))[cls]
        return rows.at[chunk, pl.ds(s * ROWS + start, size)]

    def sem(chunk_z, chunk_x, s, cls):
        return recv.at[((chunk_z % 2) * 2 + chunk_x) * 4 + s * 2 + cls]

    def arrived(chunk_z, chunk_x, s, cls):
        ref = part(chunk_z, chunk_x, s, cls)
        remote(ref, ref, send.at[0], sem(chunk_z, chunk_x, s, cls), at(z, x, 1 - core)).wait_recv()

    def forward(chunk_z, chunk_x, s, cls, index, device):
        ref = part(chunk_z, chunk_x, s, cls)
        return remote(ref, ref, send.at[index], sem(chunk_z, chunk_x, s, cls), device)

    def own_copies(cls, s):
        start, size = ((0, FIRST[s]), (FIRST[s], ROWS - FIRST[s]))[cls]
        src = normed.at[pl.ds(start, size)]
        dst = part(z, x, s, cls)
        got = sem(z, x, s, cls)
        base = cls * 4
        return (
            [
                remote(src, dst, send.at[base], got, at(z + 1, x, kept)),
                remote(src, dst, send.at[base + 1], got, at(z + 3, x, kept)),
                remote(src, dst, send.at[base + 2], got, at(z, other, kept)),
            ],
            remote(src, dst, send.at[base + 3], got, at(z, x, 1 - core)),
            pltpu.make_async_copy(src, dst, local.at[4 + cls]),
        )

    def send_own(cls, over_x, rest):
        for s in (0, 1):

            @pl.when(core == s)
            def _():
                away, sibling, here = own_copies(cls, s)
                if over_x:
                    away[2].start()
                if rest:
                    for copy in away[:2]:
                        copy.start()

                    @pl.when(core == kept)
                    def _():
                        here.start()

                    @pl.when(core != kept)
                    def _():
                        sibling.start()

    send_own(1, False, True)
    norm(0, min(FIRST))
    send_own(0, True, True)
    send_own(1, True, False)

    def multiply(chunk_z, chunk_x, start=0, size=2 * ROWS):
        chunk = (chunk_z % 2) * 2 + chunk_x

        def one(n, carry):
            out = jnp.dot(
                rows[chunk, start : start + size], w[n % 2, n // 2], preferred_element_type=jnp.float32
            )
            qkv_ref[n, pl.ds(pl.multiple_of(chunk * 256 + start, 128), size), :] = out.astype(jnp.bfloat16)
            return carry

        lax.fori_loop(0, 6, one, 0)

    source = rel < 2

    for i in (1, 3, 2):
        quarter_wait(z + i, x)
        quarter_on(i).start()
    for copy in proj_going[1:]:
        copy.start()

    fx = []
    for s in (0, 1):
        arrived(near, x, s, 1)
        fx.append(forward(near, x, s, 1, 8 + s, at(z, other, core)))
        fx[-1].start()
    def pass_on(chunk_x, cls, index):
        return [
            (ahead == bool(s), forward(near, chunk_x, s, cls, index, at(onward, x, core))) for s in (0, 1)
        ]

    def begin(pairs):
        for mine, copy in pairs:

            @pl.when(mine)
            def _():
                copy.start()

    begin(pass_on(x, 1, 10))

    for copy in w_own:
        copy.wait()
    for k in range(3):
        remote(w_hbm.at[k], w.at[1 - core, k], wsend.at[k], wrecv.at[k], at(z, x, 1 - core)).wait_recv()

    @pl.when(source)
    def _():
        for cls in (0, 1):
            for s in (0, 1):

                @pl.when(core != s)
                def _():
                    arrived(z, x, s, cls)

                @pl.when(core == s)
                def _():
                    own_copies(cls, s)[2].wait()

        multiply(z, x)

    quarter_here.wait()
    for i in range(4):
        quarter_wait(z + i, other)
    for i in (1, 2, 3):
        along(i).start()

    for s in (0, 1):
        arrived(near, x, s, 0)
    begin(pass_on(x, 0, 11))

    def spread():
        return [
            forward(z, other, s, 0, 12 + s * 2 + i, at(zz, x, core))
            for s, i, zz in ((0, 0, z + 1), (1, 1, z + 3), (1, 0, z + 1), (0, 1, z + 3))
        ]

    def crossing():
        return [forward(far, x, s, 1, 12 + s, at(z, other, core)) for s in (0, 1)]

    @pl.when(source)
    def _():
        for s in (0, 1):
            arrived(z, other, s, 0)
        for copy in spread():
            copy.start()
        for s in (0, 1):
            arrived(z, other, s, 1)
        multiply(z, other)

    @pl.when(jnp.logical_not(source))
    def _():
        for s in (0, 1):
            arrived(far, x, s, 1)
        for copy in crossing():
            copy.start()
        multiply(near, x)

    for s in (0, 1):
        arrived(near, other, s, 0)
    begin(pass_on(other, 0, 16))

    @pl.when(source)
    def _():
        multiply(near, x)

    for i in (1, 2, 3):
        ref = proj_all.at[(y + i) % 4, :, core]
        remote(ref, ref, ysend.at[0], yrecv.at[(y + i) % 4], at(z, x, 1 - core)).wait_recv()
    halves(core).start()

    for s in (0, 1):
        arrived(near, other, s, 1)
    multiply(near, other)

    @pl.when(jnp.logical_not(source))
    def _():
        for s in (0, 1):
            arrived(far, x, s, 0)
        multiply(far, x)
        for s in (0, 1):
            arrived(far, other, s, 0)
            arrived(far, other, s, 1)
            multiply(far, other, s * ROWS, ROWS)

    for cls in (0, 1):
        for s in (0, 1):

            @pl.when(core == s)
            def _():
                away, sibling, here = own_copies(cls, s)
                for copy in away:
                    copy.wait_send()

                @pl.when(core != kept)
                def _():
                    sibling.wait_send()

    for copy in fx:
        copy.wait_send()
    for mine, copy in pass_on(x, 1, 10) + pass_on(x, 0, 11) + pass_on(other, 0, 16):

        @pl.when(mine)
        def _():
            copy.wait_send()

    @pl.when(source)
    def _():
        for copy in spread():
            copy.wait_send()

    @pl.when(jnp.logical_not(source))
    def _():
        for copy in crossing():
            copy.wait_send()

    for copy in w_out_going + proj_going + quarter_going + [quarter_on(i) for i in (1, 2, 3)]:
        copy.wait_send()
    for copy in [along(i) for i in (1, 2, 3)] + [halves(core)]:
        copy.wait_send()
    halves(1 - core).wait_recv()
    proj_own.wait()
    remote(
        wout_hbm, wout_all.at[x * 2 + 1 - core], wsend.at[3], wrecv.at[3 + 1 - core], at(z, x, 1 - core)
    ).wait_recv()
    for c in (0, 1):
        remote(wout_hbm, wout_all.at[other * 2 + c], wsend.at[4], wrecv.at[5 + c], across(z, x, c)).wait_recv()


def project(hidden, gain, w_qkv, w_out, proj):
    vmem = pl.BlockSpec(memory_space=pltpu.VMEM)
    hbm = pl.BlockSpec(memory_space=pltpu.HBM)
    return pl.pallas_call(
        project_kernel,
        name="project",
        out_shape=(
            jax.ShapeDtypeStruct((6, LEN, 256), jnp.bfloat16),
            jax.ShapeDtypeStruct((4, 256, HW), jnp.bfloat16),
            jax.ShapeDtypeStruct((4, 8, 2, PROJ, 256), jnp.bfloat16),
        ),
        in_specs=[vmem, vmem, hbm, hbm, hbm],
        out_specs=(vmem, hbm, hbm),
        scratch_shapes=[
            pltpu.VMEM((ROWS, D), jnp.bfloat16),
            pltpu.VMEM((4, 2 * ROWS, D), jnp.bfloat16),
            pltpu.VMEM((2, 3, D, 256), jnp.bfloat16),
        ]
        + [pltpu.SemaphoreType.DMA((n,)) for n in (17, 16, 6, 7, 7, 8, 4, 5, 7)],
        compiler_params=pltpu.CompilerParams(
            collective_id=0, has_side_effects=True, vmem_limit_bytes=60 * MIB
        ),
    )(hidden, gain, w_qkv, w_out, proj)


def student_kernel(
    len_ref,
    scale_ref,
    qkv_ref,
    wout_hbm,
    hid_hbm,
    proj_hbm,
    student_ref,
    gain_ref,
    grad_ref,
    out_ref,
    stat_ref,
    wout_ref,
    hid_ref,
    proj_ref,
    norm_ref,
    normed,
    ctx,
    ctx_in,
    stage,
    parts,
    relay,
    mapped,
    delta,
    flipped,
    flipped_in,
    stat,
    stat_in,
    total,
    total_in,
    piece,
    piece_in,
    summed,
    send,
    recv,
    osend,
    orecv,
    rrecv,
    nsend,
    nrecv,
    dsend,
    drecv,
    ssend,
    srecv,
    tsend,
    trecv,
    gsend,
    grecv,
    asend,
    arecv,
    local,
):
    z, x, core = place()
    other = 1 - x
    kept = z // 2
    tp = lax.axis_index("tp")
    dp = lax.axis_index("dp")
    rel = (z - 2 * core + 4) % 4
    ahead = (rel == 0) | (rel == 3)
    step = jnp.where(ahead, 1, -1)
    via = jnp.where(ahead, 0, 1)
    source = rel < 2
    key_len = len_ref[dp * SEQS + core]
    count = len_ref[0]
    for i in range(1, len_ref.shape[0]):
        count += len_ref[i]
    terms = jnp.full((1, 128), 1.0, jnp.float32) * count.astype(jnp.float32) * HW
    factor = (2.0 * scale_ref[0] / terms)[:, :1]

    fetch_wout = pltpu.make_async_copy(wout_hbm, wout_ref, local.at[0])
    fetch_hid = pltpu.make_async_copy(hid_hbm.at[:, pl.ds(0, HW)], hid_ref, local.at[1])
    fetch_proj = pltpu.make_async_copy(proj_hbm, proj_ref, local.at[2])
    for copy in (fetch_wout, fetch_hid, fetch_proj):
        copy.start()

    def mate(i):
        return (tp + i) % 16

    def group(i):
        return (dp + i) % 8

    rows = student_ref[...].astype(jnp.float32)
    scale = lax.rsqrt(jnp.mean(rows * rows, axis=-1, keepdims=True) + 1e-06)
    normed[...] = (rows * scale * gain_ref[...]).astype(jnp.bfloat16)

    def attend(chunk, keys, zq, mine):
        start = pl.multiple_of(chunk * 256, 256)
        row = lax.broadcasted_iota(jnp.int32, (256, keys), 0) + start
        col = lax.broadcasted_iota(jnp.int32, (256, keys), 1)
        allowed = (col <= row) & (col < key_len)

        def pair(half, carry):
            for h in (0, 1):
                lanes = slice(h * HEAD, (h + 1) * HEAD)
                q = qkv_ref[half, pl.ds(start, 256), lanes]
                k = qkv_ref[2 + half, :keys, lanes]
                v = qkv_ref[4 + half, :keys, lanes]
                scores = lax.dot_general(
                    q, k, (((1,), (1,)), ((), ())), preferred_element_type=jnp.float32
                ) * (1.0 / math.sqrt(HEAD))
                scores = jnp.where(allowed, scores, -1e30)
                weights = jnp.exp(scores - jnp.max(scores, axis=-1, keepdims=True))
                norm = jnp.sum(weights, axis=-1, keepdims=True)
                out = jnp.dot(weights.astype(jnp.bfloat16), v, preferred_element_type=jnp.float32)
                ctx[zq * 2 + mine, half, :, lanes] = (out / norm).astype(jnp.bfloat16)
            return carry

        lax.fori_loop(0, 2, pair, 0)

    def swap(zq):
        return remote(ctx.at[zq * 2], ctx_in.at[zq], send.at[zq], recv.at[zq], at(z, other, core))

    greet(
        [{"tp": mate(i)} for i in range(1, 16)] + [{"dp": group(i)} for i in range(1, 8)],
        lambda: attend(other, 512, 0, 0),
    )
    swap(0).start()

    def block(chip_z, chip_x, c):
        chip = (chip_z % 4) * 2 + chip_x
        return norm_ref.at[pl.ds(pl.multiple_of((c * 8 + chip) * ROWS, 128), ROWS)]

    def block_sem(chip_z, chip_x):
        return nrecv.at[(chip_z % 4) * 2 + chip_x]

    norm_here = pltpu.make_async_copy(normed, block(z, x, core), local.at[3])
    norm_going = [
        remote(normed, block(z, x, core), nsend.at[i], block_sem(z, x), at(zz, xx, core))
        for i, (zz, xx) in enumerate(((z + 1, x), (z + 3, x), (z + 2, x), (z, other)))
    ]

    def norm_wait(chip_z, chip_x):
        ref = block(chip_z, chip_x, core)
        remote(ref, ref, nsend.at[0], block_sem(chip_z, chip_x), at(z, other, core)).wait_recv()

    def norm_on(i):
        ref = block(z + i, x, core)
        return remote(ref, ref, nsend.at[3 + i], block_sem(z + i, x), at(z, other, core))

    def norm_half(c):
        ref = norm_ref.at[pl.ds(pl.multiple_of(c * LEN, 128), LEN)]
        return remote(ref, ref, nsend.at[7], nrecv.at[8], at(z, x, 1 - core))

    def side(part):
        return pl.ds(pl.multiple_of(jnp.int32(part * WIDE), 128), WIDE)

    def summand(zq, s, part):
        return stage.at[zq, pl.ds(pl.multiple_of(s * ROWS, 16), ROWS), side(part)]

    def give(zq, s, part):
        slot = jnp.where(ahead, 2, 1)
        return remote(
            summand(zq, s, part),
            parts.at[slot, :, side(part)],
            osend.at[(zq * 2 + s) * PARTS + part],
            orecv.at[slot * PARTS + part],
            at(z + step + 4, x, s),
        )

    def pass_on(zq, s, part):
        return remote(
            summand(zq, s, part),
            relay.at[:, side(part)],
            osend.at[(zq * 2 + s) * PARTS + part],
            rrecv.at[part],
            at(z + (1 if s == 0 else 3), x, core),
        )

    def hand_over(zq, part):
        return remote(
            summand(zq, 1 - core, part),
            parts.at[0, :, side(part)],
            osend.at[(zq * 2 + 1 - core) * PARTS + part],
            orecv.at[part],
            at(z, x, 1 - core),
        )

    def keep(zq, part):
        return pltpu.make_async_copy(
            summand(zq, core, part), parts.at[0, :, side(part)], osend.at[(zq * 2 + core) * PARTS + part]
        )

    def is_near(zq):
        return (rel == 1 - zq) | (rel == 3 - zq)

    def is_far(zq):
        return rel == 2 + zq

    def is_own(zq):
        return rel == zq

    def project_out(zq, part):
        out = jnp.zeros((256, WIDE), jnp.float32)
        for k in (0, 1):
            out += jnp.dot(
                ctx[zq * 2 + 1, k], wout_ref[x * 2 + k, :, side(part)], preferred_element_type=jnp.float32
            )
            out += jnp.dot(
                ctx_in[zq, k], wout_ref[other * 2 + k, :, side(part)], preferred_element_type=jnp.float32
            )
        stage[zq, :, side(part)] = out.astype(jnp.bfloat16)

        @pl.when(is_far(zq))
        def _():
            for s in (0, 1):
                pass_on(zq, s, part).start()

        @pl.when(is_near(zq))
        def _():
            give(zq, 1 - via, part).start()

        @pl.when(is_own(zq))
        def _():
            keep(zq, part).start()
            hand_over(zq, part).start()

    def join(zq, part):
        @pl.when(is_near(zq))
        def _():
            src = relay.at[:, side(part)]
            remote(src, src, osend.at[0], rrecv.at[part], at(z, x, 1 - core)).wait_recv()

            def one(i, carry):
                here = pl.ds(pl.multiple_of(via * ROWS + i * 16, 16), 16)
                there = pl.ds(pl.multiple_of(i * 16, 16), 16)
                both = stage[zq, here, side(part)].astype(jnp.float32) + relay[there, side(part)].astype(
                    jnp.float32
                )
                stage[zq, here, side(part)] = both.astype(jnp.bfloat16)
                return carry

            lax.fori_loop(0, ROWS // 16, one, 0)
            give(zq, via, part).start()

    for copy in [norm_here] + norm_going[:3]:
        copy.start()
    attend(2 + other, 1024, 1, 0)
    swap(1).start()
    attend(x, 512, 0, 1)
    fetch_wout.wait()
    swap(0).wait_recv()
    for turn in TURN:
        project_out(0, (2 * core + turn) % PARTS)
    attend(2 + x, 1024, 1, 1)
    swap(1).wait_recv()
    for turn in TURN:
        project_out(1, (2 * core + 1 + turn) % PARTS)
    norm_going[3].start()
    for i in (1, 3, 2):
        norm_wait(z + i, x)
        norm_on(i).start()
    join(0, (2 * core + TURN[0]) % PARTS)

    fetch_proj.wait()

    def map_rows(n, carry):
        base = pl.multiple_of(n * 512, 512)
        out = jnp.zeros((ROWS, 512), jnp.float32)
        for k in range(4):
            out += lax.dot_general(
                normed[:, k * 256 : (k + 1) * 256],
                proj_ref[k, pl.ds(base, 512), :],
                (((1,), (1,)), ((), ())),
                preferred_element_type=jnp.float32,
            )
        mapped[:, pl.ds(base, 512)] = out
        return carry

    lax.fori_loop(0, HW // 512, map_rows, 0)
    for turn in TURN[1:]:
        join(0, (2 * core + turn) % PARTS)
    for turn in TURN:
        join(1, (2 * core + 1 + turn) % PARTS)
    fetch_hid.wait()
    position = (tp % 8) * ROWS + lax.broadcasted_iota(jnp.int32, (ROWS, 1), 0)
    valid = position < len_ref[dp * SEQS + kept]
    lane = pl.ds(pl.multiple_of((core * 8 + z * 2 + x) * ROWS, 128), ROWS)

    def owner(part, i):
        return part * EACH + (tp + i) % EACH

    def flip(part, i):
        src = flipped.at[pl.ds(pl.multiple_of(owner(part, i) * PROJ, 16), PROJ)]
        return remote(
            src, flipped_in.at[:, lane], dsend.at[part * EACH + i], drecv.at[tp], {"tp": owner(part, i)}
        )

    own_flip = pltpu.make_async_copy(
        flipped.at[pl.ds(pl.multiple_of(tp * PROJ, 16), PROJ)], flipped_in.at[:, lane], local.at[4]
    )

    def compare(n, loss):
        block_cols = pl.ds(pl.multiple_of(n * 128, 128), 128)
        mixed = parts[0, :, block_cols].astype(jnp.float32)
        for slot in (1, 2):
            mixed += parts[slot, :, block_cols].astype(jnp.float32)
        target = (hid_ref[:, block_cols].astype(jnp.float32) + mixed).astype(jnp.bfloat16)
        diff = jnp.where(valid, mapped[:, block_cols] - target.astype(jnp.float32), 0.0)
        scaled = diff * factor
        delta[:, block_cols] = scaled.astype(jnp.bfloat16)
        flipped[block_cols, :] = scaled.T.astype(jnp.bfloat16)
        return loss + diff * diff

    loss = jnp.zeros((ROWS, 128), jnp.float32)
    for turn in TURN:
        part = (z + turn) % PARTS
        for slot in (1, 2):
            ref = parts.at[slot, :, side(part)]
            remote(ref, ref, osend.at[0], orecv.at[slot * PARTS + part], at(z, x, 1 - core)).wait_recv()

        @pl.when(core == kept)
        def _():
            for zq in (0, 1):

                @pl.when(is_own(zq))
                def _():
                    keep(zq, part).wait()

        @pl.when(core != kept)
        def _():
            ref = parts.at[0, :, side(part)]
            remote(ref, ref, osend.at[0], orecv.at[part], at(z, x, 1 - core)).wait_recv()

        loss = lax.fori_loop(part * (WIDE // 128), (part + 1) * (WIDE // 128), compare, loss)
        for i in range(1, EACH):
            flip(part, i).start()

        @pl.when(tp // EACH == part)
        def _():
            own_flip.start()

        @pl.when(tp // EACH != part)
        def _():
            flip(part, 0).start()

    norm_here.wait()
    for i in range(4):
        norm_wait(z + i, other)
    norm_half(core).start()

    back = [jnp.dot(delta[...], proj_ref[k], preferred_element_type=jnp.float32) for k in range(4)]
    dots = jnp.zeros((ROWS, 1), jnp.float32)
    for k in range(4):
        cols = slice(k * 256, (k + 1) * 256)
        dots += jnp.sum(back[k] * gain_ref[:, cols] * rows[:, cols], axis=-1, keepdims=True)
    shift = dots * (scale * scale * scale) * (1.0 / DS)
    for k in range(4):
        cols = slice(k * 256, (k + 1) * 256)
        grad_ref[:, cols] = (
            back[k] * gain_ref[:, cols] * scale - rows[:, cols] * shift
        ).astype(jnp.bfloat16)
        part = jnp.sum(back[k] * (rows[:, cols] * scale), axis=0, keepdims=True)
        stat[2 * k : 2 * k + 1, :] = part[:, :128]
        stat[2 * k + 1 : 2 * k + 2, :] = part[:, 128:]
    stat[8:16, :] = jnp.zeros((8, 128), jnp.float32) + jnp.sum(loss)

    def tell(i):
        return remote(stat, stat_in.at[tp], ssend.at[i - 1], srecv.at[tp], {"tp": mate(i)})

    for i in range(1, 16):
        tell(i).start()

    norm_half(1 - core).wait_recv()
    for i in range(1, 16):
        far = mate(i)
        got = flipped_in.at[:, pl.ds(pl.multiple_of(((far % 2) * 8 + far // 2) * ROWS, 128), ROWS)]
        remote(got, got, dsend.at[0], drecv.at[far], {"tp": far}).wait_recv()
    own_flip.wait()

    def hand(g):
        return remote(piece.at[g], piece_in.at[dp], gsend.at[g], grecv.at[dp], {"dp": g})

    for k in range(4):
        out = jnp.dot(
            flipped_in[...], norm_ref[:, k * 256 : (k + 1) * 256], preferred_element_type=jnp.float32
        ).astype(jnp.bfloat16)
        for g in (2 * k, 2 * k + 1):
            piece[g] = out[:, (g % 2) * 128 : (g % 2 + 1) * 128]

            @pl.when(dp != g)
            def _():
                hand(g).start()

    for i in range(1, 16):
        far = stat_in.at[mate(i)]
        remote(far, far, ssend.at[0], srecv.at[mate(i)], {"tp": mate(i)}).wait_recv()
    stat_in[tp] = stat[...]
    total[...] = jnp.sum(stat_in[...], axis=0)

    def tell_groups(i):
        return remote(total, total_in.at[dp], tsend.at[i - 1], trecv.at[dp], {"dp": group(i)})

    for i in range(1, 8):
        tell_groups(i).start()

    for i in range(1, 8):
        far = piece_in.at[group(i)]
        remote(far, far, gsend.at[0], grecv.at[group(i)], {"dp": group(i)}).wait_recv()
    piece_in[dp] = piece[dp]
    acc = jnp.zeros((PROJ, 128), jnp.float32)
    for k in range(8):
        acc += piece_in[k].astype(jnp.float32)
    summed[...] = acc.astype(jnp.bfloat16)

    def column(g):
        return out_ref.at[:, pl.ds(pl.multiple_of(g * 128, 128), 128)]

    def publish(i):
        return remote(summed, column(dp), asend.at[i - 1], arecv.at[dp], {"dp": group(i)})

    own_column = pltpu.make_async_copy(summed, column(dp), local.at[5])
    own_column.start()
    for i in range(1, 8):
        publish(i).start()

    for i in range(1, 8):
        far = total_in.at[group(i)]
        remote(far, far, tsend.at[0], trecv.at[group(i)], {"dp": group(i)}).wait_recv()
    total_in[dp] = total[...]
    whole = jnp.sum(total_in[...], axis=0)
    stat_ref[:8, :] = whole[:8, :]
    stat_ref[8:, :] = whole[8:, :] / terms

    for zq in (0, 1):
        swap(zq).wait_send()
        for part in range(PARTS):

            @pl.when(is_far(zq))
            def _():
                for s in (0, 1):
                    pass_on(zq, s, part).wait_send()

            @pl.when(is_near(zq))
            def _():
                for s in (0, 1):
                    give(zq, s, part).wait_send()

            @pl.when(is_own(zq))
            def _():
                hand_over(zq, part).wait_send()

                @pl.when(core != kept)
                def _():
                    keep(zq, part).wait()

    for copy in norm_going + [norm_on(i) for i in (1, 2, 3)] + [norm_half(core)]:
        copy.wait_send()
    for part in range(PARTS):
        for i in range(1, EACH):
            flip(part, i).wait_send()

        @pl.when(tp // EACH != part)
        def _():
            flip(part, 0).wait_send()

    for i in range(1, 16):
        tell(i).wait_send()
    for g in range(8):

        @pl.when(dp != g)
        def _():
            hand(g).wait_send()

    for i in range(1, 8):
        tell_groups(i).wait_send()
    for i in range(1, 8):
        far = column(group(i))
        remote(far, far, asend.at[0], arecv.at[group(i)], {"dp": group(i)}).wait_recv()
        publish(i).wait_send()
    own_column.wait()


def student(lengths, loss_scale, qkv, w_out, hidden, proj, rows, gain):
    vmem = pl.BlockSpec(memory_space=pltpu.VMEM)
    smem = pl.BlockSpec(memory_space=pltpu.SMEM)
    hbm = pl.BlockSpec(memory_space=pltpu.HBM)
    return pl.pallas_call(
        student_kernel,
        name="student",
        out_shape=(
            jax.ShapeDtypeStruct((ROWS, DS), jnp.bfloat16),
            jax.ShapeDtypeStruct((PROJ, DS), jnp.bfloat16),
            jax.ShapeDtypeStruct((16, 128), jnp.float32),
        ),
        in_specs=[smem, smem, vmem, hbm, hbm, hbm, vmem, vmem],
        out_specs=(vmem, vmem, vmem),
        scratch_shapes=[
            pltpu.VMEM((4, 256, HW), jnp.bfloat16),
            pltpu.VMEM((ROWS, HW), jnp.bfloat16),
            pltpu.VMEM((4, HW, 256), jnp.bfloat16),
            pltpu.VMEM((2 * LEN, DS), jnp.bfloat16),
            pltpu.VMEM((ROWS, DS), jnp.bfloat16),
            pltpu.VMEM((4, 2, 256, 256), jnp.bfloat16),
            pltpu.VMEM((2, 2, 256, 256), jnp.bfloat16),
            pltpu.VMEM((2, 256, HW), jnp.bfloat16),
            pltpu.VMEM((3, ROWS, HW), jnp.bfloat16),
            pltpu.VMEM((ROWS, HW), jnp.bfloat16),
            pltpu.VMEM((ROWS, HW), jnp.float32),
            pltpu.VMEM((ROWS, HW), jnp.bfloat16),
            pltpu.VMEM((HW, ROWS), jnp.bfloat16),
            pltpu.VMEM((PROJ, 2 * LEN), jnp.bfloat16),
            pltpu.VMEM((16, 128), jnp.float32),
            pltpu.VMEM((16, 16, 128), jnp.float32),
            pltpu.VMEM((16, 128), jnp.float32),
            pltpu.VMEM((8, 16, 128), jnp.float32),
            pltpu.VMEM((8, PROJ, 128), jnp.bfloat16),
            pltpu.VMEM((8, PROJ, 128), jnp.bfloat16),
            pltpu.VMEM((PROJ, 128), jnp.bfloat16),
        ]
        + [pltpu.SemaphoreType.DMA((n,)) for n in (2, 2, 4 * PARTS, 3 * PARTS, PARTS, 8, 9, 16, 16, 15, 16, 7, 8, 8, 8, 7, 8, 6)],
        compiler_params=pltpu.CompilerParams(
            collective_id=1, has_side_effects=True, vmem_limit_bytes=56 * MIB
        ),
    )(lengths, loss_scale, qkv, w_out, hidden, proj, rows, gain)


def finish_kernel(grad_in, proj_in, stat_in, grad_ref, proj_ref, gain_ref, loss_ref):
    grad_ref[...] = grad_in[...]
    proj_ref[...] = proj_in[...]
    gain_ref[...] = stat_in[:8, :]
    loss_ref[...] = stat_in[8:9, :1]


def finish(grad, proj, stat):
    return pl.pallas_call(
        finish_kernel,
        name="finish",
        out_shape=(
            jax.ShapeDtypeStruct(grad.shape, grad.dtype),
            jax.ShapeDtypeStruct(proj.shape, proj.dtype),
            jax.ShapeDtypeStruct((8, 128), jnp.float32),
            jax.ShapeDtypeStruct((1, 1), jnp.float32),
        ),
    )(grad, proj, stat)


def shards(
    hidden_in, norm_gain, w_qkv, w_out, lengths, student_in, student_gain, proj_weight, loss_scale
):
    qkv, w_out_all, proj_all = project(hidden_in, norm_gain.reshape(1, D), w_qkv, w_out, proj_weight)
    row_grad, proj_grad, stat = student(
        lengths,
        loss_scale,
        qkv,
        w_out_all,
        hidden_in,
        proj_all.reshape(4, HW, 256),
        student_in,
        student_gain.reshape(1, DS),
    )
    row_grad, proj_grad, gain, loss = finish(row_grad, proj_grad, stat)
    return row_grad, proj_grad, gain.reshape(DS), loss.reshape(())


def solution(mesh):
    placed = (
        P(("dp", "tp"), None),
        P(),
        P(None, None, "tp"),
        P("tp", None),
        P(),
        P(("dp", "tp"), None),
        P(),
        P("tp", None),
        P(),
    )
    return jax.shard_map(
        shards,
        mesh=mesh,
        in_specs=placed,
        out_specs=(P(("dp", "tp"), None), P("tp", None), P(), P()),
        check_vma=False,
    )
```

```python
import functools
import math

import jax
import jax.numpy as jnp
from jax import lax
from jax.experimental import pallas as pl
from jax.experimental.pallas import tpu as pltpu
from jax.sharding import PartitionSpec as P

HEAD = 128
HW = 3584
PARTS = 4
WIDE = HW // PARTS
TURN = (2, 1, 3, 0)
EACH = 16 // PARTS
LEN = 1024
SEQS = 2
D = 7168
DS = 1024
PROJ = 224
ROWS = 128
FIRST = (64, 64)
MESH = pl.DeviceIdType.MESH
MIB = 1 << 20


def place():
    tp = lax.axis_index("tp")
    return tp // 4, (tp // 2) % 2, tp % 2


def at(z, x, core):
    return {"tp": (z % 4) * 4 + x * 2 + core}


def across(z, x, core):
    dp = lax.axis_index("dp")
    return {"tp": z * 4 + (1 - x) * 2 + core, "dp": (1 - dp // 4) * 4 + dp % 4}


def beside(z, x, core, i):
    dp = lax.axis_index("dp")
    return {"tp": z * 4 + x * 2 + core, "dp": dp // 4 * 4 + (dp + i) % 4}


def remote(src, dst, send, recv, device):
    return pltpu.make_async_remote_copy(
        src_ref=src, dst_ref=dst, send_sem=send, recv_sem=recv, device_id=device, device_id_type=MESH
    )


def rms_norm(rows, gain):
    return rows * lax.rsqrt(jnp.mean(rows * rows, axis=-1, keepdims=True) + 1e-06) * gain


def greet(devices, meanwhile):
    barrier = pltpu.get_barrier_semaphore()
    for device in devices:
        pl.semaphore_signal(barrier, 1, device_id=device, device_id_type=MESH)
    meanwhile()
    pl.semaphore_wait(barrier, len(devices))


def project_kernel(
    x_ref,
    gain_ref,
    w_hbm,
    wout_hbm,
    proj_hbm,
    qkv_ref,
    wout_all,
    proj_all,
    normed,
    rows,
    w,
    send,
    recv,
    wsend,
    wrecv,
    psend,
    precv,
    ysend,
    yrecv,
    local,
):
    z, x, core = place()
    other = 1 - x
    kept = z // 2
    rel = (z - 2 * core + 4) % 4
    ahead = (rel == 0) | (rel == 3)
    step = jnp.where(ahead, 1, -1)
    near = (z + step + 4) % 4
    onward = (z - step + 4) % 4
    far = (z + 2) % 4

    def norm(start, size):
        def one(i, carry):
            block = pl.ds(pl.multiple_of(start + i * 16, 16), 16)
            values = x_ref[block, :].astype(jnp.float32)
            centred = values - jnp.mean(values, axis=-1, keepdims=True)
            spread = jnp.mean(centred * centred, axis=-1, keepdims=True)
            normed[block, :] = (centred * lax.rsqrt(spread + 1e-05) * gain_ref[...]).astype(jnp.bfloat16)
            return carry

        lax.fori_loop(0, size // 16, one, 0)

    greet(
        [at(z, x, 1 - core)]
        + [at(zz, x, c) for zz in (z + 1, z + 3) for c in (0, 1)]
        + [at(z, other, c) for c in (0, 1)]
        + [across(z, x, c) for c in (0, 1)]
        + [at(far, x, core)]
        + [beside(z, x, core, i) for i in (1, 2, 3)],
        lambda: norm(min(FIRST), ROWS - min(FIRST)),
    )

    y = lax.axis_index("dp") % 4

    def held(chip_z, chip_x):
        return proj_all.at[y, (chip_z % 4) * 2 + chip_x, core]

    def held_sem(chip_z, chip_x):
        return precv.at[(chip_z % 4) * 2 + chip_x]

    quarter = proj_hbm.at[:, pl.ds(pl.multiple_of(y * 256, 256), 256)]
    quarter_here = pltpu.make_async_copy(quarter, held(z, x), local.at[6])
    quarter_going = [
        remote(quarter, held(z, x), psend.at[i], held_sem(z, x), device)
        for i, device in enumerate(
            (at(z + 1, x, core), at(z + 3, x, core), at(z + 2, x, core), across(z, x, core))
        )
    ]
    for copy in [quarter_here] + quarter_going:
        copy.start()

    def quarter_wait(chip_z, chip_x):
        ref = held(chip_z, chip_x)
        remote(ref, ref, psend.at[0], held_sem(chip_z, chip_x), across(z, x, core)).wait_recv()

    def quarter_on(i):
        ref = held(z + i, x)
        return remote(ref, ref, psend.at[3 + i], held_sem(z + i, x), across(z, x, core))

    def along(i):
        ref = proj_all.at[y, :, core]
        return remote(ref, ref, ysend.at[i - 1], yrecv.at[y], beside(z, x, core, i))

    w_out_going = [
        remote(w_hbm.at[k], w.at[core, k], wsend.at[k], wrecv.at[k], at(z, x, 1 - core)) for k in range(3)
    ]
    w_own = [pltpu.make_async_copy(w_hbm.at[k], w.at[core, k], local.at[k]) for k in range(3)]
    slot = x * 2 + core
    proj_going = [
        remote(wout_hbm, wout_all.at[slot], wsend.at[3], wrecv.at[3 + core], at(z, x, 1 - core)),
        remote(wout_hbm, wout_all.at[slot], wsend.at[4], wrecv.at[5 + core], across(z, x, core)),
    ]
    far_slot = wout_all.at[other * 2 + core]
    proj_on = remote(far_slot, far_slot, wsend.at[5], wrecv.at[5 + core], at(z, x, 1 - core))
    proj_own = pltpu.make_async_copy(wout_hbm, wout_all.at[slot], local.at[3])
    for copy in w_own + w_out_going + proj_going[:1] + [proj_own]:
        copy.start()

    def part(chunk_z, chunk_x, s, cls):
        chunk = (chunk_z % 2) * 2 + chunk_x
        start, size = ((0, FIRST[s]), (FIRST[s], ROWS - FIRST[s]))[cls]
        return rows.at[chunk, pl.ds(s * ROWS + start, size)]

    def sem(chunk_z, chunk_x, s, cls):
        return recv.at[((chunk_z % 2) * 2 + chunk_x) * 4 + s * 2 + cls]

    def arrived(chunk_z, chunk_x, s, cls):
        ref = part(chunk_z, chunk_x, s, cls)
        remote(ref, ref, send.at[0], sem(chunk_z, chunk_x, s, cls), at(z, x, 1 - core)).wait_recv()

    def forward(chunk_z, chunk_x, s, cls, index, device):
        ref = part(chunk_z, chunk_x, s, cls)
        return remote(ref, ref, send.at[index], sem(chunk_z, chunk_x, s, cls), device)

    def own_copies(cls, s):
        start, size = ((0, FIRST[s]), (FIRST[s], ROWS - FIRST[s]))[cls]
        src = normed.at[pl.ds(start, size)]
        dst = part(z, x, s, cls)
        got = sem(z, x, s, cls)
        base = cls * 4
        return (
            [
                remote(src, dst, send.at[base], got, at(z + 1, x, kept)),
                remote(src, dst, send.at[base + 1], got, at(z + 3, x, kept)),
                remote(src, dst, send.at[base + 2], got, at(z, other, kept)),
            ],
            remote(src, dst, send.at[base + 3], got, at(z, x, 1 - core)),
            pltpu.make_async_copy(src, dst, local.at[4 + cls]),
        )

    def send_own(cls, over_x, rest):
        for s in (0, 1):

            @pl.when(core == s)
            def _():
                away, sibling, here = own_copies(cls, s)
                if over_x:
                    away[2].start()
                if rest:
                    for copy in away[:2]:
                        copy.start()

                    @pl.when(core == kept)
                    def _():
                        here.start()

                    @pl.when(core != kept)
                    def _():
                        sibling.start()

    send_own(1, False, True)
    norm(0, min(FIRST))
    send_own(0, True, True)
    send_own(1, True, False)

    def multiply(chunk_z, chunk_x, start=0, size=2 * ROWS):
        chunk = (chunk_z % 2) * 2 + chunk_x

        def one(n, carry):
            out = jnp.dot(
                rows[chunk, start : start + size], w[n % 2, n // 2], preferred_element_type=jnp.float32
            )
            qkv_ref[n, pl.ds(pl.multiple_of(chunk * 256 + start, 128), size), :] = out.astype(jnp.bfloat16)
            return carry

        lax.fori_loop(0, 6, one, 0)

    source = rel < 2

    for i in (1, 3, 2):
        quarter_wait(z + i, x)
        quarter_on(i).start()
    for copy in proj_going[1:]:
        copy.start()

    fx = []
    for s in (0, 1):
        arrived(near, x, s, 1)
        fx.append(forward(near, x, s, 1, 8 + s, at(z, other, core)))
        fx[-1].start()
    def pass_on(chunk_x, cls, index):
        return [
            (ahead == bool(s), forward(near, chunk_x, s, cls, index, at(onward, x, core))) for s in (0, 1)
        ]

    def begin(pairs):
        for mine, copy in pairs:

            @pl.when(mine)
            def _():
                copy.start()

    begin(pass_on(x, 1, 10))


    for copy in w_own:
        copy.wait()
    for k in range(3):
        remote(w_hbm.at[k], w.at[1 - core, k], wsend.at[k], wrecv.at[k], at(z, x, 1 - core)).wait_recv()

    @pl.when(source)
    def _():
        for cls in (0, 1):
            for s in (0, 1):

                @pl.when(core != s)
                def _():
                    arrived(z, x, s, cls)

                @pl.when(core == s)
                def _():
                    own_copies(cls, s)[2].wait()

        multiply(z, x)

    quarter_here.wait()
    for i in range(4):
        quarter_wait(z + i, other)
    for i in (1, 2, 3):
        along(i).start()

    for s in (0, 1):
        arrived(near, x, s, 0)
    begin(pass_on(x, 0, 11))

    def spread():
        return [
            forward(z, other, s, 0, 12 + s * 2 + i, at(zz, x, core))
            for s, i, zz in ((0, 0, z + 1), (1, 1, z + 3), (1, 0, z + 1), (0, 1, z + 3))
        ]

    def crossing():
        return [forward(far, x, s, 1, 12 + s, at(z, other, core)) for s in (0, 1)]

    @pl.when(source)
    def _():
        for s in (0, 1):
            arrived(z, other, s, 0)
        for copy in spread():
            copy.start()
        for s in (0, 1):
            arrived(z, other, s, 1)
        multiply(z, other)

    @pl.when(jnp.logical_not(source))
    def _():
        for s in (0, 1):
            arrived(far, x, s, 1)
        for copy in crossing():
            copy.start()
        multiply(near, x)

    for s in (0, 1):
        arrived(near, other, s, 0)
    begin(pass_on(other, 0, 16))

    @pl.when(source)
    def _():
        multiply(near, x)

    remote(far_slot, far_slot, wsend.at[4], wrecv.at[5 + core], across(z, x, core)).wait_recv()
    proj_on.start()

    for s in (0, 1):
        arrived(near, other, s, 1)
    multiply(near, other)

    @pl.when(jnp.logical_not(source))
    def _():
        for s in (0, 1):
            arrived(far, x, s, 0)
        multiply(far, x)
        for s in (0, 1):
            arrived(far, other, s, 0)
            arrived(far, other, s, 1)
            multiply(far, other, s * ROWS, ROWS)

    for cls in (0, 1):
        for s in (0, 1):

            @pl.when(core == s)
            def _():
                away, sibling, here = own_copies(cls, s)
                for copy in away:
                    copy.wait_send()

                @pl.when(core != kept)
                def _():
                    sibling.wait_send()

    for copy in fx:
        copy.wait_send()
    for mine, copy in pass_on(x, 1, 10) + pass_on(x, 0, 11) + pass_on(other, 0, 16):

        @pl.when(mine)
        def _():
            copy.wait_send()

    @pl.when(source)
    def _():
        for copy in spread():
            copy.wait_send()

    @pl.when(jnp.logical_not(source))
    def _():
        for copy in crossing():
            copy.wait_send()

    for copy in w_out_going + proj_going + [proj_on] + quarter_going + [quarter_on(i) for i in (1, 2, 3)]:
        copy.wait_send()
    for i in (1, 2, 3):
        along(i).wait_send()
        ref = proj_all.at[(y + i) % 4, :, core]
        remote(ref, ref, ysend.at[0], yrecv.at[(y + i) % 4], at(z, x, 1 - core)).wait_recv()
    proj_own.wait()
    remote(
        wout_hbm, wout_all.at[x * 2 + 1 - core], wsend.at[3], wrecv.at[3 + 1 - core], at(z, x, 1 - core)
    ).wait_recv()
    beyond = wout_all.at[other * 2 + 1 - core]
    remote(beyond, beyond, wsend.at[5], wrecv.at[5 + 1 - core], at(z, x, 1 - core)).wait_recv()


def project(hidden, gain, w_qkv, w_out, proj):
    vmem = pl.BlockSpec(memory_space=pltpu.VMEM)
    hbm = pl.BlockSpec(memory_space=pltpu.HBM)
    return pl.pallas_call(
        project_kernel,
        name="project",
        out_shape=(
            jax.ShapeDtypeStruct((6, LEN, 256), jnp.bfloat16),
            jax.ShapeDtypeStruct((4, 256, HW), jnp.bfloat16),
            jax.ShapeDtypeStruct((4, 8, 2, PROJ, 256), jnp.bfloat16),
        ),
        in_specs=[vmem, vmem, hbm, hbm, hbm],
        out_specs=(vmem, hbm, hbm),
        scratch_shapes=[
            pltpu.VMEM((ROWS, D), jnp.bfloat16),
            pltpu.VMEM((4, 2 * ROWS, D), jnp.bfloat16),
            pltpu.VMEM((2, 3, D, 256), jnp.bfloat16),
        ]
        + [pltpu.SemaphoreType.DMA((n,)) for n in (17, 16, 6, 7, 7, 8, 3, 4, 7)],
        compiler_params=pltpu.CompilerParams(
            collective_id=0, has_side_effects=True, vmem_limit_bytes=60 * MIB
        ),
    )(hidden, gain, w_qkv, w_out, proj)


def student_kernel(
    len_ref,
    scale_ref,
    qkv_ref,
    wout_hbm,
    hid_hbm,
    proj_hbm,
    student_ref,
    gain_ref,
    grad_ref,
    out_ref,
    stat_ref,
    wout_ref,
    hid_ref,
    proj_ref,
    norm_ref,
    normed,
    ctx,
    ctx_in,
    stage,
    parts,
    relay,
    mapped,
    delta,
    flipped,
    flipped_in,
    stat,
    stat_in,
    total,
    total_in,
    piece,
    piece_in,
    summed,
    send,
    recv,
    osend,
    orecv,
    rrecv,
    nsend,
    nrecv,
    dsend,
    drecv,
    ssend,
    srecv,
    tsend,
    trecv,
    gsend,
    grecv,
    asend,
    arecv,
    plocal,
    psend,
    precv,
    local,
):
    z, x, core = place()
    other = 1 - x
    kept = z // 2
    tp = lax.axis_index("tp")
    dp = lax.axis_index("dp")
    rel = (z - 2 * core + 4) % 4
    ahead = (rel == 0) | (rel == 3)
    step = jnp.where(ahead, 1, -1)
    via = jnp.where(ahead, 0, 1)
    source = rel < 2
    key_len = len_ref[dp * SEQS + core]
    count = len_ref[0]
    for i in range(1, len_ref.shape[0]):
        count += len_ref[i]
    terms = jnp.full((1, 128), 1.0, jnp.float32) * count.astype(jnp.float32) * HW
    factor = (2.0 * scale_ref[0] / terms)[:, :1]

    fetch_wout = pltpu.make_async_copy(wout_hbm, wout_ref, local.at[0])
    fetch_hid = pltpu.make_async_copy(hid_hbm.at[:, pl.ds(0, HW)], hid_ref, local.at[1])

    def proj_rows(chip, c):
        return proj_ref.at[:, pl.ds(pl.multiple_of(chip * 2 * PROJ + c * PROJ, 16), PROJ)]

    fetch_proj = [
        pltpu.make_async_copy(proj_hbm.at[:, chip, core], proj_rows(chip, core), plocal.at[chip])
        for chip in range(8)
    ]
    share_proj = [
        remote(
            proj_hbm.at[:, chip, core], proj_rows(chip, core), psend.at[chip], precv.at[chip], at(z, x, 1 - core)
        )
        for chip in range(8)
    ]
    for copy in [fetch_wout, fetch_hid] + fetch_proj:
        copy.start()

    def mate(i):
        return (tp + i) % 16

    def group(i):
        return (dp + i) % 8

    rows = student_ref[...].astype(jnp.float32)
    scale = lax.rsqrt(jnp.mean(rows * rows, axis=-1, keepdims=True) + 1e-06)
    normed[...] = (rows * scale * gain_ref[...]).astype(jnp.bfloat16)

    def attend(chunk, keys, zq, mine):
        start = pl.multiple_of(chunk * 256, 256)
        row = lax.broadcasted_iota(jnp.int32, (256, keys), 0) + start
        col = lax.broadcasted_iota(jnp.int32, (256, keys), 1)
        allowed = (col <= row) & (col < key_len)

        def pair(half, carry):
            for h in (0, 1):
                lanes = slice(h * HEAD, (h + 1) * HEAD)
                q = qkv_ref[half, pl.ds(start, 256), lanes]
                k = qkv_ref[2 + half, :keys, lanes]
                v = qkv_ref[4 + half, :keys, lanes]
                scores = lax.dot_general(
                    q, k, (((1,), (1,)), ((), ())), preferred_element_type=jnp.float32
                ) * (1.0 / math.sqrt(HEAD))
                scores = jnp.where(allowed, scores, -1e30)
                weights = jnp.exp(scores - jnp.max(scores, axis=-1, keepdims=True))
                norm = jnp.sum(weights, axis=-1, keepdims=True)
                out = jnp.dot(weights.astype(jnp.bfloat16), v, preferred_element_type=jnp.float32)
                ctx[zq * 2 + mine, half, :, lanes] = (out / norm).astype(jnp.bfloat16)
            return carry

        lax.fori_loop(0, 2, pair, 0)

    def swap(zq):
        return remote(ctx.at[zq * 2], ctx_in.at[zq], send.at[zq], recv.at[zq], at(z, other, core))

    greet(
        [{"tp": mate(i)} for i in range(1, 16)] + [{"dp": group(i)} for i in range(1, 8)],
        lambda: attend(other, 512, 0, 0),
    )
    swap(0).start()

    def block(chip_z, chip_x, c):
        chip = (chip_z % 4) * 2 + chip_x
        return norm_ref.at[pl.ds(pl.multiple_of((c * 8 + chip) * ROWS, 128), ROWS)]

    def block_sem(chip_z, chip_x):
        return nrecv.at[(chip_z % 4) * 2 + chip_x]

    norm_here = pltpu.make_async_copy(normed, block(z, x, core), local.at[3])
    norm_going = [
        remote(normed, block(z, x, core), nsend.at[i], block_sem(z, x), at(zz, xx, core))
        for i, (zz, xx) in enumerate(((z + 1, x), (z + 3, x), (z + 2, x), (z, other)))
    ]

    def norm_wait(chip_z, chip_x):
        ref = block(chip_z, chip_x, core)
        remote(ref, ref, nsend.at[0], block_sem(chip_z, chip_x), at(z, other, core)).wait_recv()

    def norm_on(i):
        ref = block(z + i, x, core)
        return remote(ref, ref, nsend.at[3 + i], block_sem(z + i, x), at(z, other, core))

    def norm_half(c):
        ref = norm_ref.at[pl.ds(pl.multiple_of(c * LEN, 128), LEN)]
        return remote(ref, ref, nsend.at[7], nrecv.at[8], at(z, x, 1 - core))

    def side(part):
        return pl.ds(pl.multiple_of(jnp.int32(part * WIDE), 128), WIDE)

    def summand(zq, s, part):
        return stage.at[zq, pl.ds(pl.multiple_of(s * ROWS, 16), ROWS), side(part)]

    def give(zq, s, part):
        slot = jnp.where(ahead, 2, 1)
        return remote(
            summand(zq, s, part),
            parts.at[slot, :, side(part)],
            osend.at[(zq * 2 + s) * PARTS + part],
            orecv.at[slot * PARTS + part],
            at(z + step + 4, x, s),
        )

    def pass_on(zq, s, part):
        return remote(
            summand(zq, s, part),
            relay.at[:, side(part)],
            osend.at[(zq * 2 + s) * PARTS + part],
            rrecv.at[part],
            at(z + (1 if s == 0 else 3), x, core),
        )

    def hand_over(zq, part):
        return remote(
            summand(zq, 1 - core, part),
            parts.at[0, :, side(part)],
            osend.at[(zq * 2 + 1 - core) * PARTS + part],
            orecv.at[part],
            at(z, x, 1 - core),
        )

    def keep(zq, part):
        return pltpu.make_async_copy(
            summand(zq, core, part), parts.at[0, :, side(part)], osend.at[(zq * 2 + core) * PARTS + part]
        )

    def is_near(zq):
        return (rel == 1 - zq) | (rel == 3 - zq)

    def is_far(zq):
        return rel == 2 + zq

    def is_own(zq):
        return rel == zq

    def project_out(zq, part):
        out = jnp.zeros((256, WIDE), jnp.float32)
        for k in (0, 1):
            out += jnp.dot(
                ctx[zq * 2 + 1, k], wout_ref[x * 2 + k, :, side(part)], preferred_element_type=jnp.float32
            )
            out += jnp.dot(
                ctx_in[zq, k], wout_ref[other * 2 + k, :, side(part)], preferred_element_type=jnp.float32
            )
        stage[zq, :, side(part)] = out.astype(jnp.bfloat16)

        @pl.when(is_far(zq))
        def _():
            for s in (0, 1):
                pass_on(zq, s, part).start()

        @pl.when(is_near(zq))
        def _():
            give(zq, 1 - via, part).start()

        @pl.when(is_own(zq))
        def _():
            keep(zq, part).start()
            hand_over(zq, part).start()

    def join(zq, part):
        @pl.when(is_near(zq))
        def _():
            src = relay.at[:, side(part)]
            remote(src, src, osend.at[0], rrecv.at[part], at(z, x, 1 - core)).wait_recv()

            def one(i, carry):
                here = pl.ds(pl.multiple_of(via * ROWS + i * 16, 16), 16)
                there = pl.ds(pl.multiple_of(i * 16, 16), 16)
                both = stage[zq, here, side(part)].astype(jnp.float32) + relay[there, side(part)].astype(
                    jnp.float32
                )
                stage[zq, here, side(part)] = both.astype(jnp.bfloat16)
                return carry

            lax.fori_loop(0, ROWS // 16, one, 0)
            give(zq, via, part).start()

    for copy in [norm_here] + norm_going[:3] + share_proj:
        copy.start()
    attend(2 + other, 1024, 1, 0)
    swap(1).start()
    attend(x, 512, 0, 1)
    fetch_wout.wait()
    swap(0).wait_recv()
    for turn in TURN:
        project_out(0, (2 * core + turn) % PARTS)
    attend(2 + x, 1024, 1, 1)
    swap(1).wait_recv()
    for turn in TURN:
        project_out(1, (2 * core + 1 + turn) % PARTS)
    norm_going[3].start()
    for i in (1, 3, 2):
        norm_wait(z + i, x)
        norm_on(i).start()
    join(0, (2 * core + TURN[0]) % PARTS)

    for chip in range(8):
        fetch_proj[chip].wait()
        got = proj_rows(chip, 1 - core)
        remote(got, got, psend.at[0], precv.at[chip], at(z, x, 1 - core)).wait_recv()

    def map_rows(n, carry):
        base = pl.multiple_of(n * 512, 512)
        out = jnp.zeros((ROWS, 512), jnp.float32)
        for k in range(4):
            out += lax.dot_general(
                normed[:, k * 256 : (k + 1) * 256],
                proj_ref[k, pl.ds(base, 512), :],
                (((1,), (1,)), ((), ())),
                preferred_element_type=jnp.float32,
            )
        mapped[:, pl.ds(base, 512)] = out
        return carry

    lax.fori_loop(0, HW // 512, map_rows, 0)
    for turn in TURN[1:]:
        join(0, (2 * core + turn) % PARTS)
    for turn in TURN:
        join(1, (2 * core + 1 + turn) % PARTS)
    fetch_hid.wait()
    position = (tp % 8) * ROWS + lax.broadcasted_iota(jnp.int32, (ROWS, 1), 0)
    valid = position < len_ref[dp * SEQS + kept]
    lane = pl.ds(pl.multiple_of((core * 8 + z * 2 + x) * ROWS, 128), ROWS)

    def owner(part, i):
        return part * EACH + (tp + i) % EACH

    def flip(part, i):
        src = flipped.at[pl.ds(pl.multiple_of(owner(part, i) * PROJ, 16), PROJ)]
        return remote(
            src, flipped_in.at[:, lane], dsend.at[part * EACH + i], drecv.at[tp], {"tp": owner(part, i)}
        )

    own_flip = pltpu.make_async_copy(
        flipped.at[pl.ds(pl.multiple_of(tp * PROJ, 16), PROJ)], flipped_in.at[:, lane], local.at[4]
    )

    def compare(n, loss):
        block_cols = pl.ds(pl.multiple_of(n * 128, 128), 128)
        mixed = parts[0, :, block_cols].astype(jnp.float32)
        for slot in (1, 2):
            mixed += parts[slot, :, block_cols].astype(jnp.float32)
        target = (hid_ref[:, block_cols].astype(jnp.float32) + mixed).astype(jnp.bfloat16)
        diff = jnp.where(valid, mapped[:, block_cols] - target.astype(jnp.float32), 0.0)
        scaled = diff * factor
        delta[:, block_cols] = scaled.astype(jnp.bfloat16)
        flipped[block_cols, :] = scaled.T.astype(jnp.bfloat16)
        return loss + diff * diff

    loss = jnp.zeros((ROWS, 128), jnp.float32)
    for turn in TURN:
        part = (z + turn) % PARTS
        for slot in (1, 2):
            ref = parts.at[slot, :, side(part)]
            remote(ref, ref, osend.at[0], orecv.at[slot * PARTS + part], at(z, x, 1 - core)).wait_recv()

        @pl.when(core == kept)
        def _():
            for zq in (0, 1):

                @pl.when(is_own(zq))
                def _():
                    keep(zq, part).wait()

        @pl.when(core != kept)
        def _():
            ref = parts.at[0, :, side(part)]
            remote(ref, ref, osend.at[0], orecv.at[part], at(z, x, 1 - core)).wait_recv()

        loss = lax.fori_loop(part * (WIDE // 128), (part + 1) * (WIDE // 128), compare, loss)
        for i in range(1, EACH):
            flip(part, i).start()

        @pl.when(tp // EACH == part)
        def _():
            own_flip.start()

        @pl.when(tp // EACH != part)
        def _():
            flip(part, 0).start()

    norm_here.wait()
    for i in range(4):
        norm_wait(z + i, other)
    norm_half(core).start()

    back = [jnp.dot(delta[...], proj_ref[k], preferred_element_type=jnp.float32) for k in range(4)]
    dots = jnp.zeros((ROWS, 1), jnp.float32)
    for k in range(4):
        cols = slice(k * 256, (k + 1) * 256)
        dots += jnp.sum(back[k] * gain_ref[:, cols] * rows[:, cols], axis=-1, keepdims=True)
    shift = dots * (scale * scale * scale) * (1.0 / DS)
    for k in range(4):
        cols = slice(k * 256, (k + 1) * 256)
        grad_ref[:, cols] = (
            back[k] * gain_ref[:, cols] * scale - rows[:, cols] * shift
        ).astype(jnp.bfloat16)
        part = jnp.sum(back[k] * (rows[:, cols] * scale), axis=0, keepdims=True)
        stat[2 * k : 2 * k + 1, :] = part[:, :128]
        stat[2 * k + 1 : 2 * k + 2, :] = part[:, 128:]
    stat[8:16, :] = jnp.zeros((8, 128), jnp.float32) + jnp.sum(loss)

    def tell(i):
        return remote(stat, stat_in.at[tp], ssend.at[i - 1], srecv.at[tp], {"tp": mate(i)})

    for i in range(1, 16):
        tell(i).start()

    norm_half(1 - core).wait_recv()
    for i in range(1, 16):
        far = mate(i)
        got = flipped_in.at[:, pl.ds(pl.multiple_of(((far % 2) * 8 + far // 2) * ROWS, 128), ROWS)]
        remote(got, got, dsend.at[0], drecv.at[far], {"tp": far}).wait_recv()
    own_flip.wait()

    def hand(g):
        return remote(piece.at[g], piece_in.at[dp], gsend.at[g], grecv.at[dp], {"dp": g})

    for k in range(4):
        out = jnp.dot(
            flipped_in[...], norm_ref[:, k * 256 : (k + 1) * 256], preferred_element_type=jnp.float32
        ).astype(jnp.bfloat16)
        for g in (2 * k, 2 * k + 1):
            piece[g] = out[:, (g % 2) * 128 : (g % 2 + 1) * 128]

            @pl.when(dp != g)
            def _():
                hand(g).start()

    for i in range(1, 16):
        far = stat_in.at[mate(i)]
        remote(far, far, ssend.at[0], srecv.at[mate(i)], {"tp": mate(i)}).wait_recv()
    stat_in[tp] = stat[...]
    total[...] = jnp.sum(stat_in[...], axis=0)

    def tell_groups(i):
        return remote(total, total_in.at[dp], tsend.at[i - 1], trecv.at[dp], {"dp": group(i)})

    for i in range(1, 8):
        tell_groups(i).start()

    for i in range(1, 8):
        far = piece_in.at[group(i)]
        remote(far, far, gsend.at[0], grecv.at[group(i)], {"dp": group(i)}).wait_recv()
    piece_in[dp] = piece[dp]
    acc = jnp.zeros((PROJ, 128), jnp.float32)
    for k in range(8):
        acc += piece_in[k].astype(jnp.float32)
    summed[...] = acc.astype(jnp.bfloat16)

    def column(g):
        return out_ref.at[:, pl.ds(pl.multiple_of(g * 128, 128), 128)]

    def publish(i):
        return remote(summed, column(dp), asend.at[i - 1], arecv.at[dp], {"dp": group(i)})

    own_column = pltpu.make_async_copy(summed, column(dp), local.at[5])
    own_column.start()
    for i in range(1, 8):
        publish(i).start()

    for i in range(1, 8):
        far = total_in.at[group(i)]
        remote(far, far, tsend.at[0], trecv.at[group(i)], {"dp": group(i)}).wait_recv()
    total_in[dp] = total[...]
    whole = jnp.sum(total_in[...], axis=0)
    stat_ref[:8, :] = whole[:8, :]
    stat_ref[8:, :] = whole[8:, :] / terms

    for zq in (0, 1):
        swap(zq).wait_send()
        for part in range(PARTS):

            @pl.when(is_far(zq))
            def _():
                for s in (0, 1):
                    pass_on(zq, s, part).wait_send()

            @pl.when(is_near(zq))
            def _():
                for s in (0, 1):
                    give(zq, s, part).wait_send()

            @pl.when(is_own(zq))
            def _():
                hand_over(zq, part).wait_send()

                @pl.when(core != kept)
                def _():
                    keep(zq, part).wait()

    for copy in share_proj + norm_going + [norm_on(i) for i in (1, 2, 3)] + [norm_half(core)]:
        copy.wait_send()
    for part in range(PARTS):
        for i in range(1, EACH):
            flip(part, i).wait_send()

        @pl.when(tp // EACH != part)
        def _():
            flip(part, 0).wait_send()

    for i in range(1, 16):
        tell(i).wait_send()
    for g in range(8):

        @pl.when(dp != g)
        def _():
            hand(g).wait_send()

    for i in range(1, 8):
        tell_groups(i).wait_send()
    for i in range(1, 8):
        far = column(group(i))
        remote(far, far, asend.at[0], arecv.at[group(i)], {"dp": group(i)}).wait_recv()
        publish(i).wait_send()
    own_column.wait()


def student(lengths, loss_scale, qkv, w_out, hidden, proj, rows, gain):
    vmem = pl.BlockSpec(memory_space=pltpu.VMEM)
    smem = pl.BlockSpec(memory_space=pltpu.SMEM)
    hbm = pl.BlockSpec(memory_space=pltpu.HBM)
    return pl.pallas_call(
        student_kernel,
        name="student",
        out_shape=(
            jax.ShapeDtypeStruct((ROWS, DS), jnp.bfloat16),
            jax.ShapeDtypeStruct((PROJ, DS), jnp.bfloat16),
            jax.ShapeDtypeStruct((16, 128), jnp.float32),
        ),
        in_specs=[smem, smem, vmem, hbm, hbm, hbm, vmem, vmem],
        out_specs=(vmem, vmem, vmem),
        scratch_shapes=[
            pltpu.VMEM((4, 256, HW), jnp.bfloat16),
            pltpu.VMEM((ROWS, HW), jnp.bfloat16),
            pltpu.VMEM((4, HW, 256), jnp.bfloat16),
            pltpu.VMEM((2 * LEN, DS), jnp.bfloat16),
            pltpu.VMEM((ROWS, DS), jnp.bfloat16),
            pltpu.VMEM((4, 2, 256, 256), jnp.bfloat16),
            pltpu.VMEM((2, 2, 256, 256), jnp.bfloat16),
            pltpu.VMEM((2, 256, HW), jnp.bfloat16),
            pltpu.VMEM((3, ROWS, HW), jnp.bfloat16),
            pltpu.VMEM((ROWS, HW), jnp.bfloat16),
            pltpu.VMEM((ROWS, HW), jnp.float32),
            pltpu.VMEM((ROWS, HW), jnp.bfloat16),
            pltpu.VMEM((HW, ROWS), jnp.bfloat16),
            pltpu.VMEM((PROJ, 2 * LEN), jnp.bfloat16),
            pltpu.VMEM((16, 128), jnp.float32),
            pltpu.VMEM((16, 16, 128), jnp.float32),
            pltpu.VMEM((16, 128), jnp.float32),
            pltpu.VMEM((8, 16, 128), jnp.float32),
            pltpu.VMEM((8, PROJ, 128), jnp.bfloat16),
            pltpu.VMEM((8, PROJ, 128), jnp.bfloat16),
            pltpu.VMEM((PROJ, 128), jnp.bfloat16),
        ]
        + [pltpu.SemaphoreType.DMA((n,)) for n in (2, 2, 4 * PARTS, 3 * PARTS, PARTS, 8, 9, 16, 16, 15, 16, 7, 8, 8, 8, 7, 8, 8, 8, 8, 6)],
        compiler_params=pltpu.CompilerParams(
            collective_id=1, has_side_effects=True, vmem_limit_bytes=56 * MIB
        ),
    )(lengths, loss_scale, qkv, w_out, hidden, proj, rows, gain)


def finish_kernel(grad_in, proj_in, stat_in, grad_ref, proj_ref, gain_ref, loss_ref):
    grad_ref[...] = grad_in[...]
    proj_ref[...] = proj_in[...]
    gain_ref[...] = stat_in[:8, :]
    loss_ref[...] = stat_in[8:9, :1]


def finish(grad, proj, stat):
    return pl.pallas_call(
        finish_kernel,
        name="finish",
        out_shape=(
            jax.ShapeDtypeStruct(grad.shape, grad.dtype),
            jax.ShapeDtypeStruct(proj.shape, proj.dtype),
            jax.ShapeDtypeStruct((8, 128), jnp.float32),
            jax.ShapeDtypeStruct((1, 1), jnp.float32),
        ),
    )(grad, proj, stat)


def shards(
    hidden_in, norm_gain, w_qkv, w_out, lengths, student_in, student_gain, proj_weight, loss_scale
):
    qkv, w_out_all, proj_all = project(hidden_in, norm_gain.reshape(1, D), w_qkv, w_out, proj_weight)
    row_grad, proj_grad, stat = student(
        lengths,
        loss_scale,
        qkv,
        w_out_all,
        hidden_in,
        proj_all,
        student_in,
        student_gain.reshape(1, DS),
    )
    row_grad, proj_grad, gain, loss = finish(row_grad, proj_grad, stat)
    return row_grad, proj_grad, gain.reshape(DS), loss.reshape(())


def solution(mesh):
    placed = (
        P(("dp", "tp"), None),
        P(),
        P(None, None, "tp"),
        P("tp", None),
        P(),
        P(("dp", "tp"), None),
        P(),
        P("tp", None),
        P(),
    )
    return jax.shard_map(
        shards,
        mesh=mesh,
        in_specs=placed,
        out_specs=(P(("dp", "tp"), None), P("tp", None), P(), P()),
        check_vma=False,
    )
```

```python
import functools
import math

import jax
import jax.numpy as jnp
from jax import lax
from jax.experimental import pallas as pl
from jax.experimental.pallas import tpu as pltpu
from jax.sharding import PartitionSpec as P

HEAD = 128
HW = 3584
PARTS = 4
WIDE = HW // PARTS
TURN = (2, 1, 3, 0)
EACH = 16 // PARTS
LEN = 1024
SEQS = 2
D = 7168
DS = 1024
PROJ = 224
ROWS = 128
FIRST = (64, 64)
MESH = pl.DeviceIdType.MESH
MIB = 1 << 20


def place():
    tp = lax.axis_index("tp")
    return tp // 4, (tp // 2) % 2, tp % 2


def at(z, x, core):
    return {"tp": (z % 4) * 4 + x * 2 + core}


def across(z, x, core):
    dp = lax.axis_index("dp")
    return {"tp": z * 4 + (1 - x) * 2 + core, "dp": (1 - dp // 4) * 4 + dp % 4}


def beside(z, x, core, i):
    dp = lax.axis_index("dp")
    return {"tp": z * 4 + x * 2 + core, "dp": dp // 4 * 4 + (dp + i) % 4}


def remote(src, dst, send, recv, device):
    return pltpu.make_async_remote_copy(
        src_ref=src, dst_ref=dst, send_sem=send, recv_sem=recv, device_id=device, device_id_type=MESH
    )


def rms_norm(rows, gain):
    return rows * lax.rsqrt(jnp.mean(rows * rows, axis=-1, keepdims=True) + 1e-06) * gain


def greet(devices, meanwhile):
    barrier = pltpu.get_barrier_semaphore()
    for device in devices:
        pl.semaphore_signal(barrier, 1, device_id=device, device_id_type=MESH)
    meanwhile()
    pl.semaphore_wait(barrier, len(devices))


def project_kernel(
    x_ref,
    gain_ref,
    w_hbm,
    wout_hbm,
    proj_hbm,
    qkv_ref,
    wout_all,
    proj_all,
    normed,
    rows,
    w,
    send,
    recv,
    wsend,
    wrecv,
    psend,
    precv,
    ysend,
    yrecv,
    local,
):
    z, x, core = place()
    other = 1 - x
    kept = z // 2
    rel = (z - 2 * core + 4) % 4
    ahead = (rel == 0) | (rel == 3)
    step = jnp.where(ahead, 1, -1)
    near = (z + step + 4) % 4
    onward = (z - step + 4) % 4
    far = (z + 2) % 4

    def norm(start, size):
        def one(i, carry):
            block = pl.ds(pl.multiple_of(start + i * 16, 16), 16)
            values = x_ref[block, :].astype(jnp.float32)
            centred = values - jnp.mean(values, axis=-1, keepdims=True)
            spread = jnp.mean(centred * centred, axis=-1, keepdims=True)
            normed[block, :] = (centred * lax.rsqrt(spread + 1e-05) * gain_ref[...]).astype(jnp.bfloat16)
            return carry

        lax.fori_loop(0, size // 16, one, 0)

    greet(
        [at(z, x, 1 - core)]
        + [at(zz, x, c) for zz in (z + 1, z + 3) for c in (0, 1)]
        + [at(z, other, c) for c in (0, 1)]
        + [across(z, x, c) for c in (0, 1)]
        + [at(far, x, core)]
        + [beside(z, x, core, i) for i in (1, 2, 3)],
        lambda: norm(min(FIRST), ROWS - min(FIRST)),
    )

    y = lax.axis_index("dp") % 4

    def held(chip_z, chip_x):
        return proj_all.at[y, (chip_z % 4) * 2 + chip_x, core]

    def held_sem(chip_z, chip_x):
        return precv.at[(chip_z % 4) * 2 + chip_x]

    quarter = proj_hbm.at[:, pl.ds(pl.multiple_of(y * 256, 256), 256)]
    quarter_here = pltpu.make_async_copy(quarter, held(z, x), local.at[6])
    quarter_going = [
        remote(quarter, held(z, x), psend.at[i], held_sem(z, x), device)
        for i, device in enumerate(
            (at(z + 1, x, core), at(z + 3, x, core), at(z + 2, x, core), across(z, x, core))
        )
    ]
    for copy in [quarter_here] + quarter_going:
        copy.start()

    def quarter_wait(chip_z, chip_x):
        ref = held(chip_z, chip_x)
        remote(ref, ref, psend.at[0], held_sem(chip_z, chip_x), across(z, x, core)).wait_recv()

    def quarter_on(i):
        ref = held(z + i, x)
        return remote(ref, ref, psend.at[3 + i], held_sem(z + i, x), across(z, x, core))

    def along(i):
        ref = proj_all.at[y, :, core]
        return remote(ref, ref, ysend.at[i - 1], yrecv.at[y], beside(z, x, core, i))

    w_out_going = [
        remote(w_hbm.at[k], w.at[core, k], wsend.at[k], wrecv.at[k], at(z, x, 1 - core)) for k in range(3)
    ]
    w_own = [pltpu.make_async_copy(w_hbm.at[k], w.at[core, k], local.at[k]) for k in range(3)]
    slot = x * 2 + core
    proj_going = [
        remote(wout_hbm, wout_all.at[slot], wsend.at[3], wrecv.at[3 + core], at(z, x, 1 - core)),
        remote(wout_hbm, wout_all.at[slot], wsend.at[4], wrecv.at[5 + core], across(z, x, core)),
    ]
    far_slot = wout_all.at[other * 2 + core]
    proj_on = remote(far_slot, far_slot, wsend.at[5], wrecv.at[5 + core], at(z, x, 1 - core))
    proj_own = pltpu.make_async_copy(wout_hbm, wout_all.at[slot], local.at[3])
    for copy in w_own + w_out_going + proj_going[:1] + [proj_own]:
        copy.start()

    def part(chunk_z, chunk_x, s, cls):
        chunk = (chunk_z % 2) * 2 + chunk_x
        start, size = ((0, FIRST[s]), (FIRST[s], ROWS - FIRST[s]))[cls]
        return rows.at[chunk, pl.ds(s * ROWS + start, size)]

    def sem(chunk_z, chunk_x, s, cls):
        return recv.at[((chunk_z % 2) * 2 + chunk_x) * 4 + s * 2 + cls]

    def arrived(chunk_z, chunk_x, s, cls):
        ref = part(chunk_z, chunk_x, s, cls)
        remote(ref, ref, send.at[0], sem(chunk_z, chunk_x, s, cls), at(z, x, 1 - core)).wait_recv()

    def forward(chunk_z, chunk_x, s, cls, index, device):
        ref = part(chunk_z, chunk_x, s, cls)
        return remote(ref, ref, send.at[index], sem(chunk_z, chunk_x, s, cls), device)

    def own_copies(cls, s):
        start, size = ((0, FIRST[s]), (FIRST[s], ROWS - FIRST[s]))[cls]
        src = normed.at[pl.ds(start, size)]
        dst = part(z, x, s, cls)
        got = sem(z, x, s, cls)
        base = cls * 4
        return (
            [
                remote(src, dst, send.at[base], got, at(z + 1, x, kept)),
                remote(src, dst, send.at[base + 1], got, at(z + 3, x, kept)),
                remote(src, dst, send.at[base + 2], got, at(z, other, kept)),
            ],
            remote(src, dst, send.at[base + 3], got, at(z, x, 1 - core)),
            pltpu.make_async_copy(src, dst, local.at[4 + cls]),
        )

    def send_own(cls, over_x, rest):
        for s in (0, 1):

            @pl.when(core == s)
            def _():
                away, sibling, here = own_copies(cls, s)
                if over_x:
                    away[2].start()
                if rest:
                    for copy in away[:2]:
                        copy.start()

                    @pl.when(core == kept)
                    def _():
                        here.start()

                    @pl.when(core != kept)
                    def _():
                        sibling.start()

    send_own(1, False, True)
    norm(0, min(FIRST))
    send_own(0, True, True)
    send_own(1, True, False)

    def multiply(chunk_z, chunk_x, start=0, size=2 * ROWS):
        chunk = (chunk_z % 2) * 2 + chunk_x

        def one(n, carry):
            out = jnp.dot(
                rows[chunk, start : start + size], w[n % 2, n // 2], preferred_element_type=jnp.float32
            )
            qkv_ref[n, pl.ds(pl.multiple_of(chunk * 256 + start, 128), size), :] = out.astype(jnp.bfloat16)
            return carry

        lax.fori_loop(0, 6, one, 0)

    source = rel < 2

    for i in (1, 3, 2):
        quarter_wait(z + i, x)
        quarter_on(i).start()
    for copy in proj_going[1:]:
        copy.start()

    fx = []
    for s in (0, 1):
        arrived(near, x, s, 1)
        fx.append(forward(near, x, s, 1, 8 + s, at(z, other, core)))
        fx[-1].start()
    def pass_on(chunk_x, cls, index):
        return [
            (ahead == bool(s), forward(near, chunk_x, s, cls, index, at(onward, x, core))) for s in (0, 1)
        ]

    def begin(pairs):
        for mine, copy in pairs:

            @pl.when(mine)
            def _():
                copy.start()

    begin(pass_on(x, 1, 10))


    for copy in w_own:
        copy.wait()
    for k in range(3):
        remote(w_hbm.at[k], w.at[1 - core, k], wsend.at[k], wrecv.at[k], at(z, x, 1 - core)).wait_recv()

    @pl.when(source)
    def _():
        for cls in (0, 1):
            for s in (0, 1):

                @pl.when(core != s)
                def _():
                    arrived(z, x, s, cls)

                @pl.when(core == s)
                def _():
                    own_copies(cls, s)[2].wait()

        multiply(z, x)

    quarter_here.wait()
    for i in range(4):
        quarter_wait(z + i, other)
    for i in (1, 2, 3):
        along(i).start()

    for s in (0, 1):
        arrived(near, x, s, 0)
    begin(pass_on(x, 0, 11))

    def spread():
        return [
            forward(z, other, s, 0, 12 + s * 2 + i, at(zz, x, core))
            for s, i, zz in ((0, 0, z + 1), (1, 1, z + 3), (1, 0, z + 1), (0, 1, z + 3))
        ]

    def crossing():
        return [forward(far, x, s, 1, 12 + s, at(z, other, core)) for s in (0, 1)]

    @pl.when(source)
    def _():
        for s in (0, 1):
            arrived(z, other, s, 0)
        for copy in spread():
            copy.start()
        for s in (0, 1):
            arrived(z, other, s, 1)
        multiply(z, other)

    @pl.when(jnp.logical_not(source))
    def _():
        for s in (0, 1):
            arrived(far, x, s, 1)
        for copy in crossing():
            copy.start()
        multiply(near, x)

    for s in (0, 1):
        arrived(near, other, s, 0)
    begin(pass_on(other, 0, 16))

    @pl.when(source)
    def _():
        multiply(near, x)

    remote(far_slot, far_slot, wsend.at[4], wrecv.at[5 + core], across(z, x, core)).wait_recv()
    proj_on.start()

    for s in (0, 1):
        arrived(near, other, s, 1)
    multiply(near, other)

    @pl.when(jnp.logical_not(source))
    def _():
        for s in (0, 1):
            arrived(far, x, s, 0)
        multiply(far, x)
        for s in (0, 1):
            arrived(far, other, s, 0)
            arrived(far, other, s, 1)
            multiply(far, other, s * ROWS, ROWS)

    for cls in (0, 1):
        for s in (0, 1):

            @pl.when(core == s)
            def _():
                away, sibling, here = own_copies(cls, s)
                for copy in away:
                    copy.wait_send()

                @pl.when(core != kept)
                def _():
                    sibling.wait_send()

    for copy in fx:
        copy.wait_send()
    for mine, copy in pass_on(x, 1, 10) + pass_on(x, 0, 11) + pass_on(other, 0, 16):

        @pl.when(mine)
        def _():
            copy.wait_send()

    @pl.when(source)
    def _():
        for copy in spread():
            copy.wait_send()

    @pl.when(jnp.logical_not(source))
    def _():
        for copy in crossing():
            copy.wait_send()

    for copy in w_out_going + proj_going + [proj_on] + quarter_going + [quarter_on(i) for i in (1, 2, 3)]:
        copy.wait_send()
    for i in (1, 2, 3):
        along(i).wait_send()
        ref = proj_all.at[(y + i) % 4, :, core]
        remote(ref, ref, ysend.at[0], yrecv.at[(y + i) % 4], at(z, x, 1 - core)).wait_recv()
    proj_own.wait()
    remote(
        wout_hbm, wout_all.at[x * 2 + 1 - core], wsend.at[3], wrecv.at[3 + 1 - core], at(z, x, 1 - core)
    ).wait_recv()
    beyond = wout_all.at[other * 2 + 1 - core]
    remote(beyond, beyond, wsend.at[5], wrecv.at[5 + 1 - core], at(z, x, 1 - core)).wait_recv()


def project(hidden, gain, w_qkv, w_out, proj):
    vmem = pl.BlockSpec(memory_space=pltpu.VMEM)
    hbm = pl.BlockSpec(memory_space=pltpu.HBM)
    return pl.pallas_call(
        project_kernel,
        name="project",
        out_shape=(
            jax.ShapeDtypeStruct((6, LEN, 256), jnp.bfloat16),
            jax.ShapeDtypeStruct((4, 256, HW), jnp.bfloat16),
            jax.ShapeDtypeStruct((4, 8, 2, PROJ, 256), jnp.bfloat16),
        ),
        in_specs=[vmem, vmem, hbm, hbm, hbm],
        out_specs=(vmem, hbm, hbm),
        scratch_shapes=[
            pltpu.VMEM((ROWS, D), jnp.bfloat16),
            pltpu.VMEM((4, 2 * ROWS, D), jnp.bfloat16),
            pltpu.VMEM((2, 3, D, 256), jnp.bfloat16),
        ]
        + [pltpu.SemaphoreType.DMA((n,)) for n in (17, 16, 6, 7, 7, 8, 3, 4, 7)],
        compiler_params=pltpu.CompilerParams(
            collective_id=0, has_side_effects=True, vmem_limit_bytes=60 * MIB
        ),
    )(hidden, gain, w_qkv, w_out, proj)


def student_kernel(
    len_ref,
    scale_ref,
    qkv_ref,
    wout_hbm,
    hid_hbm,
    proj_hbm,
    student_ref,
    gain_ref,
    grad_ref,
    out_ref,
    stat_ref,
    wout_ref,
    hid_ref,
    proj_ref,
    norm_ref,
    normed,
    ctx,
    ctx_in,
    stage,
    parts,
    relay,
    mapped,
    delta,
    flipped,
    flipped_in,
    stat,
    stat_in,
    total,
    total_in,
    piece,
    piece_in,
    summed,
    send,
    recv,
    osend,
    orecv,
    rrecv,
    nsend,
    nrecv,
    dsend,
    drecv,
    ssend,
    srecv,
    tsend,
    trecv,
    gsend,
    grecv,
    asend,
    arecv,
    plocal,
    psend,
    precv,
    local,
):
    z, x, core = place()
    other = 1 - x
    kept = z // 2
    tp = lax.axis_index("tp")
    dp = lax.axis_index("dp")
    rel = (z - 2 * core + 4) % 4
    ahead = (rel == 0) | (rel == 3)
    step = jnp.where(ahead, 1, -1)
    via = jnp.where(ahead, 0, 1)
    source = rel < 2
    key_len = len_ref[dp * SEQS + core]
    count = len_ref[0]
    for i in range(1, len_ref.shape[0]):
        count += len_ref[i]
    terms = jnp.full((1, 128), 1.0, jnp.float32) * count.astype(jnp.float32) * HW
    factor = (2.0 * scale_ref[0] / terms)[:, :1]

    fetch_wout = pltpu.make_async_copy(wout_hbm, wout_ref, local.at[0])
    fetch_hid = pltpu.make_async_copy(hid_hbm.at[:, pl.ds(0, HW)], hid_ref, local.at[1])

    def proj_rows(chip, c):
        return proj_ref.at[:, pl.ds(pl.multiple_of(chip * 2 * PROJ + c * PROJ, 16), PROJ)]

    fetch_proj = [
        pltpu.make_async_copy(proj_hbm.at[:, chip, core], proj_rows(chip, core), plocal.at[chip])
        for chip in range(8)
    ]
    share_proj = [
        remote(
            proj_hbm.at[:, chip, core], proj_rows(chip, core), psend.at[chip], precv.at[chip], at(z, x, 1 - core)
        )
        for chip in range(8)
    ]
    for copy in [fetch_wout, fetch_hid] + fetch_proj:
        copy.start()

    def mate(i):
        return (tp + i) % 16

    def group(i):
        return (dp + i) % 8

    rows = student_ref[...].astype(jnp.float32)
    scale = lax.rsqrt(jnp.mean(rows * rows, axis=-1, keepdims=True) + 1e-06)
    normed[...] = (rows * scale * gain_ref[...]).astype(jnp.bfloat16)

    def attend(chunk, keys, zq, mine):
        start = pl.multiple_of(chunk * 256, 256)
        row = lax.broadcasted_iota(jnp.int32, (256, keys), 0) + start
        col = lax.broadcasted_iota(jnp.int32, (256, keys), 1)
        allowed = (col <= row) & (col < key_len)

        def pair(half, carry):
            for h in (0, 1):
                lanes = slice(h * HEAD, (h + 1) * HEAD)
                q = qkv_ref[half, pl.ds(start, 256), lanes]
                k = qkv_ref[2 + half, :keys, lanes]
                v = qkv_ref[4 + half, :keys, lanes]
                scores = lax.dot_general(
                    q, k, (((1,), (1,)), ((), ())), preferred_element_type=jnp.float32
                ) * (1.0 / math.sqrt(HEAD))
                scores = jnp.where(allowed, scores, -1e30)
                weights = jnp.exp(scores - jnp.max(scores, axis=-1, keepdims=True))
                norm = jnp.sum(weights, axis=-1, keepdims=True)
                out = jnp.dot(weights.astype(jnp.bfloat16), v, preferred_element_type=jnp.float32)
                ctx[zq * 2 + mine, half, :, lanes] = (out / norm).astype(jnp.bfloat16)
            return carry

        lax.fori_loop(0, 2, pair, 0)

    def swap(zq):
        return remote(ctx.at[zq * 2], ctx_in.at[zq], send.at[zq], recv.at[zq], at(z, other, core))

    greet(
        [{"tp": mate(i)} for i in range(1, 16)] + [{"dp": group(i)} for i in range(1, 8)],
        lambda: attend(other, 512, 0, 0),
    )
    swap(0).start()

    def block(chip_z, chip_x, c):
        chip = (chip_z % 4) * 2 + chip_x
        return norm_ref.at[pl.ds(pl.multiple_of((c * 8 + chip) * ROWS, 128), ROWS)]

    def block_sem(chip_z, chip_x):
        return nrecv.at[(chip_z % 4) * 2 + chip_x]

    norm_here = pltpu.make_async_copy(normed, block(z, x, core), local.at[3])
    norm_going = [
        remote(normed, block(z, x, core), nsend.at[i], block_sem(z, x), at(zz, xx, core))
        for i, (zz, xx) in enumerate(((z + 1, x), (z + 3, x), (z + 2, x), (z, other)))
    ]

    def norm_wait(chip_z, chip_x):
        ref = block(chip_z, chip_x, core)
        remote(ref, ref, nsend.at[0], block_sem(chip_z, chip_x), at(z, other, core)).wait_recv()

    def norm_on(i):
        ref = block(z + i, x, core)
        return remote(ref, ref, nsend.at[3 + i], block_sem(z + i, x), at(z, other, core))

    def norm_half(c):
        ref = norm_ref.at[pl.ds(pl.multiple_of(c * LEN, 128), LEN)]
        return remote(ref, ref, nsend.at[7], nrecv.at[8], at(z, x, 1 - core))

    def side(part):
        return pl.ds(pl.multiple_of(jnp.int32(part * WIDE), 128), WIDE)

    def summand(zq, s, part):
        return stage.at[zq, pl.ds(pl.multiple_of(s * ROWS, 16), ROWS), side(part)]

    def give(zq, s, part):
        slot = jnp.where(ahead, 2, 1)
        return remote(
            summand(zq, s, part),
            parts.at[slot, :, side(part)],
            osend.at[(zq * 2 + s) * PARTS + part],
            orecv.at[slot * PARTS + part],
            at(z + step + 4, x, s),
        )

    def pass_on(zq, s, part):
        return remote(
            summand(zq, s, part),
            relay.at[:, side(part)],
            osend.at[(zq * 2 + s) * PARTS + part],
            rrecv.at[part],
            at(z + (1 if s == 0 else 3), x, core),
        )

    def hand_over(zq, part):
        return remote(
            summand(zq, 1 - core, part),
            parts.at[0, :, side(part)],
            osend.at[(zq * 2 + 1 - core) * PARTS + part],
            orecv.at[part],
            at(z, x, 1 - core),
        )

    def keep(zq, part):
        return pltpu.make_async_copy(
            summand(zq, core, part), parts.at[0, :, side(part)], osend.at[(zq * 2 + core) * PARTS + part]
        )

    def is_near(zq):
        return (rel == 1 - zq) | (rel == 3 - zq)

    def is_far(zq):
        return rel == 2 + zq

    def is_own(zq):
        return rel == zq

    def project_out(zq, part):
        out = jnp.zeros((256, WIDE), jnp.float32)
        for k in (0, 1):
            out += jnp.dot(
                ctx[zq * 2 + 1, k], wout_ref[x * 2 + k, :, side(part)], preferred_element_type=jnp.float32
            )
            out += jnp.dot(
                ctx_in[zq, k], wout_ref[other * 2 + k, :, side(part)], preferred_element_type=jnp.float32
            )
        stage[zq, :, side(part)] = out.astype(jnp.bfloat16)

        @pl.when(is_far(zq))
        def _():
            for s in (0, 1):
                pass_on(zq, s, part).start()

        @pl.when(is_near(zq))
        def _():
            give(zq, 1 - via, part).start()

        @pl.when(is_own(zq))
        def _():
            keep(zq, part).start()
            hand_over(zq, part).start()

    def join(zq, part):
        @pl.when(is_near(zq))
        def _():
            src = relay.at[:, side(part)]
            remote(src, src, osend.at[0], rrecv.at[part], at(z, x, 1 - core)).wait_recv()

            def one(i, carry):
                here = pl.ds(pl.multiple_of(via * ROWS + i * 16, 16), 16)
                there = pl.ds(pl.multiple_of(i * 16, 16), 16)
                both = stage[zq, here, side(part)].astype(jnp.float32) + relay[there, side(part)].astype(
                    jnp.float32
                )
                stage[zq, here, side(part)] = both.astype(jnp.bfloat16)
                return carry

            lax.fori_loop(0, ROWS // 16, one, 0)
            give(zq, via, part).start()

    for copy in [norm_here] + norm_going[:3] + share_proj:
        copy.start()
    attend(2 + other, 1024, 1, 0)
    swap(1).start()
    attend(x, 512, 0, 1)
    fetch_wout.wait()
    swap(0).wait_recv()
    for turn in TURN:
        project_out(0, (2 * core + turn) % PARTS)
    attend(2 + x, 1024, 1, 1)
    swap(1).wait_recv()
    for turn in TURN:
        project_out(1, (2 * core + 1 + turn) % PARTS)
    norm_going[3].start()
    for i in (1, 3, 2):
        norm_wait(z + i, x)
        norm_on(i).start()
    join(0, (2 * core + TURN[0]) % PARTS)

    for chip in range(8):
        fetch_proj[chip].wait()
        got = proj_rows(chip, 1 - core)
        remote(got, got, psend.at[0], precv.at[chip], at(z, x, 1 - core)).wait_recv()

    def map_rows(n, carry):
        base = pl.multiple_of(n * 512, 512)
        out = jnp.zeros((ROWS, 512), jnp.float32)
        for k in range(4):
            out += lax.dot_general(
                normed[:, k * 256 : (k + 1) * 256],
                proj_ref[k, pl.ds(base, 512), :],
                (((1,), (1,)), ((), ())),
                preferred_element_type=jnp.float32,
            )
        mapped[:, pl.ds(base, 512)] = out
        return carry

    lax.fori_loop(0, HW // 512, map_rows, 0)
    for turn in TURN[1:]:
        join(0, (2 * core + turn) % PARTS)
    for turn in TURN:
        join(1, (2 * core + 1 + turn) % PARTS)
    fetch_hid.wait()
    position = (tp % 8) * ROWS + lax.broadcasted_iota(jnp.int32, (ROWS, 1), 0)
    valid = position < len_ref[dp * SEQS + kept]
    lane = pl.ds(pl.multiple_of((core * 8 + z * 2 + x) * ROWS, 128), ROWS)

    def owner(part, i):
        return part * EACH + (tp + i) % EACH

    def flip(part, i):
        src = flipped.at[pl.ds(pl.multiple_of(owner(part, i) * PROJ, 16), PROJ)]
        return remote(
            src, flipped_in.at[:, lane], dsend.at[part * EACH + i], drecv.at[tp], {"tp": owner(part, i)}
        )

    own_flip = pltpu.make_async_copy(
        flipped.at[pl.ds(pl.multiple_of(tp * PROJ, 16), PROJ)], flipped_in.at[:, lane], local.at[4]
    )

    def compare(n, loss):
        block_cols = pl.ds(pl.multiple_of(n * 128, 128), 128)
        mixed = parts[0, :, block_cols].astype(jnp.float32)
        for slot in (1, 2):
            mixed += parts[slot, :, block_cols].astype(jnp.float32)
        target = (hid_ref[:, block_cols].astype(jnp.float32) + mixed).astype(jnp.bfloat16)
        diff = jnp.where(valid, mapped[:, block_cols] - target.astype(jnp.float32), 0.0)
        scaled = diff * factor
        delta[:, block_cols] = scaled.astype(jnp.bfloat16)
        flipped[block_cols, :] = scaled.T.astype(jnp.bfloat16)
        return loss + diff * diff

    loss = jnp.zeros((ROWS, 128), jnp.float32)
    for turn in TURN:
        part = (z + turn) % PARTS
        for slot in (1, 2):
            ref = parts.at[slot, :, side(part)]
            remote(ref, ref, osend.at[0], orecv.at[slot * PARTS + part], at(z, x, 1 - core)).wait_recv()

        @pl.when(core == kept)
        def _():
            for zq in (0, 1):

                @pl.when(is_own(zq))
                def _():
                    keep(zq, part).wait()

        @pl.when(core != kept)
        def _():
            ref = parts.at[0, :, side(part)]
            remote(ref, ref, osend.at[0], orecv.at[part], at(z, x, 1 - core)).wait_recv()

        loss = lax.fori_loop(part * (WIDE // 128), (part + 1) * (WIDE // 128), compare, loss)
        for i in range(1, EACH):
            flip(part, i).start()

        @pl.when(tp // EACH == part)
        def _():
            own_flip.start()

        @pl.when(tp // EACH != part)
        def _():
            flip(part, 0).start()

    norm_here.wait()
    for i in range(4):
        norm_wait(z + i, other)
    norm_half(core).start()

    back = [jnp.dot(delta[...], proj_ref[k], preferred_element_type=jnp.float32) for k in range(4)]
    norm_half(1 - core).wait_recv()
    for i in range(1, 16):
        far = mate(i)
        got = flipped_in.at[:, pl.ds(pl.multiple_of(((far % 2) * 8 + far // 2) * ROWS, 128), ROWS)]
        remote(got, got, dsend.at[0], drecv.at[far], {"tp": far}).wait_recv()
    own_flip.wait()

    def hand(g):
        return remote(piece.at[g], piece_in.at[dp], gsend.at[g], grecv.at[dp], {"dp": g})

    for k in range(4):
        out = jnp.dot(
            flipped_in[...], norm_ref[:, k * 256 : (k + 1) * 256], preferred_element_type=jnp.float32
        ).astype(jnp.bfloat16)
        for g in (2 * k, 2 * k + 1):
            piece[g] = out[:, (g % 2) * 128 : (g % 2 + 1) * 128]

            @pl.when(dp != g)
            def _():
                hand(g).start()

    dots = jnp.zeros((ROWS, 1), jnp.float32)
    for k in range(4):
        cols = slice(k * 256, (k + 1) * 256)
        dots += jnp.sum(back[k] * gain_ref[:, cols] * rows[:, cols], axis=-1, keepdims=True)
    shift = dots * (scale * scale * scale) * (1.0 / DS)
    for k in range(4):
        cols = slice(k * 256, (k + 1) * 256)
        grad_ref[:, cols] = (
            back[k] * gain_ref[:, cols] * scale - rows[:, cols] * shift
        ).astype(jnp.bfloat16)
        part = jnp.sum(back[k] * (rows[:, cols] * scale), axis=0, keepdims=True)
        stat[2 * k : 2 * k + 1, :] = part[:, :128]
        stat[2 * k + 1 : 2 * k + 2, :] = part[:, 128:]
    stat[8:16, :] = jnp.zeros((8, 128), jnp.float32) + jnp.sum(loss)

    def tell(i):
        return remote(stat, stat_in.at[tp], ssend.at[i - 1], srecv.at[tp], {"tp": mate(i)})

    for i in range(1, 16):
        tell(i).start()

    for i in range(1, 8):
        far = piece_in.at[group(i)]
        remote(far, far, gsend.at[0], grecv.at[group(i)], {"dp": group(i)}).wait_recv()
    piece_in[dp] = piece[dp]
    acc = jnp.zeros((PROJ, 128), jnp.float32)
    for k in range(8):
        acc += piece_in[k].astype(jnp.float32)
    summed[...] = acc.astype(jnp.bfloat16)

    def column(g):
        return out_ref.at[:, pl.ds(pl.multiple_of(g * 128, 128), 128)]

    def publish(i):
        return remote(summed, column(dp), asend.at[i - 1], arecv.at[dp], {"dp": group(i)})

    own_column = pltpu.make_async_copy(summed, column(dp), local.at[5])
    own_column.start()
    for i in range(1, 8):
        publish(i).start()

    for i in range(1, 16):
        far = stat_in.at[mate(i)]
        remote(far, far, ssend.at[0], srecv.at[mate(i)], {"tp": mate(i)}).wait_recv()
    stat_in[tp] = stat[...]
    total[...] = jnp.sum(stat_in[...], axis=0)

    def tell_groups(i):
        return remote(total, total_in.at[dp], tsend.at[i - 1], trecv.at[dp], {"dp": group(i)})

    for i in range(1, 8):
        tell_groups(i).start()

    for i in range(1, 8):
        far = total_in.at[group(i)]
        remote(far, far, tsend.at[0], trecv.at[group(i)], {"dp": group(i)}).wait_recv()
    total_in[dp] = total[...]
    whole = jnp.sum(total_in[...], axis=0)
    stat_ref[:8, :] = whole[:8, :]
    stat_ref[8:, :] = whole[8:, :] / terms

    for zq in (0, 1):
        swap(zq).wait_send()
        for part in range(PARTS):

            @pl.when(is_far(zq))
            def _():
                for s in (0, 1):
                    pass_on(zq, s, part).wait_send()

            @pl.when(is_near(zq))
            def _():
                for s in (0, 1):
                    give(zq, s, part).wait_send()

            @pl.when(is_own(zq))
            def _():
                hand_over(zq, part).wait_send()

                @pl.when(core != kept)
                def _():
                    keep(zq, part).wait()

    for copy in share_proj + norm_going + [norm_on(i) for i in (1, 2, 3)] + [norm_half(core)]:
        copy.wait_send()
    for part in range(PARTS):
        for i in range(1, EACH):
            flip(part, i).wait_send()

        @pl.when(tp // EACH != part)
        def _():
            flip(part, 0).wait_send()

    for i in range(1, 16):
        tell(i).wait_send()
    for g in range(8):

        @pl.when(dp != g)
        def _():
            hand(g).wait_send()

    for i in range(1, 8):
        tell_groups(i).wait_send()
    for i in range(1, 8):
        far = column(group(i))
        remote(far, far, asend.at[0], arecv.at[group(i)], {"dp": group(i)}).wait_recv()
        publish(i).wait_send()
    own_column.wait()


def student(lengths, loss_scale, qkv, w_out, hidden, proj, rows, gain):
    vmem = pl.BlockSpec(memory_space=pltpu.VMEM)
    smem = pl.BlockSpec(memory_space=pltpu.SMEM)
    hbm = pl.BlockSpec(memory_space=pltpu.HBM)
    return pl.pallas_call(
        student_kernel,
        name="student",
        out_shape=(
            jax.ShapeDtypeStruct((ROWS, DS), jnp.bfloat16),
            jax.ShapeDtypeStruct((PROJ, DS), jnp.bfloat16),
            jax.ShapeDtypeStruct((16, 128), jnp.float32),
        ),
        in_specs=[smem, smem, vmem, hbm, hbm, hbm, vmem, vmem],
        out_specs=(vmem, vmem, vmem),
        scratch_shapes=[
            pltpu.VMEM((4, 256, HW), jnp.bfloat16),
            pltpu.VMEM((ROWS, HW), jnp.bfloat16),
            pltpu.VMEM((4, HW, 256), jnp.bfloat16),
            pltpu.VMEM((2 * LEN, DS), jnp.bfloat16),
            pltpu.VMEM((ROWS, DS), jnp.bfloat16),
            pltpu.VMEM((4, 2, 256, 256), jnp.bfloat16),
            pltpu.VMEM((2, 2, 256, 256), jnp.bfloat16),
            pltpu.VMEM((2, 256, HW), jnp.bfloat16),
            pltpu.VMEM((3, ROWS, HW), jnp.bfloat16),
            pltpu.VMEM((ROWS, HW), jnp.bfloat16),
            pltpu.VMEM((ROWS, HW), jnp.float32),
            pltpu.VMEM((ROWS, HW), jnp.bfloat16),
            pltpu.VMEM((HW, ROWS), jnp.bfloat16),
            pltpu.VMEM((PROJ, 2 * LEN), jnp.bfloat16),
            pltpu.VMEM((16, 128), jnp.float32),
            pltpu.VMEM((16, 16, 128), jnp.float32),
            pltpu.VMEM((16, 128), jnp.float32),
            pltpu.VMEM((8, 16, 128), jnp.float32),
            pltpu.VMEM((8, PROJ, 128), jnp.bfloat16),
            pltpu.VMEM((8, PROJ, 128), jnp.bfloat16),
            pltpu.VMEM((PROJ, 128), jnp.bfloat16),
        ]
        + [pltpu.SemaphoreType.DMA((n,)) for n in (2, 2, 4 * PARTS, 3 * PARTS, PARTS, 8, 9, 16, 16, 15, 16, 7, 8, 8, 8, 7, 8, 8, 8, 8, 6)],
        compiler_params=pltpu.CompilerParams(
            collective_id=1, has_side_effects=True, vmem_limit_bytes=56 * MIB
        ),
    )(lengths, loss_scale, qkv, w_out, hidden, proj, rows, gain)


def finish_kernel(grad_in, proj_in, stat_in, grad_ref, proj_ref, gain_ref, loss_ref):
    grad_ref[...] = grad_in[...]
    proj_ref[...] = proj_in[...]
    gain_ref[...] = stat_in[:8, :]
    loss_ref[...] = stat_in[8:9, :1]


def finish(grad, proj, stat):
    return pl.pallas_call(
        finish_kernel,
        name="finish",
        out_shape=(
            jax.ShapeDtypeStruct(grad.shape, grad.dtype),
            jax.ShapeDtypeStruct(proj.shape, proj.dtype),
            jax.ShapeDtypeStruct((8, 128), jnp.float32),
            jax.ShapeDtypeStruct((1, 1), jnp.float32),
        ),
    )(grad, proj, stat)


def shards(
    hidden_in, norm_gain, w_qkv, w_out, lengths, student_in, student_gain, proj_weight, loss_scale
):
    qkv, w_out_all, proj_all = project(hidden_in, norm_gain.reshape(1, D), w_qkv, w_out, proj_weight)
    row_grad, proj_grad, stat = student(
        lengths,
        loss_scale,
        qkv,
        w_out_all,
        hidden_in,
        proj_all,
        student_in,
        student_gain.reshape(1, DS),
    )
    row_grad, proj_grad, gain, loss = finish(row_grad, proj_grad, stat)
    return row_grad, proj_grad, gain.reshape(DS), loss.reshape(())


def solution(mesh):
    placed = (
        P(("dp", "tp"), None),
        P(),
        P(None, None, "tp"),
        P("tp", None),
        P(),
        P(("dp", "tp"), None),
        P(),
        P("tp", None),
        P(),
    )
    return jax.shard_map(
        shards,
        mesh=mesh,
        in_specs=placed,
        out_specs=(P(("dp", "tp"), None), P("tp", None), P(), P()),
        check_vma=False,
    )
```
